32 devices in a mesh: section: 2 (over x), dp: 8 (over z, core), rep: 2 (over y).
Axes of the slice: x: 2, y: 2, z: 4, core: 2. Of those that a mesh axis runs over, the one named last changes fastest.
Arguments:
- tokens: bfloat16 [32, 1024, 512], P(('dp', 'rep')), may hold values from -6 to 6
- resets: int32 [32, 1024], P(('dp', 'rep')), may hold values 0 or 1
- cotangent: bfloat16 [32, 1024, 512], P(('dp', 'rep')), may hold values from -6 to 6
- g_one: float32 [2, 512], P('section'), may hold values from 0.25 to 1.75
- w_gate: bfloat16 [2, 512, 2048], P('section'), may hold values from -0.25 to 0.25
- b_gate: float32 [2, 2048], P('section'), may hold values from -8 to 8
- w_cand: bfloat16 [2, 512, 1024], P('section'), may hold values from -0.25 to 0.25
- b_cand: float32 [2, 1024], P('section'), may hold values from -3 to 3
- w_out: bfloat16 [2, 1024, 512], P('section'), may hold values from -0.1875 to 0.1875
- b_out: float32 [2, 512], P('section'), may hold values from -3 to 3
- g_two: float32 [2, 512], P('section'), may hold values from 0.25 to 1.75
- w_up: bfloat16 [2, 512, 2048], P('section'), may hold values from -0.25 to 0.25
- b_up: float32 [2, 2048], P('section'), may hold values from -3 to 3
- w_down: bfloat16 [2, 2048, 512], P('section'), may hold values from -0.125 to 0.125
- b_down: float32 [2, 512], P('section'), may hold values from -3 to 3
Outputs:
- block_outputs: bfloat16 [2, 32, 1024, 512], P('section', ('dp', 'rep'))
- input_grads: float32 [2, 32, 1024, 512], P('section', ('dp', 'rep'))
- grad_g_one: float32 [2, 512], P('section')
- grad_w_gate: float32 [2, 512, 2048], P('section')
- grad_b_gate: float32 [2, 2048], P('section')
- grad_w_cand: float32 [2, 512, 1024], P('section')
- grad_b_cand: float32 [2, 1024], P('section')
- grad_w_out: float32 [2, 1024, 512], P('section')
- grad_b_out: float32 [2, 512], P('section')
- grad_g_two: float32 [2, 512], P('section')
- grad_w_up: float32 [2, 512, 2048], P('section')
- grad_b_up: float32 [2, 2048], P('section')
- grad_w_down: float32 [2, 2048, 512], P('section')
- grad_b_down: float32 [2, 512], P('section')
The draws below stay inside these ranges and needn't reach their ends.
All inputs are finite; a program needn't handle non-finite values. No bound on the sum of `resets` on one device may be relied on, other than what follows from the above.
Results may differ from the reference program's by a relative error of at most 0.013.
Values may be sent and summed in bfloat16 or wider, within the bound.
A program may use at most 320 MiB of HBM per device.

```python
import jax
import jax.numpy as jnp
from jax import lax

D = 512
HID = 1024
FF = 2048
SEQ = 1024
ROWS_DEV = 2
ROWS = 32
N_SECTION = 2


def plant(result, stream_key, low, high):
    shape = result.shape
    spot = [jax.random.randint(jax.random.fold_in(stream_key, axis), (), 0, shape[axis]) for axis in range(len(shape))]
    result = result.at[tuple(spot)].set(low)
    longest = shape.index(max(shape))
    spot[longest] = (spot[longest] + 1) % shape[longest]
    return result.at[tuple(spot)].set(high)


def levels(rng, dims, shards, low, high):
    level = 1.0
    for axis_at, parts in shards:
        steps = jax.random.uniform(jax.random.fold_in(jax.random.fold_in(rng, 6), axis_at), (parts,), jnp.float32, low / len(shards), high / len(shards))
        level = level * jnp.repeat(jnp.exp(steps), dims[axis_at] // parts).reshape((-1,) + (1,) * (len(dims) - 1 - axis_at))
    return level


def scatter_about(key, dims, scale, most, pieces=(), kind=jnp.bfloat16):
    level = levels(key, dims, pieces, -0.22, 0.18) if pieces else 1.0
    array = jax.random.normal(key, dims, jnp.float32) * scale * level
    return jnp.minimum(jnp.maximum(array, -most), most).astype(kind)


def setup_inputs(seed: int = 0) -> dict:
    key_list = jax.random.split(jax.random.key(seed), 16)
    tokens = scatter_about(key_list[0], (ROWS, SEQ, D), 1.0, 6.0, ((0, 16),))
    resets = plant((jax.random.randint(key_list[1], (ROWS, SEQ), 0, 64) < 1).astype(jnp.int32), jax.random.fold_in(key_list[1], 1), 0, 1)
    cotangent = scatter_about(key_list[2], (ROWS, SEQ, D), 1.0, 6.0, ((0, 16),))
    g_one = jnp.clip(1.0 + 0.15 * jax.random.normal(key_list[3], (N_SECTION, D), jnp.float32), 0.25, 1.75)
    w_gate = scatter_about(key_list[4], (N_SECTION, D, 2 * HID), D ** -0.5, 0.25, ((0, 2),))
    b_gate = scatter_about(key_list[5], (N_SECTION, 2 * HID), 2.0, 8.0, ((0, 2),), jnp.float32)
    w_cand = scatter_about(key_list[6], (N_SECTION, D, HID), D ** -0.5, 0.25, ((0, 2),))
    b_cand = scatter_about(key_list[7], (N_SECTION, HID), 0.5, 3.0, ((0, 2),), jnp.float32)
    w_out = scatter_about(key_list[8], (N_SECTION, HID, D), HID ** -0.5, 0.1875, ((0, 2),))
    b_out = scatter_about(key_list[9], (N_SECTION, D), 0.5, 3.0, ((0, 2),), jnp.float32)
    g_two = jnp.clip(1.0 + 0.15 * jax.random.normal(key_list[10], (N_SECTION, D), jnp.float32), 0.25, 1.75)
    w_up = scatter_about(key_list[11], (N_SECTION, D, FF), D ** -0.5, 0.25, ((0, 2),))
    b_up = scatter_about(key_list[12], (N_SECTION, FF), 0.5, 3.0, ((0, 2),), jnp.float32)
    w_down = scatter_about(key_list[13], (N_SECTION, FF, D), FF ** -0.5, 0.125, ((0, 2),))
    b_down = scatter_about(key_list[14], (N_SECTION, D), 0.5, 3.0, ((0, 2),), jnp.float32)
    return dict(tokens=tokens, resets=resets, cotangent=cotangent, g_one=g_one, w_gate=w_gate, b_gate=b_gate, w_cand=w_cand, b_cand=b_cand, w_out=w_out, b_out=b_out, g_two=g_two, w_up=w_up, b_up=b_up, w_down=w_down, b_down=b_down)


@jax.custom_vjp
def low(v):
    return lax.optimization_barrier(v.astype(jnp.bfloat16)).astype(jnp.float32)

@jax.custom_vjp
def low_back(v):
    return v

def low_keep(v):
    return (low(v), None)

def low_pass(kept, grad):
    return (grad,)

def back_keep(v):
    return (v, None)

def back_low(kept, grad):
    return (low(grad),)
low.defvjp(low_keep, low_pass)
low_back.defvjp(back_keep, back_low)
EPS = 1e-06

def norm_rows(values, norm_gain):
    return values * lax.rsqrt(lax.optimization_barrier(jnp.mean(values * values, axis=-1, keepdims=True)) + EPS) * norm_gain

def matmul(operand, weight):
    return jnp.einsum('rsk,kn->rsn', operand, weight, precision=lax.Precision.HIGHEST)

def combine(earlier, later):
    return (earlier[0] * later[0], later[0] * earlier[1] + later[1])

def block(resid_in, keep_mask, params):
    g_one, w_gate, b_gate, w_cand, b_cand, w_out, b_out, g_two, w_up, b_up, w_down, b_down = params
    normed = low(norm_rows(resid_in, g_one))
    gate_pre = low_back(matmul(normed, w_gate) + b_gate)
    forget = jax.nn.sigmoid(gate_pre[..., :HID])
    inward = jax.nn.sigmoid(gate_pre[..., HID:])
    gate_total = forget + inward
    candidate = low_back(matmul(normed, w_cand) + b_cand)
    decay_rate = forget / gate_total * keep_mask[..., None]
    drive_term = inward / gate_total * candidate
    _, hidden_state = lax.associative_scan(combine, (decay_rate, drive_term), axis=1)
    mixed = low_back(matmul(low(hidden_state), w_out) + b_out)
    middle = resid_in + mixed
    up_pre = low_back(matmul(low(norm_rows(middle, g_two)), w_up) + b_up)
    down_out = low_back(matmul(low(jax.nn.gelu(up_pre, approximate=True)), w_down) + b_down)
    return middle + down_out

def run_block(resid_all, keep_all, params):
    grouped = resid_all.reshape((-1, ROWS_DEV, SEQ, D))
    keep_groups = keep_all.reshape((-1, ROWS_DEV, SEQ))

    def one_group(pair):
        return block(pair[0], pair[1], params)
    outcome = lax.map(jax.checkpoint(one_group), (grouped, keep_groups))
    return outcome.reshape(resid_all.shape)

def reference(tokens, resets, cotangent, g_one, w_gate, b_gate, w_cand, b_cand, w_out, b_out, g_two, w_up, b_up, w_down, b_down):
    stacked = (g_one, w_gate, b_gate, w_cand, b_cand, w_out, b_out, g_two, w_up, b_up, w_down, b_down)
    keep_all = (1 - resets).astype(jnp.float32)
    params_first = tuple((member[0].astype(jnp.float32) for member in stacked))
    params_second = tuple((member[1].astype(jnp.float32) for member in stacked))
    first_out, back_first = jax.vjp(lambda resid, ps: run_block(resid, keep_all, ps), tokens.astype(jnp.float32), params_first)
    sent_low = first_out.astype(jnp.bfloat16)
    second_out, back_second = jax.vjp(lambda resid, ps: run_block(resid, keep_all, ps), sent_low.astype(jnp.float32), params_second)
    grad_sent, grads_second = back_second(cotangent.astype(jnp.float32))
    grad_sent_low = grad_sent.astype(jnp.bfloat16).astype(jnp.float32)
    grad_tokens, grads_first = back_first(grad_sent_low)
    block_outputs = jnp.stack([sent_low, second_out.astype(jnp.bfloat16)])
    input_grads = jnp.stack([grad_tokens, grad_sent_low])
    grads = [jnp.stack([grads_first[k], grads_second[k]]) for k in range(12)]
    return (block_outputs, input_grads, grads[0], grads[1], grads[2], grads[3], grads[4], grads[5], grads[6], grads[7], grads[8], grads[9], grads[10], grads[11])
```

```python
import functools
import math

import jax
import jax.numpy as jnp
from jax import lax
from jax.experimental import pallas as pl
from jax.experimental.pallas import tpu as pltpu
from jax.sharding import PartitionSpec as P

EPS = 1e-06
F32 = jnp.float32
BF16 = jnp.bfloat16
CHUNK = 128
LANES = 8
WIDTH = 256
GELU_A = math.sqrt(2.0 / math.pi)
GELU_B = 0.044715
LN4 = math.log(4.0)
EXP_TOP = 85.6
VMEM_LIMIT = 60 * 1024 * 1024


def dot(a, b):
    return jnp.dot(a, b, preferred_element_type=F32)


def dot_nt(a, b):
    return lax.dot_general(a, b, (((1,), (1,)), ((), ())), preferred_element_type=F32)


def inv_scale(values):
    return lax.rsqrt(jnp.mean(values * values, axis=-1, keepdims=True) + EPS)


def partner_barrier_signal(partner):
    pl.semaphore_signal(
        pltpu.get_barrier_semaphore(),
        inc=1,
        device_id={"section": partner},
        device_id_type=pl.DeviceIdType.MESH,
    )


def chunk_copy(send, recv, send_sem, recv_sem, slot, partner):
    return pltpu.make_async_remote_copy(
        src_ref=send.at[slot],
        dst_ref=recv.at[slot],
        send_sem=send_sem.at[slot],
        recv_sem=recv_sem.at[slot],
        device_id={"section": partner},
        device_id_type=pl.DeviceIdType.MESH,
    )


def segment_index(width, per_row):
    return lax.broadcasted_iota(jnp.int32, (LANES, width), 0) % per_row


def forward_kernel(
    steps,
    per_row,
    tok,
    keep,
    perm,
    perm_t,
    g_one,
    w_gate,
    b_gate,
    w_cand,
    b_cand,
    w_out,
    b_out,
    g_two,
    w_up,
    b_up,
    w_down,
    b_down,
    out,
    x_o,
    normed_o,
    decay_o,
    slope_forget_o,
    slope_inward_o,
    slope_cand_o,
    state_o,
    middle_o,
    normed_two_o,
    active_o,
    slope_up_o,
    send,
    recv,
    carry,
    send_sem,
    recv_sem,
):
    c = pl.program_id(0)
    section = lax.axis_index("section")
    partner = 1 - section
    rows, chunk, width = tok.shape
    tokens = rows * chunk
    hidden = w_cand.shape[1]
    ff = w_up.shape[1]
    span = tokens // LANES

    @pl.when(c == 0)
    def _():
        partner_barrier_signal(partner)
        carry[...] = jnp.zeros_like(carry)
        pl.semaphore_wait(pltpu.get_barrier_semaphore(), 1)

    @pl.when(section == 0)
    def _():
        x_o[0] = dot(perm[...], tok[...].reshape(tokens, width)).astype(BF16)

    @pl.when(section == 1)
    def _():
        chunk_copy(send, recv, send_sem, recv_sem, c, partner).wait_recv()
        x_o[0] = recv[c]

    x = x_o[0].astype(F32)
    normed = (x * inv_scale(x) * g_one[...]).astype(BF16)
    normed_o[0] = normed
    mixed = jnp.zeros((tokens, width), F32)
    which = segment_index(WIDTH, per_row)
    for at in range(0, hidden, WIDTH):
        cols = slice(at, at + WIDTH)
        cols_in = slice(hidden + at, hidden + at + WIDTH)
        pre_f = dot(normed, w_gate[:, cols])
        pre_i = dot(normed, w_gate[:, cols_in])
        cand = dot(normed, w_cand[:, cols]) + b_cand[:, cols]
        u = jnp.exp(jnp.minimum((-LN4 - b_gate[:, cols]) - pre_f, EXP_TOP))
        v = jnp.exp(jnp.minimum((-LN4 - b_gate[:, cols_in]) - pre_i, EXP_TOP))
        d = 1.0 / (0.5 + u + v)
        ratio_f = (0.25 + v) * d
        ratio_i = (0.25 + u) * d
        keep_w = jnp.concatenate([keep[0]] * (WIDTH // 128), axis=1)
        decay = ratio_f * keep_w
        drive = ratio_i * cand
        decay_o[0, :, cols] = decay
        slope_cand_o[0, :, cols] = ratio_i.astype(BF16)
        product = decay[0:LANES]
        accum = drive[0:LANES]
        for j in range(1, span):
            r = slice(j * LANES, (j + 1) * LANES)
            accum = decay[r] * accum + drive[r]
            product = decay[r] * product
        incoming = carry[:, cols]
        for q in range(1, per_row):
            nxt = pltpu.roll(product * incoming + accum, 1, 0)
            incoming = jnp.where(which == q, nxt, incoming)
        carry[:, cols] = pltpu.roll(product * incoming + accum, LANES - per_row + 1, 0)
        state = incoming
        before = []
        after = []
        for j in range(span):
            r = slice(j * LANES, (j + 1) * LANES)
            before.append(state)
            state = decay[r] * state + drive[r]
            after.append(state)
        state_low = jnp.concatenate(after, axis=0).astype(BF16)
        state_o[0, :, cols] = state_low
        lever = keep_w * jnp.concatenate(before, axis=0) - cand
        slope_forget_o[0, :, cols] = (lever * (u * d) * ratio_f).astype(BF16)
        slope_inward_o[0, :, cols] = (-lever * (v * d) * ratio_i).astype(BF16)
        mixed = mixed + dot(state_low, w_out[cols, :])
    middle = x + (mixed + b_out[...])
    middle_o[0] = middle
    normed_two = (middle * inv_scale(middle) * g_two[...]).astype(BF16)
    normed_two_o[0] = normed_two
    down = jnp.zeros((tokens, width), F32)
    for at in range(0, ff, WIDTH):
        cols = slice(at, at + WIDTH)
        up = dot(normed_two, w_up[:, cols]) + b_up[:, cols]
        square = up * up
        half = 0.5 + 0.5 * jnp.tanh(up * (GELU_A + (GELU_A * GELU_B) * square))
        act = up * half
        active = act.astype(BF16)
        active_o[0, :, cols] = active
        slope = half + act * (1.0 - half) * (2 * GELU_A + (6 * GELU_A * GELU_B) * square)
        slope_up_o[0, :, cols] = slope.astype(BF16)
        down = down + dot(active, w_down[cols, :])
    low = (middle + (down + b_down[...])).astype(BF16)

    @pl.when(section == 0)
    def _():
        send[c] = low
        chunk_copy(send, recv, send_sem, recv_sem, c, partner).start()

    out[...] = dot(perm_t[...], low).astype(BF16).reshape(out.shape)

    @pl.when((c == steps - 1) & (section == 0))
    def _():
        for slot in range(steps):
            chunk_copy(send, recv, send_sem, recv_sem, slot, partner).wait_send()


def backward_kernel(
    steps,
    per_row,
    cot,
    x_i,
    decay_i,
    slope_forget_i,
    slope_inward_i,
    slope_cand_i,
    middle_i,
    slope_up_i,
    perm,
    perm_t,
    g_one,
    w_gate,
    w_cand,
    w_out,
    g_two,
    w_up,
    w_down,
    grad_in,
    down_o,
    up_o,
    mix_o,
    gate_o,
    cand_o,
    small_o,
    send,
    recv,
    carry,
    send_sem,
    recv_sem,
):
    c = pl.program_id(0)
    section = lax.axis_index("section")
    partner = 1 - section
    rows, chunk, width = cot.shape
    tokens = rows * chunk
    hidden = w_cand.shape[1]
    ff = w_up.shape[1]
    span = tokens // LANES
    at_b_gate = width
    at_b_cand = at_b_gate + 2 * hidden
    at_b_out = at_b_cand + hidden
    at_g_two = at_b_out + width
    at_b_up = at_g_two + width
    at_b_down = at_b_up + ff

    def add_small(at, values):
        n = values.shape[1]
        part = jnp.sum(values.reshape(-1, LANES, n), axis=0)
        small_o[:, at : at + n] += part

    @pl.when(c == 0)
    def _():
        partner_barrier_signal(partner)
        carry[...] = jnp.zeros_like(carry)
        small_o[...] = jnp.zeros_like(small_o)
        pl.semaphore_wait(pltpu.get_barrier_semaphore(), 1)

    @pl.when(section == 1)
    def _():
        down_o[0] = dot(perm[...], cot[...].reshape(tokens, width)).astype(BF16)

    @pl.when(section == 0)
    def _():
        chunk_copy(send, recv, send_sem, recv_sem, c, partner).wait_recv()
        down_o[0] = recv[c]

    grad_down = down_o[0]
    dy = grad_down.astype(F32)
    add_small(at_b_down, dy)
    q = jnp.zeros((tokens, width), F32)
    for at in range(0, ff, WIDTH):
        cols = slice(at, at + WIDTH)
        grad_up = dot_nt(grad_down, w_down[cols, :]) * slope_up_i[0, :, cols].astype(F32)
        add_small(at_b_up + at, grad_up)
        grad_up = grad_up.astype(BF16)
        up_o[0, :, cols] = grad_up
        q = q + dot_nt(grad_up, w_up[:, cols])
    middle = middle_i[0]
    r = inv_scale(middle)
    scaled = middle * r
    add_small(at_g_two, q * scaled)
    weighted = q * g_two[...]
    grad_middle = dy + r * (
        weighted - scaled * jnp.mean(weighted * scaled, axis=-1, keepdims=True)
    )
    add_small(at_b_out, grad_middle)
    grad_mix = grad_middle.astype(BF16)
    mix_o[0] = grad_mix
    p = jnp.zeros((tokens, width), F32)
    which = segment_index(WIDTH, per_row)
    for at in range(0, hidden, WIDTH):
        cols = slice(at, at + WIDTH)
        cols_in = slice(hidden + at, hidden + at + WIDTH)
        grad_state = dot_nt(grad_mix, w_out[cols, :])
        decay = decay_i[0, :, cols]
        last = slice((span - 1) * LANES, span * LANES)
        product = decay[last]
        accum = decay[last] * grad_state[last]
        for j in range(span - 2, -1, -1):
            rj = slice(j * LANES, (j + 1) * LANES)
            accum = decay[rj] * (grad_state[rj] + accum)
            product = decay[rj] * product
        incoming = carry[:, cols]
        for k in range(per_row - 2, -1, -1):
            nxt = pltpu.roll(product * incoming + accum, LANES - 1, 0)
            incoming = jnp.where(which == k, nxt, incoming)
        carry[:, cols] = pltpu.roll(product * incoming + accum, per_row - 1, 0)
        later = incoming
        parts = [None] * span
        for j in range(span - 1, -1, -1):
            rj = slice(j * LANES, (j + 1) * LANES)
            carried = grad_state[rj] + later
            parts[j] = carried
            later = decay[rj] * carried
        carried = jnp.concatenate(parts, axis=0)
        grad_forget = carried * slope_forget_i[0, :, cols].astype(F32)
        grad_inward = carried * slope_inward_i[0, :, cols].astype(F32)
        grad_cand = carried * slope_cand_i[0, :, cols].astype(F32)
        add_small(at_b_gate + at, grad_forget)
        add_small(at_b_gate + hidden + at, grad_inward)
        add_small(at_b_cand + at, grad_cand)
        grad_forget = grad_forget.astype(BF16)
        grad_inward = grad_inward.astype(BF16)
        grad_cand = grad_cand.astype(BF16)
        gate_o[0, :, cols] = grad_forget
        gate_o[0, :, cols_in] = grad_inward
        cand_o[0, :, cols] = grad_cand
        p = p + dot_nt(grad_forget, w_gate[:, cols])
        p = p + dot_nt(grad_inward, w_gate[:, cols_in])
        p = p + dot_nt(grad_cand, w_cand[:, cols])
    x = x_i[0].astype(F32)
    r = inv_scale(x)
    scaled = x * r
    add_small(0, p * scaled)
    weighted = p * g_one[...]
    grad_input = grad_middle + r * (
        weighted - scaled * jnp.mean(weighted * scaled, axis=-1, keepdims=True)
    )
    low = grad_input.astype(BF16)

    @pl.when(section == 1)
    def _():
        send[c] = low
        chunk_copy(send, recv, send_sem, recv_sem, c, partner).start()

    rest = jnp.where(section == 0, grad_input - low.astype(F32), 0.0).astype(BF16)
    grad_in[...] = (dot(perm_t[...], low) + dot(perm_t[...], rest)).reshape(grad_in.shape)

    @pl.when((c == steps - 1) & (section == 1))
    def _():
        for slot in range(steps):
            chunk_copy(send, recv, send_sem, recv_sem, slot, partner).wait_send()


def whole(array):
    zeros = (0,) * array.ndim
    return pl.BlockSpec(array.shape, lambda c: zeros, pipeline_mode=pl.Buffered(1))


def run_forward(tokens, keep, perm, perm_t, weights, chunk):
    rows, seq, width = tokens.shape
    steps = seq // chunk
    size = rows * chunk
    hidden = weights[3].shape[1]
    ff = weights[8].shape[1]

    def saved(columns, dtype):
        shape = jax.ShapeDtypeStruct((steps, size, columns), dtype)
        return shape, pl.BlockSpec((1, size, columns), lambda c: (c, 0, 0))

    out = (
        jax.ShapeDtypeStruct((1, rows, seq, width), BF16),
        pl.BlockSpec((1, rows, chunk, width), lambda c: (0, 0, c, 0)),
    )
    outs = [
        out,
        saved(width, BF16),
        saved(width, BF16),
        saved(hidden, F32),
        saved(hidden, BF16),
        saved(hidden, BF16),
        saved(hidden, BF16),
        saved(hidden, BF16),
        saved(width, F32),
        saved(width, BF16),
        saved(ff, BF16),
        saved(ff, BF16),
    ]
    return pl.pallas_call(
        functools.partial(forward_kernel, steps, LANES // rows),
        grid=(steps,),
        out_shape=[o[0] for o in outs],
        in_specs=[
            pl.BlockSpec((rows, chunk, width), lambda c: (0, c, 0)),
            pl.BlockSpec((1, size, 128), lambda c: (c, 0, 0)),
            whole(perm),
            whole(perm_t),
        ]
        + [whole(w) for w in weights],
        out_specs=[o[1] for o in outs],
        scratch_shapes=[
            pltpu.VMEM((steps, size, width), BF16),
            pltpu.VMEM((steps, size, width), BF16),
            pltpu.VMEM((LANES, hidden), F32),
            pltpu.SemaphoreType.DMA((steps,)),
            pltpu.SemaphoreType.DMA((steps,)),
        ],
        compiler_params=pltpu.CompilerParams(
            collective_id=0, has_side_effects=True, vmem_limit_bytes=VMEM_LIMIT
        ),
        name="forward_block",
    )(tokens, keep, perm, perm_t, *weights)


def run_backward(cotangent, saved_vals, perm, perm_t, weights, chunk):
    rows, seq, width = cotangent.shape
    steps = seq // chunk
    size = rows * chunk
    g_one, w_gate, _, w_cand, _, w_out, _, g_two, w_up, _, w_down, _ = weights
    hidden = w_cand.shape[1]
    ff = w_up.shape[1]
    small = 4 * width + 3 * hidden + ff

    def back(c):
        return (steps - 1 - c, 0, 0)

    def given(columns, dtype):
        shape = jax.ShapeDtypeStruct((steps, size, columns), dtype)
        return shape, pl.BlockSpec((1, size, columns), back)

    outs = [
        (
            jax.ShapeDtypeStruct((1, rows, seq, width), F32),
            pl.BlockSpec((1, rows, chunk, width), lambda c: (0, 0, steps - 1 - c, 0)),
        ),
        given(width, BF16),
        given(ff, BF16),
        given(width, BF16),
        given(2 * hidden, BF16),
        given(hidden, BF16),
        (
            jax.ShapeDtypeStruct((LANES, small), F32),
            pl.BlockSpec((LANES, small), lambda c: (0, 0)),
        ),
    ]
    consts = (perm, perm_t, g_one, w_gate, w_cand, w_out, g_two, w_up, w_down)
    return pl.pallas_call(
        functools.partial(backward_kernel, steps, LANES // rows),
        grid=(steps,),
        out_shape=[o[0] for o in outs],
        in_specs=[pl.BlockSpec((rows, chunk, width), lambda c: (0, steps - 1 - c, 0))]
        + [pl.BlockSpec((1, size, v.shape[2]), back) for v in saved_vals]
        + [whole(w) for w in consts],
        out_specs=[o[1] for o in outs],
        scratch_shapes=[
            pltpu.VMEM((steps, size, width), BF16),
            pltpu.VMEM((steps, size, width), BF16),
            pltpu.VMEM((LANES, hidden), F32),
            pltpu.SemaphoreType.DMA((steps,)),
            pltpu.SemaphoreType.DMA((steps,)),
        ],
        compiler_params=pltpu.CompilerParams(
            collective_id=1, has_side_effects=True, vmem_limit_bytes=VMEM_LIMIT
        ),
        name="backward_block",
    )(cotangent, *saved_vals, *consts)


def weight_grad(operand, gradient):
    a = operand.reshape(-1, operand.shape[-1])
    b = gradient.reshape(-1, gradient.shape[-1])
    return lax.dot_general(a, b, (((0,), (0,)), ((), ())), preferred_element_type=F32)


def local_grads(tokens, resets, cotangent, stacked):
    weights = tuple(w if w.ndim == 2 else w[0] for w in stacked)
    rows, seq, width = tokens.shape
    chunk = min(CHUNK, seq)
    steps = seq // chunk
    size = rows * chunk
    per_row = LANES // rows
    span = size // LANES
    keep = (1 - resets).astype(F32).reshape(rows, steps, per_row, span)
    keep = keep.transpose(1, 3, 0, 2).reshape(steps, size, 1)
    keep = jnp.broadcast_to(keep, (steps, size, 128))
    at = lax.broadcasted_iota(jnp.int32, (size, size), 0)
    source = lax.broadcasted_iota(jnp.int32, (size, size), 1)
    perm = (source == (at % LANES) * span + at // LANES).astype(BF16)
    perm_t = (at == (source % LANES) * span + source // LANES).astype(BF16)
    (
        block_out,
        x,
        normed,
        decay,
        slope_forget,
        slope_inward,
        slope_cand,
        state_low,
        middle,
        normed_two,
        active,
        slope_up,
    ) = run_forward(tokens, keep, perm, perm_t, weights, chunk)
    grad_in, g_down, g_up, g_mix, g_gate, g_cand, small = run_backward(
        cotangent,
        (x, decay, slope_forget, slope_inward, slope_cand, middle, slope_up),
        perm,
        perm_t,
        weights,
        chunk,
    )
    large = (
        weight_grad(normed, g_gate),
        weight_grad(normed, g_cand),
        weight_grad(state_low, g_mix),
        weight_grad(normed_two, g_up),
        weight_grad(active, g_down),
    )
    return block_out, grad_in, large, jnp.sum(small, axis=0)


def split_small(small, width, hidden, ff):
    sizes = (width, 2 * hidden, hidden, width, width, ff, width)
    out = []
    at = 0
    for n in sizes:
        out.append(small[at : at + n])
        at += n
    return out


def body(tokens, resets, cotangent, *stacked):
    block_out, grad_in, large, small = local_grads(tokens, resets, cotangent, stacked)
    width = tokens.shape[2]
    hidden = stacked[3].shape[2]
    ff = stacked[8].shape[2]
    sums = lax.psum(tuple(g.astype(BF16) for g in large) + (small,), ("dp", "rep"))
    w_gate, w_cand, w_out, w_up, w_down = (s.astype(F32) for s in sums[:5])
    g_one, b_gate, b_cand, b_out, g_two, b_up, b_down = split_small(sums[5], width, hidden, ff)
    grads = (g_one, w_gate, b_gate, w_cand, b_cand, w_out, b_out, g_two, w_up, b_up, w_down, b_down)
    return (block_out, grad_in) + tuple(g[None] for g in grads)


def solution(mesh):
    vector = P("section", None)
    matrix = P("section", None, None)
    weight_specs = (
        vector,
        matrix,
        vector,
        matrix,
        vector,
        matrix,
        vector,
        vector,
        matrix,
        vector,
        matrix,
        vector,
    )
    tokens = P(("dp", "rep"), None, None)
    by_rows = P("section", ("dp", "rep"), None, None)
    return jax.shard_map(
        body,
        mesh=mesh,
        in_specs=(tokens, P(("dp", "rep"), None), tokens) + weight_specs,
        out_specs=(by_rows, by_rows) + weight_specs,
        check_vma=False,
    )
```

```python
import functools
import math

import jax
import jax.numpy as jnp
from jax import lax
from jax.experimental import pallas as pl
from jax.experimental.pallas import tpu as pltpu
from jax.sharding import PartitionSpec as P

EPS = 1e-06
F32 = jnp.float32
BF16 = jnp.bfloat16
CHUNK = 128
LANES = 8
WIDTH = 256
GELU_A = math.sqrt(2.0 / math.pi)
GELU_B = 0.044715
LN4 = math.log(4.0)
EXP_TOP = 85.6
VMEM_LIMIT = 60 * 1024 * 1024


def dot(a, b):
    return jnp.dot(a, b, preferred_element_type=F32)


def dot_nt(a, b):
    return lax.dot_general(a, b, (((1,), (1,)), ((), ())), preferred_element_type=F32)


def inv_scale(values):
    return lax.rsqrt(jnp.mean(values * values, axis=-1, keepdims=True) + EPS)


def partner_barrier_signal(partner):
    pl.semaphore_signal(
        pltpu.get_barrier_semaphore(),
        inc=1,
        device_id={"section": partner},
        device_id_type=pl.DeviceIdType.MESH,
    )


def chunk_copy(send, recv, send_sem, recv_sem, slot, partner):
    return pltpu.make_async_remote_copy(
        src_ref=send.at[slot],
        dst_ref=recv.at[slot],
        send_sem=send_sem.at[slot],
        recv_sem=recv_sem.at[slot],
        device_id={"section": partner},
        device_id_type=pl.DeviceIdType.MESH,
    )


def segment_index(width, per_row):
    return lax.broadcasted_iota(jnp.int32, (LANES, width), 0) % per_row


def forward_kernel(
    steps,
    per_row,
    tok,
    keep,
    perm,
    perm_t,
    g_one,
    w_gate,
    b_gate,
    w_cand,
    b_cand,
    w_out,
    b_out,
    g_two,
    w_up,
    b_up,
    w_down,
    b_down,
    out,
    x_o,
    normed_o,
    decay_o,
    slope_forget_o,
    slope_inward_o,
    slope_cand_o,
    state_o,
    middle_o,
    normed_two_o,
    active_o,
    slope_up_o,
    send,
    recv,
    carry,
    send_sem,
    recv_sem,
):
    c = pl.program_id(0)
    section = lax.axis_index("section")
    partner = 1 - section
    rows, chunk, width = tok.shape
    tokens = rows * chunk
    hidden = w_cand.shape[1]
    ff = w_up.shape[1]
    span = tokens // LANES

    @pl.when(c == 0)
    def _():
        partner_barrier_signal(partner)
        carry[...] = jnp.zeros_like(carry)
        pl.semaphore_wait(pltpu.get_barrier_semaphore(), 1)

    @pl.when(section == 0)
    def _():
        x_o[0] = dot(perm[...], tok[...].reshape(tokens, width)).astype(BF16)

    @pl.when(section == 1)
    def _():
        chunk_copy(send, recv, send_sem, recv_sem, c, partner).wait_recv()
        x_o[0] = recv[c]

    x = x_o[0].astype(F32)
    normed = (x * inv_scale(x) * g_one[...]).astype(BF16)
    normed_o[0] = normed
    mixed = jnp.zeros((tokens, width), F32)
    which = segment_index(WIDTH, per_row)
    for at in range(0, hidden, WIDTH):
        cols = slice(at, at + WIDTH)
        cols_in = slice(hidden + at, hidden + at + WIDTH)
        pre_f = dot(normed, w_gate[:, cols])
        pre_i = dot(normed, w_gate[:, cols_in])
        cand = dot(normed, w_cand[:, cols]) + b_cand[:, cols]
        u = jnp.exp(jnp.minimum((-LN4 - b_gate[:, cols]) - pre_f, EXP_TOP))
        v = jnp.exp(jnp.minimum((-LN4 - b_gate[:, cols_in]) - pre_i, EXP_TOP))
        d = 1.0 / (0.5 + u + v)
        ratio_f = (0.25 + v) * d
        ratio_i = (0.25 + u) * d
        keep_w = jnp.concatenate([keep[0]] * (WIDTH // 128), axis=1)
        decay = ratio_f * keep_w
        drive = ratio_i * cand
        decay_o[0, :, cols] = decay
        slope_cand_o[0, :, cols] = ratio_i.astype(BF16)
        product = decay[0:LANES]
        accum = drive[0:LANES]
        for j in range(1, span):
            r = slice(j * LANES, (j + 1) * LANES)
            accum = decay[r] * accum + drive[r]
            product = decay[r] * product
        incoming = carry[:, cols]
        for q in range(1, per_row):
            nxt = pltpu.roll(product * incoming + accum, 1, 0)
            incoming = jnp.where(which == q, nxt, incoming)
        carry[:, cols] = pltpu.roll(product * incoming + accum, LANES - per_row + 1, 0)
        state = incoming
        before = []
        after = []
        for j in range(span):
            r = slice(j * LANES, (j + 1) * LANES)
            before.append(state)
            state = decay[r] * state + drive[r]
            after.append(state)
        state_low = jnp.concatenate(after, axis=0).astype(BF16)
        state_o[0, :, cols] = state_low
        lever = keep_w * jnp.concatenate(before, axis=0) - cand
        slope_forget_o[0, :, cols] = (lever * (u * d) * ratio_f).astype(BF16)
        slope_inward_o[0, :, cols] = (-lever * (v * d) * ratio_i).astype(BF16)
        mixed = mixed + dot(state_low, w_out[cols, :])
    middle = x + (mixed + b_out[...])
    middle_o[0] = middle
    normed_two = (middle * inv_scale(middle) * g_two[...]).astype(BF16)
    normed_two_o[0] = normed_two
    down = jnp.zeros((tokens, width), F32)
    for at in range(0, ff, WIDTH):
        cols = slice(at, at + WIDTH)
        up = dot(normed_two, w_up[:, cols]) + b_up[:, cols]
        square = up * up
        half = 0.5 + 0.5 * jnp.tanh(up * (GELU_A + (GELU_A * GELU_B) * square))
        act = up * half
        active = act.astype(BF16)
        active_o[0, :, cols] = active
        slope = half + act * (1.0 - half) * (2 * GELU_A + (6 * GELU_A * GELU_B) * square)
        slope_up_o[0, :, cols] = slope.astype(BF16)
        down = down + dot(active, w_down[cols, :])
    low = (middle + (down + b_down[...])).astype(BF16)

    @pl.when(section == 0)
    def _():
        send[c] = low
        chunk_copy(send, recv, send_sem, recv_sem, c, partner).start()

    out[...] = dot(perm_t[...], low).astype(BF16).reshape(out.shape)

    @pl.when((c == steps - 1) & (section == 0))
    def _():
        for slot in range(steps):
            chunk_copy(send, recv, send_sem, recv_sem, slot, partner).wait_send()


def backward_kernel(
    steps,
    per_row,
    cot,
    x_i,
    decay_i,
    slope_forget_i,
    slope_inward_i,
    slope_cand_i,
    middle_i,
    slope_up_i,
    perm,
    perm_t,
    g_one,
    w_gate,
    w_cand,
    w_out,
    g_two,
    w_up,
    w_down,
    grad_in,
    down_o,
    up_o,
    mix_o,
    gate_o,
    cand_o,
    small_o,
    send,
    recv,
    carry,
    send_sem,
    recv_sem,
):
    c = pl.program_id(0)
    section = lax.axis_index("section")
    partner = 1 - section
    rows, chunk, width = cot.shape
    tokens = rows * chunk
    hidden = w_cand.shape[1]
    ff = w_up.shape[1]
    span = tokens // LANES
    at_b_gate = width
    at_b_cand = at_b_gate + 2 * hidden
    at_b_out = at_b_cand + hidden
    at_g_two = at_b_out + width
    at_b_up = at_g_two + width
    at_b_down = at_b_up + ff

    def add_small(at, values):
        n = values.shape[1]
        part = jnp.sum(values.reshape(-1, LANES, n), axis=0)
        small_o[:, at : at + n] += part

    @pl.when(c == 0)
    def _():
        partner_barrier_signal(partner)
        carry[...] = jnp.zeros_like(carry)
        small_o[...] = jnp.zeros_like(small_o)
        pl.semaphore_wait(pltpu.get_barrier_semaphore(), 1)

    @pl.when(section == 1)
    def _():
        down_o[0] = dot(perm[...], cot[...].reshape(tokens, width)).astype(BF16)

    @pl.when(section == 0)
    def _():
        chunk_copy(send, recv, send_sem, recv_sem, c, partner).wait_recv()
        down_o[0] = recv[c]

    grad_down = down_o[0]
    dy = grad_down.astype(F32)
    add_small(at_b_down, dy)
    q = jnp.zeros((tokens, width), F32)
    for at in range(0, ff, WIDTH):
        cols = slice(at, at + WIDTH)
        grad_up = dot_nt(grad_down, w_down[cols, :]) * slope_up_i[0, :, cols].astype(F32)
        add_small(at_b_up + at, grad_up)
        grad_up = grad_up.astype(BF16)
        up_o[0, :, cols] = grad_up
        q = q + dot_nt(grad_up, w_up[:, cols])
    middle = middle_i[0]
    r = inv_scale(middle)
    scaled = middle * r
    add_small(at_g_two, q * scaled)
    weighted = q * g_two[...]
    grad_middle = dy + r * (
        weighted - scaled * jnp.mean(weighted * scaled, axis=-1, keepdims=True)
    )
    add_small(at_b_out, grad_middle)
    grad_mix = grad_middle.astype(BF16)
    mix_o[0] = grad_mix
    p = jnp.zeros((tokens, width), F32)
    which = segment_index(WIDTH, per_row)
    for at in range(0, hidden, WIDTH):
        cols = slice(at, at + WIDTH)
        cols_in = slice(hidden + at, hidden + at + WIDTH)
        grad_state = dot_nt(grad_mix, w_out[cols, :])
        decay = decay_i[0, :, cols]
        last = slice((span - 1) * LANES, span * LANES)
        product = decay[last]
        accum = decay[last] * grad_state[last]
        for j in range(span - 2, -1, -1):
            rj = slice(j * LANES, (j + 1) * LANES)
            accum = decay[rj] * (grad_state[rj] + accum)
            product = decay[rj] * product
        incoming = carry[:, cols]
        for k in range(per_row - 2, -1, -1):
            nxt = pltpu.roll(product * incoming + accum, LANES - 1, 0)
            incoming = jnp.where(which == k, nxt, incoming)
        carry[:, cols] = pltpu.roll(product * incoming + accum, per_row - 1, 0)
        later = incoming
        parts = [None] * span
        for j in range(span - 1, -1, -1):
            rj = slice(j * LANES, (j + 1) * LANES)
            carried = grad_state[rj] + later
            parts[j] = carried
            later = decay[rj] * carried
        carried = jnp.concatenate(parts, axis=0)
        grad_forget = carried * slope_forget_i[0, :, cols].astype(F32)
        grad_inward = carried * slope_inward_i[0, :, cols].astype(F32)
        grad_cand = carried * slope_cand_i[0, :, cols].astype(F32)
        add_small(at_b_gate + at, grad_forget)
        add_small(at_b_gate + hidden + at, grad_inward)
        add_small(at_b_cand + at, grad_cand)
        grad_forget = grad_forget.astype(BF16)
        grad_inward = grad_inward.astype(BF16)
        grad_cand = grad_cand.astype(BF16)
        gate_o[0, :, cols] = grad_forget
        gate_o[0, :, cols_in] = grad_inward
        cand_o[0, :, cols] = grad_cand
        p = p + dot_nt(grad_forget, w_gate[:, cols])
        p = p + dot_nt(grad_inward, w_gate[:, cols_in])
        p = p + dot_nt(grad_cand, w_cand[:, cols])
    x = x_i[0].astype(F32)
    r = inv_scale(x)
    scaled = x * r
    add_small(0, p * scaled)
    weighted = p * g_one[...]
    grad_input = grad_middle + r * (
        weighted - scaled * jnp.mean(weighted * scaled, axis=-1, keepdims=True)
    )
    low = grad_input.astype(BF16)

    @pl.when(section == 1)
    def _():
        send[c] = low
        chunk_copy(send, recv, send_sem, recv_sem, c, partner).start()

    rest = jnp.where(section == 0, grad_input - low.astype(F32), 0.0).astype(BF16)
    grad_in[...] = (dot(perm_t[...], low) + dot(perm_t[...], rest)).reshape(grad_in.shape)

    @pl.when((c == steps - 1) & (section == 1))
    def _():
        for slot in range(steps):
            chunk_copy(send, recv, send_sem, recv_sem, slot, partner).wait_send()


def whole(array):
    zeros = (0,) * array.ndim
    return pl.BlockSpec(array.shape, lambda c: zeros, pipeline_mode=pl.Buffered(1))


def run_forward(tokens, keep, perm, perm_t, weights, chunk):
    rows, seq, width = tokens.shape
    steps = seq // chunk
    size = rows * chunk
    hidden = weights[3].shape[1]
    ff = weights[8].shape[1]

    def saved(columns, dtype):
        shape = jax.ShapeDtypeStruct((steps, size, columns), dtype)
        return shape, pl.BlockSpec((1, size, columns), lambda c: (c, 0, 0))

    out = (
        jax.ShapeDtypeStruct((1, rows, seq, width), BF16),
        pl.BlockSpec((1, rows, chunk, width), lambda c: (0, 0, c, 0)),
    )
    outs = [
        out,
        saved(width, BF16),
        saved(width, BF16),
        saved(hidden, F32),
        saved(hidden, BF16),
        saved(hidden, BF16),
        saved(hidden, BF16),
        saved(hidden, BF16),
        saved(width, F32),
        saved(width, BF16),
        saved(ff, BF16),
        saved(ff, BF16),
    ]
    return pl.pallas_call(
        functools.partial(forward_kernel, steps, LANES // rows),
        grid=(steps,),
        out_shape=[o[0] for o in outs],
        in_specs=[
            pl.BlockSpec((rows, chunk, width), lambda c: (0, c, 0)),
            pl.BlockSpec((1, size, 128), lambda c: (c, 0, 0)),
            whole(perm),
            whole(perm_t),
        ]
        + [whole(w) for w in weights],
        out_specs=[o[1] for o in outs],
        scratch_shapes=[
            pltpu.VMEM((steps, size, width), BF16),
            pltpu.VMEM((steps, size, width), BF16),
            pltpu.VMEM((LANES, hidden), F32),
            pltpu.SemaphoreType.DMA((steps,)),
            pltpu.SemaphoreType.DMA((steps,)),
        ],
        compiler_params=pltpu.CompilerParams(
            collective_id=0, has_side_effects=True, vmem_limit_bytes=VMEM_LIMIT
        ),
        name="forward_block",
    )(tokens, keep, perm, perm_t, *weights)


def run_backward(cotangent, saved_vals, perm, perm_t, weights, chunk):
    rows, seq, width = cotangent.shape
    steps = seq // chunk
    size = rows * chunk
    g_one, w_gate, _, w_cand, _, w_out, _, g_two, w_up, _, w_down, _ = weights
    hidden = w_cand.shape[1]
    ff = w_up.shape[1]
    small = 4 * width + 3 * hidden + ff

    def back(c):
        return (steps - 1 - c, 0, 0)

    def given(columns, dtype):
        shape = jax.ShapeDtypeStruct((steps, size, columns), dtype)
        return shape, pl.BlockSpec((1, size, columns), back)

    outs = [
        (
            jax.ShapeDtypeStruct((1, rows, seq, width), F32),
            pl.BlockSpec((1, rows, chunk, width), lambda c: (0, 0, steps - 1 - c, 0)),
        ),
        given(width, BF16),
        given(ff, BF16),
        given(width, BF16),
        given(2 * hidden, BF16),
        given(hidden, BF16),
        (
            jax.ShapeDtypeStruct((LANES, small), F32),
            pl.BlockSpec((LANES, small), lambda c: (0, 0)),
        ),
    ]
    consts = (perm, perm_t, g_one, w_gate, w_cand, w_out, g_two, w_up, w_down)
    return pl.pallas_call(
        functools.partial(backward_kernel, steps, LANES // rows),
        grid=(steps,),
        out_shape=[o[0] for o in outs],
        in_specs=[pl.BlockSpec((rows, chunk, width), lambda c: (0, steps - 1 - c, 0))]
        + [pl.BlockSpec((1, size, v.shape[2]), back) for v in saved_vals]
        + [whole(w) for w in consts],
        out_specs=[o[1] for o in outs],
        scratch_shapes=[
            pltpu.VMEM((steps, size, width), BF16),
            pltpu.VMEM((steps, size, width), BF16),
            pltpu.VMEM((LANES, hidden), F32),
            pltpu.SemaphoreType.DMA((steps,)),
            pltpu.SemaphoreType.DMA((steps,)),
        ],
        compiler_params=pltpu.CompilerParams(
            collective_id=1, has_side_effects=True, vmem_limit_bytes=VMEM_LIMIT
        ),
        name="backward_block",
    )(cotangent, *saved_vals, *consts)


def local_grads(tokens, resets, cotangent, stacked):
    weights = tuple(w if w.ndim == 2 else w[0] for w in stacked)
    rows, seq, width = tokens.shape
    chunk = min(CHUNK, seq)
    steps = seq // chunk
    size = rows * chunk
    per_row = LANES // rows
    span = size // LANES
    keep = (1 - resets).astype(F32).reshape(rows, steps, per_row, span)
    keep = keep.transpose(1, 3, 0, 2).reshape(steps, size, 1)
    keep = jnp.broadcast_to(keep, (steps, size, 128))
    at = lax.broadcasted_iota(jnp.int32, (size, size), 0)
    source = lax.broadcasted_iota(jnp.int32, (size, size), 1)
    perm = (source == (at % LANES) * span + at // LANES).astype(BF16)
    perm_t = (at == (source % LANES) * span + source // LANES).astype(BF16)
    (
        block_out,
        x,
        normed,
        decay,
        slope_forget,
        slope_inward,
        slope_cand,
        state_low,
        middle,
        normed_two,
        active,
        slope_up,
    ) = run_forward(tokens, keep, perm, perm_t, weights, chunk)
    grad_in, g_down, g_up, g_mix, g_gate, g_cand, small = run_backward(
        cotangent,
        (x, decay, slope_forget, slope_inward, slope_cand, middle, slope_up),
        perm,
        perm_t,
        weights,
        chunk,
    )
    operands = (active, g_down, g_up, normed_two, g_gate, normed, g_cand, state_low, g_mix)
    return block_out, grad_in, operands, jnp.sum(small, axis=0)


class Ring:
    def __init__(self):
        dp_size = lax.axis_size("dp")
        rep_size = lax.axis_size("rep")
        chips = dp_size // 2
        self.inner = 4 if chips % 4 == 0 else chips
        self.size = self.inner * rep_size
        dp = lax.axis_index("dp")
        self.rep = lax.axis_index("rep")
        self.core = dp % 2
        self.base = (dp // 2) // self.inner * self.inner
        self.spot = (dp // 2) % self.inner
        self.at = self.rep * self.inner + jnp.where(
            self.rep % 2 == 0, self.spot, self.inner - 1 - self.spot
        )
        self.rep_size = rep_size

    def device(self, place):
        rep = place // self.inner
        spot = place % self.inner
        spot = jnp.where(rep % 2 == 0, spot, self.inner - 1 - spot)
        return {"dp": (self.base + spot) * 2 + self.core, "rep": rep}

    def next(self, direction):
        step = 1 if direction == 0 else self.size - 1
        return self.device((self.at + step) % self.size)

    def shard(self, direction, back):
        step = self.size - back if direction == 0 else back
        return (self.at + step) % self.size

    def other_core(self):
        return {"dp": (self.base + self.spot) * 2 + 1 - self.core}

    def doubling(self):
        found = [self.other_core()]
        span = 1
        while span < self.inner:
            flip = self.spot + span - 2 * span * ((self.spot // span) % 2)
            found.append({"dp": (self.base + flip) * 2 + self.core})
            span *= 2
        span = 1
        while span < self.rep_size:
            found.append({"rep": self.rep + span - 2 * span * ((self.rep // span) % 2)})
            span *= 2
        return found


def remote(src, dst, send_sem, recv_sem, device):
    return pltpu.make_async_remote_copy(
        src_ref=src,
        dst_ref=dst,
        send_sem=send_sem,
        recv_sem=recv_sem,
        device_id=device,
        device_id_type=pl.DeviceIdType.MESH,
    )


def sum_kernel(
    ring_size,
    rounds,
    active,
    down,
    up,
    normed_two,
    gate,
    normed,
    cand,
    state,
    mix,
    small,
    out,
    small_out,
    wide,
    narrow,
    turned,
    own,
    leave,
    core_in,
    first,
    partial,
    result,
    small_buf,
    wide_sem,
    narrow_sem,
    core_sem,
    rs_send,
    rs_recv,
    ag_send,
    ag_recv,
    keep_sem,
    pair_sem,
    small_sem,
):
    ring = Ring()
    width = down.shape[1]
    groups = out.shape[0]
    half_rows = out.shape[2]
    side_rows = half_rows // 2
    block = side_rows // ring_size
    core = ring.core
    away = 1 - core
    pair = ring.other_core()
    following = [ring.next(0), ring.next(1)]
    doubling = ring.doubling()

    barrier = pltpu.get_barrier_semaphore()
    peers = following + doubling
    for peer in peers:
        pl.semaphore_signal(
            barrier, inc=1, device_id=peer, device_id_type=pl.DeviceIdType.MESH
        )

    sources = [(active, down), (up, normed_two), (gate, normed), (None, mix)]

    def wide_copy(g, half, t):
        slot = g % 2
        to = wide.at[slot, t, half]
        if g < 3:
            cols = pl.ds(pl.multiple_of((half * 2 + t) * width, width), width)
            src = sources[g][0].at[:, cols]
        else:
            cols = pl.ds(pl.multiple_of(half * width, width), width)
            src = (cand, state)[t].at[:, cols]
        return pltpu.make_async_copy(src, to, wide_sem.at[slot, t, half])

    def narrow_copy(g):
        return pltpu.make_async_copy(
            sources[g][1], narrow.at[g % 2], narrow_sem.at[g % 2]
        )

    def load(g):
        narrow_copy(g).start()
        for half in (away, core):
            for t in range(2):
                wide_copy(g, half, t).start()

    def rows_of(direction, shard):
        return pl.ds(pl.multiple_of(direction * side_rows + shard * block, block), block)

    def core_copy(g, direction):
        rows = pl.ds(direction * side_rows, side_rows)
        return remote(
            leave.at[g, rows],
            core_in.at[g, rows],
            core_sem.at[0, g, direction],
            core_sem.at[1, g, direction],
            pair,
        )

    def rs_copy(g, direction, k):
        src = first.at[g, direction] if k == 0 else partial.at[g, direction, k - 1]
        return remote(
            src,
            partial.at[g, direction, k],
            rs_send.at[g, direction],
            rs_recv.at[g, direction, k],
            following[direction],
        )

    def ag_copy(g, direction, k):
        rows = rows_of(direction, ring.shard(direction, k))
        return remote(
            result.at[g, rows],
            result.at[g, rows],
            ag_send.at[g, direction],
            ag_recv.at[g, direction, k],
            following[direction],
        )

    def hand_out(g, direction, k):
        rows = rows_of(direction, ring.shard(direction, k))
        pltpu.make_async_copy(
            result.at[g, rows], out.at[g, core, rows], keep_sem.at[g, direction]
        ).start()
        remote(
            result.at[g, rows],
            out.at[g, core, rows],
            pair_sem.at[0, g, direction],
            pair_sem.at[1, g, direction],
            pair,
        ).start()

    def mine(g, rows):
        return own[g, rows, :] + core_in[g, rows, :].astype(F32)

    last = ring_size - 1

    def advance(g, stage):
        for direction in range(2):
            if stage == 0:
                core_copy(g, direction).wait_recv()
                rows = rows_of(direction, ring.shard(direction, 1))
                first[g, direction] = mine(g, rows).astype(BF16)
                rs_copy(g, direction, 0).start()
            elif stage <= last:
                k = stage - 1
                rs_copy(g, direction, k).wait_recv()
                rows = rows_of(direction, ring.shard(direction, k + 2))
                total = partial[g, direction, k].astype(F32) + mine(g, rows)
                if k < last - 1:
                    partial[g, direction, k] = total.astype(BF16)
                    rs_copy(g, direction, k + 1).start()
                else:
                    result[g, rows, :] = total.astype(BF16)
                    ag_copy(g, direction, 0).start()
                    hand_out(g, direction, 0)
            else:
                k = stage - last - 1
                rows = rows_of(direction, ring.shard(direction, k + 1))
                remote(
                    result.at[g, rows],
                    result.at[g, rows],
                    ag_send.at[g, direction],
                    ag_recv.at[g, direction, k],
                    following[direction],
                ).wait_recv()
                if k < last - 1:
                    ag_copy(g, direction, k + 1).start()
                hand_out(g, direction, k + 1)

    def small_copy(k):
        return remote(
            small_buf.at[0, k],
            small_buf.at[1, k],
            small_sem.at[0, k],
            small_sem.at[1, k],
            doubling[k],
        )

    def small_round(k):
        if k == 0:
            total = small[...]
        else:
            small_copy(k - 1).wait()
            total = small_buf[0, k - 1] + small_buf[1, k - 1]
        if k < rounds:
            small_buf[0, k] = total
            small_copy(k).start()
        else:
            small_out[...] = total

    stages = 2 * last + 1
    progress = [0] * groups
    small_at = 0

    load(0)
    for g in range(groups):
        if g + 1 < groups:
            load(g + 1)
        narrow_copy(g).wait()
        turned[g % 2] = narrow[g % 2].T
        for half in (away, core):
            for t in range(2):
                wide_copy(g, half, t).wait()
                left = turned[(g if g < 3 or t == 1 else 2) % 2]
                tile = dot(left, wide[g % 2, t, half])
                if g == 0 or (g == 3 and t == 1):
                    tile = tile.T
                rows = pl.ds(t * width, width)
                if half is away:
                    leave[g, rows, :] = tile.astype(BF16)
                else:
                    own[g, rows, :] = tile
            if half is away:
                if g == 0:
                    pl.semaphore_wait(barrier, len(peers))
                for direction in range(2):
                    core_copy(g, direction).start()
            if small_at <= rounds:
                small_round(small_at)
                small_at += 1
            for k in range(g):
                advance(k, progress[k])
                progress[k] += 1
    while min(progress) < stages:
        behind = sorted((k for k in range(groups) if progress[k] < stages), key=lambda k: progress[k])
        for k in behind[:3]:
            advance(k, progress[k])
            progress[k] += 1
        if small_at <= rounds:
            small_round(small_at)
            small_at += 1
    while small_at <= rounds:
        small_round(small_at)
        small_at += 1

    for g in range(groups):
        for direction in range(2):
            rows = pl.ds(direction * side_rows, side_rows)
            core_copy(g, direction).wait_send()
            sent = partial.at[g, direction]
            remote(sent, sent, rs_send.at[g, direction], rs_recv.at[g, direction, 0], pair).wait_send()
            sent = result.at[g, pl.ds(direction * side_rows, last * block)]
            remote(sent, sent, ag_send.at[g, direction], ag_recv.at[g, direction, 0], pair).wait_send()
            pltpu.make_async_copy(
                result.at[g, rows], out.at[g, core, rows], keep_sem.at[g, direction]
            ).wait()
            whole_side = remote(
                result.at[g, rows],
                out.at[g, away, rows],
                pair_sem.at[0, g, direction],
                pair_sem.at[1, g, direction],
                pair,
            )
            whole_side.wait_send()
            whole_side.wait_recv()


def unpack_kernel(down_i, up_i, gate_i, cand_i, out_i, w_gate, w_cand, w_out, w_up, w_down):
    for source, target in (
        (down_i, w_down),
        (up_i, w_up),
        (gate_i, w_gate),
        (cand_i, w_cand),
        (out_i, w_out),
    ):
        target[0] = source[0].astype(F32)


def unpack(packed, width, hidden, ff):
    packed = packed.reshape(4, ff, width)
    parts = 8
    tall = ff // parts
    short = tall // 2
    spread = width // tall
    per_tile = width // short

    def column_block(t):
        return (0, t % spread, t // spread)

    return pl.pallas_call(
        unpack_kernel,
        grid=(parts,),
        out_shape=[
            jax.ShapeDtypeStruct((1, width, 2 * hidden), F32),
            jax.ShapeDtypeStruct((1, width, hidden), F32),
            jax.ShapeDtypeStruct((1, hidden, width), F32),
            jax.ShapeDtypeStruct((1, width, ff), F32),
            jax.ShapeDtypeStruct((1, ff, width), F32),
        ],
        in_specs=[
            pl.BlockSpec((1, tall, width), lambda t: (0, t, 0)),
            pl.BlockSpec((1, tall, width), lambda t: (1, t, 0)),
            pl.BlockSpec((1, tall, width), lambda t: (2, t, 0)),
            pl.BlockSpec(
                (1, short, width),
                lambda t: (3, t // per_tile * 2 * per_tile + t % per_tile, 0),
            ),
            pl.BlockSpec(
                (1, short, width),
                lambda t: (3, t // per_tile * 2 * per_tile + per_tile + t % per_tile, 0),
            ),
        ],
        out_specs=[
            pl.BlockSpec((1, tall, width), column_block),
            pl.BlockSpec((1, short, width), lambda t: (0, t % per_tile, t // per_tile)),
            pl.BlockSpec((1, short, width), lambda t: (0, t, 0)),
            pl.BlockSpec((1, tall, width), column_block),
            pl.BlockSpec((1, tall, width), lambda t: (0, t, 0)),
        ],
        name="unpack",
    )(packed, packed, packed, packed, packed)


def sum_gradients(operands, small, hidden, ff):
    ring = Ring()
    n = ring.size
    rounds = len(ring.doubling())
    operands = [a.reshape(-1, a.shape[-1]) for a in operands]
    tokens, width = operands[1].shape
    groups = 4
    half_rows = ff // 2
    side_rows = half_rows // 2
    block = side_rows // n
    anywhere = pl.BlockSpec(memory_space=pl.ANY)
    here = pl.BlockSpec(memory_space=pltpu.VMEM)
    packed, small_sum = pl.pallas_call(
        functools.partial(sum_kernel, n, rounds),
        out_shape=[
            jax.ShapeDtypeStruct((groups, 2, half_rows, width), BF16),
            jax.ShapeDtypeStruct(small.shape, F32),
        ],
        in_specs=[anywhere] * 9 + [here],
        out_specs=[anywhere, here],
        scratch_shapes=[
            pltpu.VMEM((2, 2, 2, tokens, width), BF16),
            pltpu.VMEM((2, tokens, width), BF16),
            pltpu.VMEM((2, width, tokens), BF16),
            pltpu.VMEM((groups, half_rows, width), F32),
            pltpu.VMEM((groups, half_rows, width), BF16),
            pltpu.VMEM((groups, half_rows, width), BF16),
            pltpu.VMEM((groups, 2, block, width), BF16),
            pltpu.VMEM((groups, 2, n - 1, block, width), BF16),
            pltpu.VMEM((groups, half_rows, width), BF16),
            pltpu.VMEM((2, rounds) + small.shape, F32),
            pltpu.SemaphoreType.DMA((2, 2, 2)),
            pltpu.SemaphoreType.DMA((2,)),
            pltpu.SemaphoreType.DMA((2, groups, 2)),
            pltpu.SemaphoreType.DMA((groups, 2)),
            pltpu.SemaphoreType.DMA((groups, 2, n - 1)),
            pltpu.SemaphoreType.DMA((groups, 2)),
            pltpu.SemaphoreType.DMA((groups, 2, n - 1)),
            pltpu.SemaphoreType.DMA((groups, 2)),
            pltpu.SemaphoreType.DMA((2, groups, 2)),
            pltpu.SemaphoreType.DMA((2, rounds)),
        ],
        compiler_params=pltpu.CompilerParams(
            collective_id=2, has_side_effects=True, vmem_limit_bytes=VMEM_LIMIT
        ),
        name="sum_gradients",
    )(*operands, small)
    dp_size = lax.axis_size("dp")
    inner = 2 * ring.inner
    if dp_size > inner:
        members = [list(range(i, dp_size, inner)) for i in range(inner)]
        packed, small_sum = lax.psum((packed, small_sum), "dp", axis_index_groups=members)
    return unpack(packed, width, hidden, ff), small_sum


def split_small(small, width, hidden, ff):
    sizes = (width, 2 * hidden, hidden, width, width, ff, width)
    out = []
    at = 0
    for n in sizes:
        out.append(small[at : at + n])
        at += n
    return out


def body(tokens, resets, cotangent, *stacked):
    block_out, grad_in, operands, small = local_grads(tokens, resets, cotangent, stacked)
    width = tokens.shape[2]
    hidden = stacked[3].shape[2]
    ff = stacked[8].shape[2]
    large, small_sum = sum_gradients(operands, small.reshape(LANES, -1), hidden, ff)
    w_gate, w_cand, w_out, w_up, w_down = large
    g_one, b_gate, b_cand, b_out, g_two, b_up, b_down = split_small(
        small_sum.reshape(-1), width, hidden, ff
    )
    grads = (g_one, w_gate, b_gate, w_cand, b_cand, w_out, b_out, g_two, w_up, b_up, w_down, b_down)
    return (block_out, grad_in) + tuple(g if g.ndim == 3 else g[None] for g in grads)


def solution(mesh):
    vector = P("section", None)
    matrix = P("section", None, None)
    weight_specs = (
        vector,
        matrix,
        vector,
        matrix,
        vector,
        matrix,
        vector,
        vector,
        matrix,
        vector,
        matrix,
        vector,
    )
    tokens = P(("dp", "rep"), None, None)
    by_rows = P("section", ("dp", "rep"), None, None)
    return jax.shard_map(
        body,
        mesh=mesh,
        in_specs=(tokens, P(("dp", "rep"), None), tokens) + weight_specs,
        out_specs=(by_rows, by_rows) + weight_specs,
        check_vma=False,
    )
```

```python
import functools
import math

import jax
import jax.numpy as jnp
from jax import lax
from jax.experimental import pallas as pl
from jax.experimental.pallas import tpu as pltpu
from jax.sharding import PartitionSpec as P

EPS = 1e-06
F32 = jnp.float32
BF16 = jnp.bfloat16
CHUNK = 256
LANES = 8
WIDTH = 256
GELU_A = math.sqrt(2.0 / math.pi)
GELU_B = 0.044715
LN4 = math.log(4.0)
EXP_TOP = 85.6
VMEM_LIMIT = 60 * 1024 * 1024
BLOCKS_VMEM = 63 * 1024 * 1024


def dot(a, b):
    return jnp.dot(a, b, preferred_element_type=F32)


def dot_nt(a, b):
    return lax.dot_general(a, b, (((1,), (1,)), ((), ())), preferred_element_type=F32)


def inv_scale(values):
    return lax.rsqrt(jnp.mean(values * values, axis=-1, keepdims=True) + EPS)


def partner_barrier_signal(partner):
    pl.semaphore_signal(
        pltpu.get_barrier_semaphore(),
        inc=1,
        device_id={"section": partner},
        device_id_type=pl.DeviceIdType.MESH,
    )


def interleave(*streams):
    live = list(streams)
    while live:
        for stream in list(live):
            if next(stream, live) is live:
                live.remove(stream)


def scan_segments(product, accum, carry, reverse):
    which = lax.broadcasted_iota(jnp.int32, product.shape, 0)
    span = 1
    while span < LANES:
        turn = LANES - span if reverse else span
        inside = which < LANES - span if reverse else which >= span
        accum = jnp.where(inside, product * pltpu.roll(accum, turn, 0) + accum, accum)
        product = jnp.where(inside, product * pltpu.roll(product, turn, 0), product)
        span *= 2
    reached = product * carry + accum
    edge = LANES - 1 if reverse else 0
    incoming = jnp.where(which == edge, carry, pltpu.roll(reached, LANES - 1 if reverse else 1, 0))
    end = 0 if reverse else LANES - 1
    return incoming, jnp.broadcast_to(reached[end : end + 1], reached.shape)


class Step:
    def __init__(self, step, rows, chunks):
        first = lax.axis_index("section") == 0
        phase = step // (chunks + 1)
        self.at = step % (chunks + 1)
        self.forward = jnp.where(first, phase < rows, phase % 2 == 0)
        self.row = jnp.where(first, phase % rows, phase // 2)
        base = self.row * chunks
        last = chunks - 1
        before = jnp.where(first, last, jnp.maximum(base - chunks, jnp.where(self.row == 0, last, 0)))
        after = jnp.where(first, rows * chunks - 1, base + last)
        self.mixer = jnp.where(self.forward, base + jnp.minimum(self.at, last), after)
        self.feed = jnp.where(self.forward, base + jnp.maximum(self.at - 1, 0), after)
        self.back_feed = jnp.where(self.forward, before, base + jnp.maximum(last - self.at, 0))
        self.back_mixer = jnp.where(self.forward, before, base + jnp.minimum(chunks - self.at, last))
        self.next_mixer = jnp.minimum(self.mixer + 1, rows * chunks - 1)
        later = jnp.minimum(base + self.at + 1, rows * chunks - 1)
        later = jnp.where(self.forward, base, jnp.minimum(later, base + chunks))
        later = jnp.minimum(later, rows * chunks - 1)
        self.next_back = later // chunks * chunks + last - later % chunks


def blocks_kernel(
    rows,
    chunks,
    first_tok,
    tok,
    first_cot,
    cot,
    keep,
    perm,
    g_one,
    w_gate,
    b_gate,
    w_cand,
    b_cand,
    w_out,
    b_out,
    g_two,
    w_up,
    b_up,
    w_down,
    b_down,
    operands_o,
    active_o,
    low_o,
    down_o,
    up_o,
    mix_o,
    gate_o,
    cand_o,
    grad_in,
    small_o,
    ratio_s,
    slopes_s,
    middle_s,
    slope_up_s,
    inputs,
    send,
    received,
    coming,
    coming_back,
    carry,
    carry_back,
    normed_two_s,
    grad_middle_s,
    mix_s,
    send_sem,
    input_sem,
    back_send_sem,
    received_sem,
):
    c = pl.program_id(0)
    section = lax.axis_index("section")
    partner = 1 - section
    step = Step(c, rows, chunks)
    _, tokens, width = tok.shape
    hidden = w_cand.shape[1]
    ff = w_up.shape[1]
    span = tokens // LANES
    total = rows * chunks
    final = 2 * rows * (chunks + 1) - 1

    def chunk_copy(slot):
        return remote(
            send.at[slot],
            inputs.at[slot],
            send_sem.at[slot],
            input_sem.at[slot],
            {"section": partner},
        )

    def back_copy(slot):
        return remote(
            send.at[slot],
            received.at[slot],
            back_send_sem.at[slot],
            received_sem.at[slot],
            {"section": partner},
        )

    def add_small(which, values):
        part = jnp.sum(values.reshape(-1, LANES, width), axis=0)
        small_o[:, which * width : (which + 1) * width] += part

    @pl.when(c == 0)
    def _():
        partner_barrier_signal(partner)
        small_o[...] = jnp.zeros_like(small_o)
        coming[...] = dot(perm[...], first_tok[0]).astype(BF16)
        coming_back[...] = dot(perm[...], first_cot[0]).astype(BF16)
        pl.semaphore_wait(pltpu.get_barrier_semaphore(), 1)

    @pl.when(step.forward & (step.at == 0))
    def _():
        carry[...] = jnp.zeros_like(carry)

    @pl.when(jnp.logical_not(step.forward) & (step.at == 0))
    def _():
        carry_back[...] = jnp.zeros_like(carry_back)

    @pl.when(step.forward & (step.at < chunks) & (section == 0))
    def _():
        inputs[step.mixer] = coming[...]

    @pl.when(step.forward & (step.at < chunks) & (section == 1))
    def _():
        chunk_copy(step.mixer).wait_recv()

    @pl.when(jnp.logical_not(step.forward) & (step.at < chunks) & (section == 0))
    def _():
        back_copy(step.back_feed).wait_recv()
        coming_back[...] = received[step.back_feed]

    def mixer():
        at_chunk = step.mixer
        x = inputs[at_chunk].astype(F32)
        normed = (x * inv_scale(x) * g_one[...]).astype(BF16)
        operands_o[0, :, :width] = normed
        yield
        for at in range(0, hidden, WIDTH):
            cols = slice(at, at + WIDTH)
            cols_in = slice(hidden + at, hidden + at + WIDTH)
            pre_f = dot(normed, w_gate[:, cols])
            pre_i = dot(normed, w_gate[:, cols_in])
            cand = dot(normed, w_cand[:, cols]) + b_cand[:, cols]
            u = jnp.exp(jnp.minimum((-LN4 - b_gate[:, cols]) - pre_f, EXP_TOP))
            v = jnp.exp(jnp.minimum((-LN4 - b_gate[:, cols_in]) - pre_i, EXP_TOP))
            d = 1.0 / (0.5 + u + v)
            ratio_f = (0.25 + v) * d
            ratio_i = (0.25 + u) * d
            ratio_s[at_chunk, :, cols] = ratio_f
            keep_w = jnp.concatenate([keep[0]] * (WIDTH // 128), axis=1)
            decay = ratio_f * keep_w
            drive = ratio_i * cand
            product = decay[0:LANES]
            accum = drive[0:LANES]
            for j in range(1, span):
                r = slice(j * LANES, (j + 1) * LANES)
                accum = decay[r] * accum + drive[r]
                product = decay[r] * product
            state, carry[:, cols] = scan_segments(product, accum, carry[:, cols], False)
            before = []
            after = []
            for j in range(span):
                r = slice(j * LANES, (j + 1) * LANES)
                before.append(state)
                state = decay[r] * state + drive[r]
                after.append(state)
            operands_o[0, :, width + at : width + at + WIDTH] = jnp.concatenate(
                after, axis=0
            ).astype(BF16)
            lever = keep_w * jnp.concatenate(before, axis=0) - cand
            slopes_s[at_chunk, :, cols] = (lever * ((u * d) * ratio_f)).astype(BF16)
            slopes_s[at_chunk, :, cols_in] = (-lever * ((v * d) * ratio_i)).astype(BF16)
            yield
        mixed = dot(operands_o[0, :, width : width + hidden], w_out[...])
        yield
        middle = x + (mixed + b_out[...])
        normed_two = (middle * inv_scale(middle) * g_two[...]).astype(BF16)
        operands_o[0, :, width + hidden :] = normed_two
        yield
        middle_s[at_chunk] = middle
        normed_two_s[...] = normed_two

    def feed():
        at_chunk = step.feed
        for at in range(0, ff, WIDTH):
            cols = slice(at, at + WIDTH)
            up = dot(normed_two_s[...], w_up[:, cols]) + b_up[:, cols]
            square = up * up
            half = 0.5 + 0.5 * jnp.tanh(up * (GELU_A + (GELU_A * GELU_B) * square))
            act = up * half
            active_o[0, :, cols] = act.astype(BF16)
            slope = half + act * (1.0 - half) * (2 * GELU_A + (6 * GELU_A * GELU_B) * square)
            slope_up_s[at_chunk, :, cols] = slope.astype(BF16)
            if at % (2 * WIDTH):
                yield
        down = dot(active_o[0], w_down[...])
        yield
        low_o[0] = (middle_s[at_chunk] + (down + b_down[...])).astype(BF16)

    def reorder():
        yield
        yield
        coming[...] = dot(perm[...], tok[0]).astype(BF16)

    def back_feed():
        at_chunk = step.back_feed
        grad_down = coming_back[...]
        down_o[0] = grad_down
        yield
        for at in range(0, ff, WIDTH):
            cols = slice(at, at + WIDTH)
            grad_active = dot_nt(grad_down, w_down[cols, :])
            slope = slope_up_s[at_chunk, :, cols].astype(F32)
            up_o[0, :, cols] = (grad_active * slope).astype(BF16)
            if at % (2 * WIDTH):
                yield
        q = dot_nt(up_o[0], w_up[...])
        yield
        dy = grad_down.astype(F32)
        add_small(3, dy)
        middle = middle_s[at_chunk]
        r = inv_scale(middle)
        scaled = middle * r
        add_small(2, q * scaled)
        weighted = q * g_two[...]
        grad_middle = dy + r * (
            weighted - scaled * jnp.mean(weighted * scaled, axis=-1, keepdims=True)
        )
        add_small(1, grad_middle)
        grad_mix = grad_middle.astype(BF16)
        mix_o[0] = grad_mix
        yield
        yield
        grad_middle_s[...] = grad_middle
        mix_s[...] = grad_mix

    def back_mixer():
        at_chunk = step.back_mixer
        for at in range(0, hidden, WIDTH):
            cols = slice(at, at + WIDTH)
            cols_in = slice(hidden + at, hidden + at + WIDTH)
            grad_state = dot_nt(mix_s[...], w_out[cols, :])
            ratio_f = ratio_s[at_chunk, :, cols]
            decay = ratio_f * jnp.concatenate([keep[0]] * (WIDTH // 128), axis=1)
            last = slice((span - 1) * LANES, span * LANES)
            product = decay[last]
            accum = decay[last] * grad_state[last]
            for j in range(span - 2, -1, -1):
                rj = slice(j * LANES, (j + 1) * LANES)
                accum = decay[rj] * (grad_state[rj] + accum)
                product = decay[rj] * product
            later, carry_back[:, cols] = scan_segments(product, accum, carry_back[:, cols], True)
            parts = [None] * span
            for j in range(span - 1, -1, -1):
                rj = slice(j * LANES, (j + 1) * LANES)
                carried = grad_state[rj] + later
                parts[j] = carried
                later = decay[rj] * carried
            carried = jnp.concatenate(parts, axis=0)
            gate_o[0, :, cols] = (carried * slopes_s[at_chunk, :, cols].astype(F32)).astype(BF16)
            gate_o[0, :, cols_in] = (
                carried * slopes_s[at_chunk, :, cols_in].astype(F32)
            ).astype(BF16)
            cand_o[0, :, cols] = (carried * (1.0 - ratio_f)).astype(BF16)
            yield
        p = dot_nt(gate_o[0], w_gate[...]) + dot_nt(cand_o[0], w_cand[...])
        yield
        x = inputs[at_chunk].astype(F32)
        r = inv_scale(x)
        scaled = x * r
        add_small(0, p * scaled)
        weighted = p * g_one[...]
        grad_in[0] = grad_middle_s[...] + r * (
            weighted - scaled * jnp.mean(weighted * scaled, axis=-1, keepdims=True)
        )

    def back_reorder():
        yield
        yield
        coming_back[...] = dot(perm[...], cot[0]).astype(BF16)

    opening = step.at == 0
    closing = step.at == chunks
    between = jnp.logical_not(opening | closing)
    backward = jnp.logical_not(step.forward)

    @pl.when(step.forward & opening)
    def _():
        interleave(mixer(), reorder())

    @pl.when(step.forward & between)
    def _():
        interleave(mixer(), feed(), reorder())

    @pl.when(step.forward & closing)
    def _():
        interleave(feed())

    @pl.when(backward & opening)
    def _():
        interleave(back_feed(), back_reorder())

    @pl.when(backward & between)
    def _():
        interleave(back_feed(), back_mixer(), back_reorder())

    @pl.when(backward & closing)
    def _():
        interleave(back_mixer())

    @pl.when(step.forward & jnp.logical_not(opening) & (section == 0))
    def _():
        send[step.feed] = low_o[0]
        chunk_copy(step.feed).start()

    @pl.when(backward & jnp.logical_not(opening) & (section == 1))
    def _():
        send[step.back_mixer] = grad_in[0].astype(BF16)
        back_copy(step.back_mixer).start()

    @pl.when((c == final) & (section == 0))
    def _():
        for slot in range(total):
            chunk_copy(slot).wait_send()

    @pl.when((c == final) & (section == 1))
    def _():
        for slot in range(total):
            back_copy(slot).wait_send()


def whole(array):
    zeros = (0,) * array.ndim
    return pl.BlockSpec(array.shape, lambda c: zeros, pipeline_mode=pl.Buffered(1))


def run_blocks(tokens, cotangent, keep, perm, weights, chunk):
    rows, seq, width = tokens.shape
    chunks = seq // chunk
    total = rows * chunks
    hidden = weights[3].shape[1]
    ff = weights[8].shape[1]

    def index(name):
        def of_step(c):
            return (getattr(Step(c, rows, chunks), name), 0, 0)

        return of_step

    def rows_of(name):
        def of_step(c):
            at = getattr(Step(c, rows, chunks), name)
            return (at // chunks, at % chunks, 0)

        return of_step

    def keep_of(c):
        step = Step(c, rows, chunks)
        return (jnp.where(step.forward, step.mixer, step.back_mixer), 0, 0)

    def given(columns, dtype, name):
        shape = jax.ShapeDtypeStruct((total, chunk, columns), dtype)
        return shape, pl.BlockSpec((1, chunk, columns), index(name))

    outs = [
        given(2 * width + hidden, BF16, "mixer"),
        given(ff, BF16, "feed"),
        given(width, BF16, "feed"),
        given(width, BF16, "back_feed"),
        given(ff, BF16, "back_feed"),
        given(width, BF16, "back_feed"),
        given(2 * hidden, BF16, "back_mixer"),
        given(hidden, BF16, "back_mixer"),
        given(width, F32, "back_mixer"),
        (
            jax.ShapeDtypeStruct((LANES, 4 * width), F32),
            pl.BlockSpec((LANES, 4 * width), lambda c: (0, 0)),
        ),
    ]
    part = (1, chunk, width)
    once = pl.Buffered(1)
    return pl.pallas_call(
        functools.partial(blocks_kernel, rows, chunks),
        grid=(2 * rows * (chunks + 1),),
        out_shape=[o[0] for o in outs],
        in_specs=[
            pl.BlockSpec(part, lambda c: (0, 0, 0), pipeline_mode=once),
            pl.BlockSpec(part, rows_of("next_mixer")),
            pl.BlockSpec(part, lambda c: (0, chunks - 1, 0), pipeline_mode=once),
            pl.BlockSpec(part, rows_of("next_back")),
            pl.BlockSpec((1, chunk, 128), keep_of),
            whole(perm),
        ]
        + [whole(w) for w in weights],
        out_specs=[o[1] for o in outs],
        scratch_shapes=[
            pltpu.VMEM((total, chunk, hidden), F32),
            pltpu.VMEM((total, chunk, 2 * hidden), BF16),
            pltpu.VMEM((total, chunk, width), F32),
            pltpu.VMEM((total, chunk, ff), BF16),
            pltpu.VMEM((total, chunk, width), BF16),
            pltpu.VMEM((total, chunk, width), BF16),
            pltpu.VMEM((total, chunk, width), BF16),
            pltpu.VMEM((chunk, width), BF16),
            pltpu.VMEM((chunk, width), BF16),
            pltpu.VMEM((LANES, hidden), F32),
            pltpu.VMEM((LANES, hidden), F32),
            pltpu.VMEM((chunk, width), BF16),
            pltpu.VMEM((chunk, width), F32),
            pltpu.VMEM((chunk, width), BF16),
            pltpu.SemaphoreType.DMA((total,)),
            pltpu.SemaphoreType.DMA((total,)),
            pltpu.SemaphoreType.DMA((total,)),
            pltpu.SemaphoreType.DMA((total,)),
        ],
        compiler_params=pltpu.CompilerParams(
            collective_id=0, has_side_effects=True, vmem_limit_bytes=BLOCKS_VMEM
        ),
        name="blocks",
    )(tokens, tokens, cotangent, cotangent, keep, perm, *weights)


def local_grads(tokens, resets, cotangent, stacked):
    weights = tuple(w if w.ndim == 2 else w[0] for w in stacked)
    rows, seq, width = tokens.shape
    chunk = min(CHUNK, seq)
    total = rows * (seq // chunk)
    span = chunk // LANES
    keep = (1 - resets).astype(F32).reshape(total, LANES, span)
    keep = keep.transpose(0, 2, 1).reshape(total, chunk, 1)
    keep = jnp.broadcast_to(keep, (total, chunk, 128))
    at = lax.broadcasted_iota(jnp.int32, (chunk, chunk), 0)
    source = lax.broadcasted_iota(jnp.int32, (chunk, chunk), 1)
    perm = (source == (at % LANES) * span + at // LANES).astype(BF16)
    perm_t = (at == (source % LANES) * span + source // LANES).astype(BF16)
    operands, active, low, *grads, grad_in, small = run_blocks(
        tokens, cotangent, keep, perm, weights, chunk
    )
    return low, grad_in, perm_t, (operands, active, *grads, small)


class Place:
    def __init__(self):
        dp_size = lax.axis_size("dp")
        chips = dp_size // 2
        self.line = 4 if chips % 4 == 0 else chips
        dp = lax.axis_index("dp")
        self.side = lax.axis_index("rep")
        self.core = dp % 2
        self.base = (dp // 2) // self.line * self.line
        self.spot = (dp // 2) % self.line

    def along(self, step):
        return {"dp": (self.base + self.spot + step) * 2 + self.core}

    def across(self):
        return {"rep": 1 - self.side}

    def other_core(self):
        return {"dp": (self.base + self.spot) * 2 + 1 - self.core}

    def doubling(self):
        found = [self.other_core()]
        span = 1
        while span < self.line:
            found.append(self.along(span - 2 * span * ((self.spot // span) % 2)))
            span *= 2
        return found + [self.across()]


def remote(src, dst, send_sem, recv_sem, device):
    return pltpu.make_async_remote_copy(
        src_ref=src,
        dst_ref=dst,
        send_sem=send_sem,
        recv_sem=recv_sem,
        device_id=device,
        device_id_type=pl.DeviceIdType.MESH,
    )


SUM_ORDER = (
    -1, -1, 1, 0, -1, 1, -1, 3, 1, 2, 3, -1, 0, 3, 0, -1, 1, 5, 0, 3, 4, 2, 5, 1, 2, 0, -1, 3,
    2, 5, 0, 1, -1, 3, 7, 6, 4, 2, 5, 0, 4, 1, 7, 2, 4, 3, 6, 7, 2, 6, 4, 7, 6, 2, 3, 0, 4, 6,
    4, 1, 5, 6, 7, 6, 5, 2, 4, 7, 6, 4, 5, 7, 5, 0, 6, 7,
)


def sum_order(groups, lengths):
    if all(SUM_ORDER.count(c) == n for c, n in enumerate(lengths)):
        return SUM_ORDER
    order = []
    left = list(lengths)
    for g in range(groups):
        for _ in range(2):
            order.append(-1)
            for c in range(2 * g):
                if left[c]:
                    order.append(c)
                    left[c] -= 1
    while any(left):
        for c, n in enumerate(left):
            if n:
                order.append(c)
                left[c] -= 1
    return order


def sum_kernel(
    line,
    rounds,
    operands,
    feed,
    down,
    up,
    mix,
    gate,
    cand,
    small,
    out,
    small_out,
    wide,
    narrow,
    turned,
    own,
    leave,
    core_in,
    across_out,
    across_in,
    short_out,
    short_in,
    partial,
    result,
    small_buf,
    sums,
    wide_sem,
    narrow_sem,
    core_sem,
    across_sem,
    back_sem,
    short_sem,
    line_send,
    rs_recv,
    ag_recv,
    keep_sem,
    pair_sem,
    small_sem,
):
    place = Place()
    width = down.shape[1]
    groups = out.shape[0]
    half_rows = out.shape[2]
    last = line - 1
    side_rows = across_out.shape[1]
    shard_rows = (side_rows // line, short_out.shape[1])
    short_at = 2 * side_rows
    core = place.core
    away = 1 - core
    pair = place.other_core()
    opposite = place.across()
    neighbours = (place.along(1), place.along(-1))
    spots = (place.spot, last - place.spot)
    doubling = place.doubling()

    barrier = pltpu.get_barrier_semaphore()

    def greet(peer):
        pl.semaphore_signal(
            barrier, inc=1, device_id=peer, device_id_type=pl.DeviceIdType.MESH
        )

    for peer in doubling:
        greet(peer)
    for direction in range(2):
        pl.when(spots[direction] < last)(functools.partial(greet, neighbours[direction]))
    greeted = len(doubling) + jnp.where(spots[0] < last, 1, 0) + jnp.where(spots[1] < last, 1, 0)

    hidden = cand.shape[1]
    ff = up.shape[1]
    normed_two = operands.at[:, pl.ds(width + hidden, width)]
    normed = operands.at[:, pl.ds(0, width)]
    sources = [(feed, down), (up, normed_two), (gate, normed), (None, mix)]
    sum_at = [None, 0, ff, ff + 2 * hidden]

    def wide_copy(g, half, t):
        slot = g % 2
        to = wide.at[slot, t, half]
        if g < 3:
            cols = pl.ds(pl.multiple_of((half * 2 + t) * width, width), width)
            src = sources[g][0].at[:, cols]
        elif t == 0:
            cols = pl.ds(pl.multiple_of(half * width, width), width)
            src = cand.at[:, cols]
        else:
            cols = pl.ds(pl.multiple_of(width + half * width, width), width)
            src = operands.at[:, cols]
        return pltpu.make_async_copy(src, to, wide_sem.at[slot, t, half])

    def narrow_copy(g):
        return pltpu.make_async_copy(
            sources[g][1], narrow.at[g % 2], narrow_sem.at[g % 2]
        )

    def load(g):
        narrow_copy(g).start()
        for half in (away, core):
            for t in range(2):
                wide_copy(g, half, t).start()

    def side_at(side):
        return pl.ds(pl.multiple_of(side * side_rows, side_rows), side_rows)

    def shard_at(kind, shard):
        n = shard_rows[kind]
        start = place.side * side_rows if kind == 0 else short_at
        return pl.ds(pl.multiple_of(start + shard * n, 16), n)

    def core_copy(g, kind):
        rows = pl.ds(0, short_at) if kind == 0 else pl.ds(short_at, half_rows - short_at)
        return remote(
            leave.at[g, rows],
            core_in.at[g, rows],
            core_sem.at[0, g, kind],
            core_sem.at[1, g, kind],
            pair,
        )

    def rs_copy(g, kind, direction, source, s):
        rows = pl.ds(0, shard_rows[kind])
        return remote(
            partial.at[g, kind, direction, source, rows],
            partial.at[g, kind, direction, s, rows],
            line_send.at[g, kind, direction],
            rs_recv.at[g, kind, direction, s],
            neighbours[direction],
        )

    def ag_copy(g, kind, direction, shard, s):
        rows = shard_at(kind, shard)
        return remote(
            result.at[g, rows],
            result.at[g, rows],
            line_send.at[g, kind, direction],
            ag_recv.at[g, kind, direction, s],
            neighbours[direction],
        )

    def across_copy(g):
        return remote(
            across_out.at[g], across_in.at[g], across_sem.at[0, g], across_sem.at[1, g], opposite
        )

    def short_copy(g):
        return remote(
            short_out.at[g], short_in.at[g], short_sem.at[0, g], short_sem.at[1, g], opposite
        )

    def back_copy(g, rows):
        return remote(
            result.at[g, rows], result.at[g, rows], back_sem.at[0, g], back_sem.at[1, g], opposite
        )

    def keep_copy(g, rows):
        return pltpu.make_async_copy(result.at[g, rows], out.at[g, core, rows], keep_sem.at[g])

    def pair_copy(g, rows, to):
        return remote(
            result.at[g, rows], out.at[g, to, rows], pair_sem.at[0, g], pair_sem.at[1, g], pair
        )

    def hand_out(g, rows):
        keep_copy(g, rows).start()
        pair_copy(g, rows, core).start()

    def shard_of(direction, steps):
        return steps if direction == 0 else last - steps

    def rs_stage(g, kind, s):
        rows = pl.ds(0, shard_rows[kind])
        for direction in range(2):
            spot = spots[direction]
            mine = shard_at(kind, shard_of(direction, spot + last - s))

            def begin(direction=direction):
                first = shard_at(kind, shard_of(direction, last - s))
                partial[g, kind, direction, s, rows] = own[g, first].astype(BF16)
                rs_copy(g, kind, direction, s, s).start()

            def go_on(direction=direction, mine=mine):
                rs_copy(g, kind, direction, s - 1, s - 1).wait_recv()
                total = own[g, mine] + partial[g, kind, direction, s - 1, rows].astype(F32)
                partial[g, kind, direction, s - 1, rows] = total.astype(BF16)
                rs_copy(g, kind, direction, s - 1, s).start()

            pl.when(spot == 0)(begin)
            if s > 0:
                pl.when((spot > 0) & (spot <= s))(go_on)

    def combine(g, kind):
        rows = pl.ds(0, shard_rows[kind])
        mine = shard_at(kind, place.spot)
        for direction in range(2):

            def add(direction=direction):
                rs_copy(g, kind, direction, last - 1, last - 1).wait_recv()
                own[g, mine] += partial[g, kind, direction, last - 1, rows].astype(F32)

            pl.when(spots[direction] > 0)(add)

    def finished(g, kind, shard):
        rows = shard_at(kind, shard)
        hand_out(g, rows)
        if kind == 0:
            back_copy(g, rows).start()

    def ag_stage(g, kind, s):
        for direction in range(2):
            spot = spots[direction]
            shard = shard_of(direction, spot - s)

            def send(direction=direction, shard=shard):
                ag_copy(g, kind, direction, shard, s).start()

            def receive(direction=direction, shard=shard, send=send, spot=spot):
                ag_copy(g, kind, direction, shard, s - 1).wait_recv()
                if s < last:
                    pl.when(spot < last)(send)
                finished(g, kind, shard)

            if s == 0:
                pl.when(spot < last)(send)
            else:
                pl.when(spot >= s)(receive)
        if s == 0:
            finished(g, kind, place.spot)

    def across_first(g):
        core_copy(g, 0).wait_recv()
        theirs = side_at(1 - place.side)
        ours = side_at(place.side)
        across_out[g] = (own[g, theirs] + core_in[g, theirs].astype(F32)).astype(BF16)
        across_copy(g).start()
        own[g, ours] += core_in[g, ours].astype(F32)

    def across_done(g):
        across_copy(g).wait_recv()
        ours = side_at(place.side)
        own[g, ours] += across_in[g].astype(F32)
        rs_stage(g, 0, 0)

    def line_first(g):
        core_copy(g, 1).wait_recv()
        rows = pl.ds(short_at, half_rows - short_at)
        own[g, rows] += core_in[g, rows].astype(F32)
        rs_stage(g, 1, 0)

    def combine_across(g):
        combine(g, 0)
        mine = shard_at(0, place.spot)
        result[g, mine] = own[g, mine].astype(BF16)
        ag_stage(g, 0, 0)

    def combine_line(g):
        combine(g, 1)
        short_out[g] = own[g, shard_at(1, place.spot)].astype(BF16)
        short_copy(g).start()

    def short_done(g):
        short_copy(g).wait_recv()
        total = short_out[g].astype(F32) + short_in[g].astype(F32)
        result[g, shard_at(1, place.spot)] = total.astype(BF16)
        ag_stage(g, 1, 0)

    def back_done(g):
        rows = side_at(1 - place.side)
        back_copy(g, rows).wait_recv()
        hand_out(g, rows)

    chains = []
    for g in range(groups):
        middle_steps = [functools.partial(rs_stage, g, 0, s) for s in range(1, last)]
        later_steps = [functools.partial(ag_stage, g, 0, s) for s in range(1, line)]
        chains.append(
            [functools.partial(across_first, g), functools.partial(across_done, g)]
            + middle_steps
            + [functools.partial(combine_across, g)]
            + later_steps
            + [functools.partial(back_done, g)]
        )
        middle_steps = [functools.partial(rs_stage, g, 1, s) for s in range(1, last)]
        later_steps = [functools.partial(ag_stage, g, 1, s) for s in range(1, line)]
        chains.append(
            [functools.partial(line_first, g)]
            + middle_steps
            + [functools.partial(combine_line, g), functools.partial(short_done, g)]
            + later_steps
        )

    def advance(chain):
        if chain:
            chain.pop(0)()

    def small_copy(k):
        return remote(
            small_buf.at[0, k],
            small_buf.at[1, k],
            small_sem.at[0, k],
            small_sem.at[1, k],
            doubling[k],
        )

    def small_round(k):
        if k == 0:
            here = small.shape[1]
            small_buf[0, 0, 0:1, 0:here] = jnp.sum(small[...], axis=0, keepdims=True)
            small_buf[0, 0, 0:1, here:] = sums[0:1, :]
            small_copy(0).start()
            return
        small_copy(k - 1).wait()
        total = small_buf[0, k - 1] + small_buf[1, k - 1]
        if k < rounds:
            small_buf[0, k] = total
            small_copy(k).start()
        else:
            small_out[...] = total

    ones = turned.shape[1] - width
    for slot in range(2):
        turned[slot, width:] = jnp.ones((ones, turned.shape[2]), BF16)
    def tiles():
        load(0)
        for g in range(groups):
            if g + 1 < groups:
                load(g + 1)
            narrow_copy(g).wait()
            turned[g % 2, :width] = narrow[g % 2].T
            for half in (away, core):
                for t in range(2):
                    wide_copy(g, half, t).wait()
                    left = turned[(g if g < 3 or t == 1 else 2) % 2]
                    tile = dot(left, wide[g % 2, t, half])
                    if g in (1, 2) or (g == 3 and t == 0):
                        spot = half * width if g == 3 else (half * 2 + t) * width
                        spot = pl.multiple_of(sum_at[g] + spot, width)
                        sums[:, pl.ds(spot, width)] = tile[width : width + LANES]
                    tile = tile[:width]
                    if g == 0 or (g == 3 and t == 1):
                        tile = tile.T
                    rows = pl.ds(t * width, width)
                    if half is away:
                        leave[g, rows, :] = tile.astype(BF16)
                    else:
                        own[g, rows, :] = tile
                if half is away:
                    if g == 0:
                        pl.semaphore_wait(barrier, greeted)
                    for kind in range(2):
                        core_copy(g, kind).start()
                yield

    work = tiles()
    halves = 2 * groups
    small_at = 0
    for at, item in enumerate(sum_order(groups, [len(chain) for chain in chains])):
        if item < 0:
            next(work, None)
            halves -= 1
        else:
            advance(chains[item])
        if halves == 0 and at % 4 == 0 and small_at <= rounds:
            small_round(small_at)
            small_at += 1
    while small_at <= rounds:
        small_round(small_at)
        small_at += 1

    for g in range(groups):
        for kind in range(2):
            core_copy(g, kind).wait_send()
            for direction in range(2):

                def sent(kind=kind, direction=direction):
                    rows = side_at(0) if kind == 0 else pl.ds(short_at, half_rows - short_at)
                    remote(
                        result.at[g, rows],
                        result.at[g, rows],
                        line_send.at[g, kind, direction],
                        ag_recv.at[g, kind, direction, 0],
                        pair,
                    ).wait_send()

                pl.when(spots[direction] < last)(sent)
        across_copy(g).wait_send()
        short_copy(g).wait_send()
        back_copy(g, side_at(place.side)).wait_send()
        rows = pl.ds(0, half_rows)
        keep_copy(g, rows).wait()
        pair_copy(g, rows, away).wait_send()
        pair_copy(g, rows, away).wait_recv()


def unpack_kernel(
    perm_t,
    low_i,
    grad_i,
    down_i,
    up_i,
    gate_i,
    cand_i,
    out_i,
    block_out,
    grad_in,
    w_gate,
    w_cand,
    w_out,
    w_up,
    w_down,
):
    for source, target in (
        (down_i, w_down),
        (up_i, w_up),
        (gate_i, w_gate),
        (cand_i, w_cand),
        (out_i, w_out),
    ):
        target[0] = source[0].astype(F32)
    block_out[...] = dot(perm_t[...], low_i[0]).astype(BF16).reshape(block_out.shape)
    grad = grad_i[0]
    high = grad.astype(BF16)
    rest = jnp.where(lax.axis_index("section") == 0, grad - high.astype(F32), 0.0)
    grad_in[...] = (dot(perm_t[...], high) + dot(perm_t[...], rest.astype(BF16))).reshape(
        grad_in.shape
    )


def unpack(packed, low, grad, perm_t, rows, width, hidden, ff):
    packed = packed.reshape(4, ff, width)
    parts, chunk = low.shape[0], low.shape[1]
    chunks = parts // rows
    seq = chunks * chunk
    tall = ff // parts
    short = tall // 2
    spread = width // tall
    per_tile = width // short

    def column_block(t):
        return (0, t % spread, t // spread)

    return pl.pallas_call(
        unpack_kernel,
        grid=(parts,),
        out_shape=[
            jax.ShapeDtypeStruct((1, rows, seq, width), BF16),
            jax.ShapeDtypeStruct((1, rows, seq, width), F32),
            jax.ShapeDtypeStruct((1, width, 2 * hidden), F32),
            jax.ShapeDtypeStruct((1, width, hidden), F32),
            jax.ShapeDtypeStruct((1, hidden, width), F32),
            jax.ShapeDtypeStruct((1, width, ff), F32),
            jax.ShapeDtypeStruct((1, ff, width), F32),
        ],
        in_specs=[
            whole(perm_t),
            pl.BlockSpec((1, chunk, width), lambda t: (t, 0, 0)),
            pl.BlockSpec((1, chunk, width), lambda t: (t, 0, 0)),
            pl.BlockSpec((1, tall, width), lambda t: (0, t, 0)),
            pl.BlockSpec((1, tall, width), lambda t: (1, t, 0)),
            pl.BlockSpec((1, tall, width), lambda t: (2, t, 0)),
            pl.BlockSpec(
                (1, short, width),
                lambda t: (3, t // per_tile * 2 * per_tile + t % per_tile, 0),
            ),
            pl.BlockSpec(
                (1, short, width),
                lambda t: (3, t // per_tile * 2 * per_tile + per_tile + t % per_tile, 0),
            ),
        ],
        out_specs=[
            pl.BlockSpec((1, 1, chunk, width), lambda t: (0, t // chunks, t % chunks, 0)),
            pl.BlockSpec((1, 1, chunk, width), lambda t: (0, t // chunks, t % chunks, 0)),
            pl.BlockSpec((1, tall, width), column_block),
            pl.BlockSpec((1, short, width), lambda t: (0, t % per_tile, t // per_tile)),
            pl.BlockSpec((1, short, width), lambda t: (0, t, 0)),
            pl.BlockSpec((1, tall, width), column_block),
            pl.BlockSpec((1, tall, width), lambda t: (0, t, 0)),
        ],
        compiler_params=pltpu.CompilerParams(vmem_limit_bytes=VMEM_LIMIT),
        name="unpack",
    )(perm_t, low, grad, packed, packed, packed, packed, packed)


def sum_gradients(operands, small, hidden, ff):
    place = Place()
    line = place.line
    rounds = len(place.doubling())
    operands = [a.reshape(-1, a.shape[-1]) for a in operands]
    tokens, width = operands[2].shape
    total = small.shape[1] + ff + 3 * hidden
    groups = 4
    half_rows = ff // 2
    side_rows = half_rows * 3 // 8
    shard = side_rows // line
    short = (half_rows - 2 * side_rows) // line
    anywhere = pl.BlockSpec(memory_space=pl.ANY)
    here = pl.BlockSpec(memory_space=pltpu.VMEM)
    packed, small_sum = pl.pallas_call(
        functools.partial(sum_kernel, line, rounds),
        out_shape=[
            jax.ShapeDtypeStruct((groups, 2, half_rows, width), BF16),
            jax.ShapeDtypeStruct((1, total), F32),
        ],
        in_specs=[anywhere] * 7 + [here],
        out_specs=[anywhere, here],
        scratch_shapes=[
            pltpu.VMEM((2, 2, 2, tokens, width), BF16),
            pltpu.VMEM((2, tokens, width), BF16),
            pltpu.VMEM((2, width + 2 * LANES, tokens), BF16),
            pltpu.VMEM((groups, half_rows, width), F32),
            pltpu.VMEM((groups, half_rows, width), BF16),
            pltpu.VMEM((groups, half_rows, width), BF16),
            pltpu.VMEM((groups, side_rows, width), BF16),
            pltpu.VMEM((groups, side_rows, width), BF16),
            pltpu.VMEM((groups, short, width), BF16),
            pltpu.VMEM((groups, short, width), BF16),
            pltpu.VMEM((groups, 2, 2, line - 1, max(shard, short), width), BF16),
            pltpu.VMEM((groups, half_rows, width), BF16),
            pltpu.VMEM((2, rounds, 1, total), F32),
            pltpu.VMEM((LANES, ff + 3 * hidden), F32),
            pltpu.SemaphoreType.DMA((2, 2, 2)),
            pltpu.SemaphoreType.DMA((2,)),
            pltpu.SemaphoreType.DMA((2, groups, 2)),
            pltpu.SemaphoreType.DMA((2, groups)),
            pltpu.SemaphoreType.DMA((2, groups)),
            pltpu.SemaphoreType.DMA((2, groups)),
            pltpu.SemaphoreType.DMA((groups, 2, 2)),
            pltpu.SemaphoreType.DMA((groups, 2, 2, line - 1)),
            pltpu.SemaphoreType.DMA((groups, 2, 2, line - 1)),
            pltpu.SemaphoreType.DMA((groups,)),
            pltpu.SemaphoreType.DMA((2, groups)),
            pltpu.SemaphoreType.DMA((2, rounds)),
        ],
        compiler_params=pltpu.CompilerParams(
            collective_id=2, has_side_effects=True, vmem_limit_bytes=VMEM_LIMIT
        ),
        name="sum_gradients",
    )(*operands, small)
    dp_size = lax.axis_size("dp")
    inner = 2 * line
    if dp_size > inner:
        members = [list(range(i, dp_size, inner)) for i in range(inner)]
        packed, small_sum = lax.psum((packed, small_sum), "dp", axis_index_groups=members)
    return packed, small_sum


def split_small(small, width, hidden, ff):
    sizes = (width, width, width, width, ff, 2 * hidden, hidden)
    out = []
    at = 0
    for n in sizes:
        out.append(small[:, at : at + n])
        at += n
    return out


def body(tokens, resets, cotangent, *stacked):
    rows, _, width = tokens.shape
    hidden = stacked[3].shape[2]
    ff = stacked[8].shape[2]
    low, grad_in, perm_t, (*operands, small) = local_grads(tokens, resets, cotangent, stacked)
    packed, small_sum = sum_gradients(operands, small, hidden, ff)
    block_out, grad_in, w_gate, w_cand, w_out, w_up, w_down = unpack(
        packed, low, grad_in, perm_t, rows, width, hidden, ff
    )
    g_one, b_out, g_two, b_down, b_up, b_gate, b_cand = split_small(small_sum, width, hidden, ff)
    grads = (g_one, w_gate, b_gate, w_cand, b_cand, w_out, b_out, g_two, w_up, b_up, w_down, b_down)
    return (block_out, grad_in) + grads


def solution(mesh):
    vector = P("section", None)
    matrix = P("section", None, None)
    weight_specs = (
        vector,
        matrix,
        vector,
        matrix,
        vector,
        matrix,
        vector,
        vector,
        matrix,
        vector,
        matrix,
        vector,
    )
    tokens = P(("dp", "rep"), None, None)
    by_rows = P("section", ("dp", "rep"), None, None)
    return jax.shard_map(
        body,
        mesh=mesh,
        in_specs=(tokens, P(("dp", "rep"), None), tokens) + weight_specs,
        out_specs=(by_rows, by_rows) + weight_specs,
        check_vma=False,
    )
```

```python
import functools
import math

import jax
import jax.numpy as jnp
import numpy as np
from jax import lax
from jax.experimental import pallas as pl
from jax.experimental.pallas import tpu as pltpu
from jax.sharding import PartitionSpec as P

EPS = 1e-06
F32 = jnp.float32
BF16 = jnp.bfloat16
CHUNK = 256
LANES = 8
WIDTH = 256
GELU_A = math.sqrt(2.0 / math.pi)
GELU_B = 0.044715
LN4 = math.log(4.0)
EXP_TOP = 85.6
VMEM_LIMIT = 60 * 1024 * 1024
BLOCKS_VMEM = 63 * 1024 * 1024


def dot(a, b):
    return jnp.dot(a, b, preferred_element_type=F32)


def dot_nt(a, b):
    return lax.dot_general(a, b, (((1,), (1,)), ((), ())), preferred_element_type=F32)


def inv_scale(values):
    return lax.rsqrt(jnp.mean(values * values, axis=-1, keepdims=True) + EPS)


def partner_barrier_signal(partner):
    pl.semaphore_signal(
        pltpu.get_barrier_semaphore(),
        inc=1,
        device_id={"section": partner},
        device_id_type=pl.DeviceIdType.MESH,
    )


def interleave(*streams):
    live = list(streams)
    while live:
        for stream in list(live):
            if next(stream, live) is live:
                live.remove(stream)


def scan_segments(product, accum, carry, reverse):
    which = lax.broadcasted_iota(jnp.int32, product.shape, 0)
    span = 1
    while span < LANES:
        turn = LANES - span if reverse else span
        inside = which < LANES - span if reverse else which >= span
        accum = jnp.where(inside, product * pltpu.roll(accum, turn, 0) + accum, accum)
        product = jnp.where(inside, product * pltpu.roll(product, turn, 0), product)
        span *= 2
    reached = product * carry + accum
    edge = LANES - 1 if reverse else 0
    incoming = jnp.where(which == edge, carry, pltpu.roll(reached, LANES - 1 if reverse else 1, 0))
    end = 0 if reverse else LANES - 1
    return incoming, jnp.broadcast_to(reached[end : end + 1], reached.shape)


class Step:
    def __init__(self, step, rows, chunks):
        first = lax.axis_index("section") == 0
        phase = step // (chunks + 1)
        self.at = step % (chunks + 1)
        self.forward = jnp.where(first, phase < rows, phase % 2 == 0)
        self.row = jnp.where(first, phase % rows, phase // 2)
        base = self.row * chunks
        last = chunks - 1
        self.mixer = base + jnp.minimum(self.at, last)
        self.feed = base + jnp.maximum(self.at - 1, 0)
        self.back_feed = base + jnp.maximum(last - self.at, 0)
        self.back_mixer = base + jnp.minimum(chunks - self.at, last)
        total = rows * chunks
        self.next_mixer = jnp.minimum(self.mixer + 1, total - 1)
        later = jnp.minimum(base + self.at + 1, total - 1)
        self.next_back = later // chunks * chunks + last - later % chunks


def blocks_kernel(
    rows,
    chunks,
    tok,
    cot,
    w_gate_all,
    w_cand_all,
    w_out_all,
    w_up_all,
    w_down_all,
    keep_rows,
    perm,
    g_one,
    b_gate,
    b_cand,
    b_out,
    g_two,
    b_up,
    b_down,
    operands_all,
    active_all,
    low_all,
    down_all,
    up_all,
    mix_all,
    gate_all,
    cand_all,
    grad_all,
    small_o,
    raw,
    keep,
    w_gate,
    w_cand,
    w_out,
    w_up,
    w_down,
    operands_o,
    active_o,
    low_o,
    down_o,
    up_o,
    mix_o,
    gate_o,
    cand_o,
    grad_o,
    ratio_s,
    slopes_s,
    middle_s,
    slope_up_s,
    inputs,
    send,
    received,
    coming,
    coming_back,
    carry,
    carry_back,
    normed_two_s,
    grad_middle_s,
    mix_s,
    load_sem,
    stage_sem,
    send_sem,
    input_sem,
    back_send_sem,
    received_sem,
):
    section = lax.axis_index("section")
    partner = 1 - section
    chunk, width = coming.shape
    hidden = w_cand.shape[1]
    ff = w_up.shape[1]
    span = chunk // LANES
    total = rows * chunks
    steps = 2 * rows * (chunks + 1)
    stages = (
        (operands_o, operands_all),
        (active_o, active_all),
        (low_o, low_all),
        (down_o, down_all),
        (up_o, up_all),
        (mix_o, mix_all),
        (gate_o, gate_all),
        (cand_o, cand_all),
        (grad_o, grad_all),
    )

    def stage_copy(which, at_chunk):
        source, target = stages[which]
        slot = at_chunk % 2
        return pltpu.make_async_copy(
            source.at[slot], target.at[at_chunk], stage_sem.at[which, slot]
        )

    def load_copy(which):
        pairs = (
            (w_gate_all, w_gate),
            (w_cand_all, w_cand),
            (w_out_all, w_out),
            (w_up_all, w_up),
            (w_down_all, w_down),
        )
        return pltpu.make_async_copy(*pairs[which], load_sem.at[which])

    def raw_copy(source):
        return pltpu.make_async_copy(source, raw, load_sem.at[5])

    def raw_chunk(at_chunk):
        start = pl.multiple_of(at_chunk % chunks * chunk, chunk)
        return raw[at_chunk // chunks, pl.ds(start, chunk)]

    def chunk_copy(slot):
        return remote(
            send.at[slot],
            inputs.at[slot],
            send_sem.at[slot],
            input_sem.at[slot],
            {"section": partner},
        )

    def back_copy(slot):
        return remote(
            send.at[slot],
            received.at[slot],
            back_send_sem.at[slot],
            received_sem.at[slot],
            {"section": partner},
        )

    def add_small(which, values):
        part = jnp.sum(values.reshape(-1, LANES, width), axis=0)
        small_o[:, which * width : (which + 1) * width] += part

    def blocks_step(c):
        step = Step(c, rows, chunks)

        @pl.when(c == 1)
        def _():
            load_copy(3).wait()
            load_copy(4).wait()

        @pl.when(step.forward & (step.at == 0))
        def _():
            carry[...] = jnp.zeros_like(carry)

        @pl.when(jnp.logical_not(step.forward) & (step.at == 0))
        def _():
            carry_back[...] = jnp.zeros_like(carry_back)

        @pl.when(step.forward & (step.at < chunks) & (section == 0))
        def _():
            inputs[step.mixer] = coming[...]

        @pl.when(step.forward & (step.at < chunks) & (section == 1))
        def _():
            chunk_copy(step.mixer).wait_recv()

        @pl.when(jnp.logical_not(step.forward) & (step.at < chunks) & (section == 0))
        def _():
            back_copy(step.back_feed).wait_recv()
            coming_back[...] = received[step.back_feed]

        @pl.when(step.forward & (step.at < chunks) & (step.mixer >= 2))
        def _():
            stage_copy(0, step.mixer).wait()

        @pl.when(step.forward & (step.at > 0) & (step.feed >= 2))
        def _():
            for which in (1, 2):
                stage_copy(which, step.feed).wait()

        @pl.when(jnp.logical_not(step.forward) & (step.at < chunks) & (step.row * chunks + step.at >= 2))
        def _():
            for which in (3, 4, 5):
                stage_copy(which, step.back_feed).wait()

        @pl.when(jnp.logical_not(step.forward) & (step.at > 0) & (step.row * chunks + step.at >= 3))
        def _():
            for which in (6, 7, 8):
                stage_copy(which, step.back_mixer).wait()

        def mixer():
            at_chunk = step.mixer
            slot = at_chunk % 2
            x = inputs[at_chunk].astype(F32)
            normed = (x * inv_scale(x) * g_one[...]).astype(BF16)
            operands_o[slot, :, :width] = normed
            yield
            for at in range(0, hidden, WIDTH):
                cols = slice(at, at + WIDTH)
                cols_in = slice(hidden + at, hidden + at + WIDTH)
                pre_f = dot(normed, w_gate[:, cols])
                pre_i = dot(normed, w_gate[:, cols_in])
                cand = dot(normed, w_cand[:, cols]) + b_cand[:, cols]
                u = jnp.exp(jnp.minimum((-LN4 - b_gate[:, cols]) - pre_f, EXP_TOP))
                v = jnp.exp(jnp.minimum((-LN4 - b_gate[:, cols_in]) - pre_i, EXP_TOP))
                d = 1.0 / (0.5 + u + v)
                ratio_f = (0.25 + v) * d
                ratio_i = (0.25 + u) * d
                ratio_s[at_chunk, :, cols] = ratio_f
                keep_w = jnp.concatenate([keep[at_chunk]] * (WIDTH // 128), axis=1)
                decay = ratio_f * keep_w
                drive = ratio_i * cand
                product = decay[0:LANES]
                accum = drive[0:LANES]
                for j in range(1, span):
                    r = slice(j * LANES, (j + 1) * LANES)
                    accum = decay[r] * accum + drive[r]
                    product = decay[r] * product
                state, carry[:, cols] = scan_segments(product, accum, carry[:, cols], False)
                before = []
                after = []
                for j in range(span):
                    r = slice(j * LANES, (j + 1) * LANES)
                    before.append(state)
                    state = decay[r] * state + drive[r]
                    after.append(state)
                operands_o[slot, :, width + at : width + at + WIDTH] = jnp.concatenate(
                    after, axis=0
                ).astype(BF16)
                lever = keep_w * jnp.concatenate(before, axis=0) - cand
                slopes_s[at_chunk, :, cols] = (lever * ((u * d) * ratio_f)).astype(BF16)
                slopes_s[at_chunk, :, cols_in] = (-lever * ((v * d) * ratio_i)).astype(BF16)
                yield
            mixed = dot(operands_o[slot, :, width : width + hidden], w_out[...])
            yield
            middle = x + (mixed + b_out[...])
            normed_two = (middle * inv_scale(middle) * g_two[...]).astype(BF16)
            operands_o[slot, :, width + hidden :] = normed_two
            yield
            middle_s[at_chunk] = middle
            normed_two_s[...] = normed_two

        def feed():
            at_chunk = step.feed
            slot = at_chunk % 2
            for at in range(0, ff, WIDTH):
                cols = slice(at, at + WIDTH)
                up = dot(normed_two_s[...], w_up[:, cols]) + b_up[:, cols]
                square = up * up
                half = 0.5 + 0.5 * jnp.tanh(up * (GELU_A + (GELU_A * GELU_B) * square))
                act = up * half
                active_o[slot, :, cols] = act.astype(BF16)
                slope = half + act * (1.0 - half) * (2 * GELU_A + (6 * GELU_A * GELU_B) * square)
                slope_up_s[at_chunk, :, cols] = slope.astype(BF16)
                if at % (2 * WIDTH):
                    yield
            down = dot(active_o[slot], w_down[...])
            yield
            low_o[slot] = (middle_s[at_chunk] + (down + b_down[...])).astype(BF16)

        def reorder():
            yield
            yield
            coming[...] = dot(perm[...], raw_chunk(step.next_mixer)).astype(BF16)

        def back_feed():
            at_chunk = step.back_feed
            slot = at_chunk % 2
            grad_down = coming_back[...]
            down_o[slot] = grad_down
            yield
            for at in range(0, ff, WIDTH):
                cols = slice(at, at + WIDTH)
                grad_active = dot_nt(grad_down, w_down[cols, :])
                slope = slope_up_s[at_chunk, :, cols].astype(F32)
                up_o[slot, :, cols] = (grad_active * slope).astype(BF16)
                if at % (2 * WIDTH):
                    yield
            q = dot_nt(up_o[slot], w_up[...])
            yield
            dy = grad_down.astype(F32)
            add_small(3, dy)
            middle = middle_s[at_chunk]
            r = inv_scale(middle)
            scaled = middle * r
            add_small(2, q * scaled)
            weighted = q * g_two[...]
            grad_middle = dy + r * (
                weighted - scaled * jnp.mean(weighted * scaled, axis=-1, keepdims=True)
            )
            add_small(1, grad_middle)
            grad_mix = grad_middle.astype(BF16)
            mix_o[slot] = grad_mix
            yield
            yield
            grad_middle_s[...] = grad_middle
            mix_s[...] = grad_mix

        def back_mixer():
            at_chunk = step.back_mixer
            slot = at_chunk % 2
            for at in range(0, hidden, WIDTH):
                cols = slice(at, at + WIDTH)
                cols_in = slice(hidden + at, hidden + at + WIDTH)
                grad_state = dot_nt(mix_s[...], w_out[cols, :])
                ratio_f = ratio_s[at_chunk, :, cols]
                decay = ratio_f * jnp.concatenate([keep[at_chunk]] * (WIDTH // 128), axis=1)
                last = slice((span - 1) * LANES, span * LANES)
                product = decay[last]
                accum = decay[last] * grad_state[last]
                for j in range(span - 2, -1, -1):
                    rj = slice(j * LANES, (j + 1) * LANES)
                    accum = decay[rj] * (grad_state[rj] + accum)
                    product = decay[rj] * product
                later, carry_back[:, cols] = scan_segments(product, accum, carry_back[:, cols], True)
                parts = [None] * span
                for j in range(span - 1, -1, -1):
                    rj = slice(j * LANES, (j + 1) * LANES)
                    carried = grad_state[rj] + later
                    parts[j] = carried
                    later = decay[rj] * carried
                carried = jnp.concatenate(parts, axis=0)
                gate_o[slot, :, cols] = (carried * slopes_s[at_chunk, :, cols].astype(F32)).astype(BF16)
                gate_o[slot, :, cols_in] = (
                    carried * slopes_s[at_chunk, :, cols_in].astype(F32)
                ).astype(BF16)
                cand_o[slot, :, cols] = (carried * (1.0 - ratio_f)).astype(BF16)
                yield
            p = dot_nt(gate_o[slot], w_gate[...]) + dot_nt(cand_o[slot], w_cand[...])
            yield
            x = inputs[at_chunk].astype(F32)
            r = inv_scale(x)
            scaled = x * r
            add_small(0, p * scaled)
            weighted = p * g_one[...]
            grad_input = grad_middle_s[...] + r * (
                weighted - scaled * jnp.mean(weighted * scaled, axis=-1, keepdims=True)
            )
            grad_o[slot] = grad_input.astype(BF16)

        def back_reorder():
            yield
            yield
            coming_back[...] = dot(perm[...], raw_chunk(step.next_back)).astype(BF16)

        opening = step.at == 0
        closing = step.at == chunks
        between = jnp.logical_not(opening | closing)
        backward = jnp.logical_not(step.forward)

        @pl.when(step.forward & opening)
        def _():
            interleave(mixer(), reorder())

        @pl.when(step.forward & between)
        def _():
            interleave(mixer(), feed(), reorder())

        @pl.when(step.forward & closing)
        def _():
            interleave(feed())

        @pl.when(backward & opening)
        def _():
            interleave(back_feed(), back_reorder())

        @pl.when(backward & between)
        def _():
            interleave(back_feed(), back_mixer(), back_reorder())

        @pl.when(backward & closing)
        def _():
            interleave(back_mixer())

        @pl.when(step.forward & jnp.logical_not(closing))
        def _():
            stage_copy(0, step.mixer).start()

        @pl.when(step.forward & jnp.logical_not(opening))
        def _():
            for which in (1, 2):
                stage_copy(which, step.feed).start()

        @pl.when(backward & jnp.logical_not(closing))
        def _():
            for which in (3, 4, 5):
                stage_copy(which, step.back_feed).start()

        @pl.when(backward & jnp.logical_not(opening))
        def _():
            for which in (6, 7, 8):
                stage_copy(which, step.back_mixer).start()

        @pl.when(step.forward & jnp.logical_not(opening) & (section == 0))
        def _():
            send[step.feed] = low_o[step.feed % 2]
            chunk_copy(step.feed).start()

        @pl.when(backward & jnp.logical_not(opening) & (section == 1))
        def _():
            send[step.back_mixer] = grad_o[step.back_mixer % 2]
            back_copy(step.back_mixer).start()

    partner_barrier_signal(partner)
    pl.when(section == 0)(lambda: raw_copy(tok).start())
    pl.when(section == 1)(lambda: raw_copy(cot).start())
    for which in range(5):
        load_copy(which).start()
    small_o[...] = jnp.zeros_like(small_o)
    raw_copy(tok).wait()
    coming[...] = dot(perm[...], raw_chunk(0)).astype(BF16)
    coming_back[...] = dot(perm[...], raw_chunk(chunks - 1)).astype(BF16)
    pl.semaphore_wait(pltpu.get_barrier_semaphore(), 1)
    for at_chunk in range(total):
        row = keep_rows[at_chunk : at_chunk + 1, :]
        keep[at_chunk] = jnp.broadcast_to(row, (128, chunk)).T
    for which in range(3):
        load_copy(which).wait()

    @pl.loop(0, steps)
    def _(c):
        blocks_step(c)

    @pl.when(section == 0)
    def _():
        for slot in range(total):
            chunk_copy(slot).wait_send()

    @pl.when(section == 1)
    def _():
        for slot in range(total):
            back_copy(slot).wait_send()

    for which in range(len(stages)):
        for slot in range(2):
            stage_copy(which, slot).wait()


def whole(array):
    zeros = (0,) * array.ndim
    return pl.BlockSpec(array.shape, lambda c: zeros, pipeline_mode=pl.Buffered(1))


def run_blocks(tokens, cotangent, keep, perm, weights, chunk):
    rows, seq, width = tokens.shape
    chunks = seq // chunk
    total = rows * chunks
    g_one, w_gate, b_gate, w_cand, b_cand, w_out, b_out, g_two, w_up, b_up, w_down, b_down = weights
    hidden = w_cand.shape[1]
    ff = w_up.shape[1]
    large = (w_gate, w_cand, w_out, w_up, w_down)
    little = (keep, perm, g_one, b_gate, b_cand, b_out, g_two, b_up, b_down)
    columns = (2 * width + hidden, ff, width, width, ff, width, 2 * hidden, hidden, width)
    anywhere = pl.BlockSpec(memory_space=pl.ANY)
    here = pl.BlockSpec(memory_space=pltpu.VMEM)
    return pl.pallas_call(
        functools.partial(blocks_kernel, rows, chunks),
        out_shape=[jax.ShapeDtypeStruct((total, chunk, n), BF16) for n in columns]
        + [jax.ShapeDtypeStruct((LANES, 4 * width), F32)],
        in_specs=[anywhere] * 7 + [here] * len(little),
        out_specs=[anywhere] * len(columns) + [here],
        scratch_shapes=[
            pltpu.VMEM(tokens.shape, BF16),
            pltpu.VMEM((total, chunk, 128), F32),
        ]
        + [pltpu.VMEM(w.shape, BF16) for w in large]
        + [pltpu.VMEM((2, chunk, n), BF16) for n in columns]
        + [
            pltpu.VMEM((total, chunk, hidden), F32),
            pltpu.VMEM((total, chunk, 2 * hidden), BF16),
            pltpu.VMEM((total, chunk, width), F32),
            pltpu.VMEM((total, chunk, ff), BF16),
            pltpu.VMEM((total, chunk, width), BF16),
            pltpu.VMEM((total, chunk, width), BF16),
            pltpu.VMEM((total, chunk, width), BF16),
            pltpu.VMEM((chunk, width), BF16),
            pltpu.VMEM((chunk, width), BF16),
            pltpu.VMEM((LANES, hidden), F32),
            pltpu.VMEM((LANES, hidden), F32),
            pltpu.VMEM((chunk, width), BF16),
            pltpu.VMEM((chunk, width), F32),
            pltpu.VMEM((chunk, width), BF16),
            pltpu.SemaphoreType.DMA((6,)),
            pltpu.SemaphoreType.DMA((len(columns), 2)),
            pltpu.SemaphoreType.DMA((total,)),
            pltpu.SemaphoreType.DMA((total,)),
            pltpu.SemaphoreType.DMA((total,)),
            pltpu.SemaphoreType.DMA((total,)),
        ],
        compiler_params=pltpu.CompilerParams(
            collective_id=0, has_side_effects=True, vmem_limit_bytes=BLOCKS_VMEM
        ),
        name="blocks",
    )(tokens, cotangent, *large, *little)


def local_grads(tokens, resets, cotangent, stacked):
    weights = tuple(w if w.ndim == 2 else w[0] for w in stacked)
    rows, seq, width = tokens.shape
    chunk = min(CHUNK, seq)
    total = rows * (seq // chunk)
    span = chunk // LANES
    keep = (1 - resets).astype(F32).reshape(total, LANES, span)
    keep = keep.transpose(0, 2, 1).reshape(total, chunk)
    at = np.arange(chunk)
    source = (at % LANES) * span + at // LANES
    perm_t = np.equal(at[:, None], source[None, :])
    perm = jnp.asarray(perm_t.T, BF16)
    perm_t = jnp.asarray(perm_t, BF16)
    operands, active, low, *grads, grad_in, small = run_blocks(
        tokens, cotangent, keep, perm, weights, chunk
    )
    return low, grad_in, perm_t, (operands, active, *grads, small)


class Place:
    def __init__(self):
        dp_size = lax.axis_size("dp")
        chips = dp_size // 2
        self.line = 4 if chips % 4 == 0 else chips
        dp = lax.axis_index("dp")
        self.side = lax.axis_index("rep")
        self.core = dp % 2
        self.base = (dp // 2) // self.line * self.line
        self.spot = (dp // 2) % self.line

    def along(self, step):
        return {"dp": (self.base + self.spot + step) * 2 + self.core}

    def across(self):
        return {"rep": 1 - self.side}

    def other_core(self):
        return {"dp": (self.base + self.spot) * 2 + 1 - self.core}

    def doubling(self):
        found = [self.other_core()]
        span = 1
        while span < self.line:
            found.append(self.along(span - 2 * span * ((self.spot // span) % 2)))
            span *= 2
        return found + [self.across()]


def remote(src, dst, send_sem, recv_sem, device):
    return pltpu.make_async_remote_copy(
        src_ref=src,
        dst_ref=dst,
        send_sem=send_sem,
        recv_sem=recv_sem,
        device_id=device,
        device_id_type=pl.DeviceIdType.MESH,
    )


SUM_ORDER = (
    -1, -1, 1, 0, -1, 1, -1, 3, 1, 2, 3, -1, 0, 3, 0, -1, 1, 5, 0, 3, 4, 2, 5, 1, 2, 0, -1, 3,
    2, 5, 0, 1, -1, 3, 7, 6, 4, 2, 5, 0, 4, 1, 7, 2, 4, 3, 6, 7, 2, 6, 4, 7, 6, 2, 3, 0, 4, 6,
    4, 1, 5, 6, 7, 6, 5, 2, 4, 7, 6, 4, 5, 7, 5, 0, 6, 7,
)


def sum_order(groups, lengths):
    if all(SUM_ORDER.count(c) == n for c, n in enumerate(lengths)):
        return SUM_ORDER
    order = []
    left = list(lengths)
    for g in range(groups):
        for _ in range(2):
            order.append(-1)
            for c in range(2 * g):
                if left[c]:
                    order.append(c)
                    left[c] -= 1
    while any(left):
        for c, n in enumerate(left):
            if n:
                order.append(c)
                left[c] -= 1
    return order


def sum_kernel(
    line,
    rounds,
    operands,
    feed,
    down,
    up,
    mix,
    gate,
    cand,
    small,
    out,
    small_out,
    wide,
    narrow,
    turned,
    own,
    leave,
    core_in,
    across_out,
    across_in,
    short_out,
    short_in,
    partial,
    result,
    small_buf,
    sums,
    wide_sem,
    narrow_sem,
    core_sem,
    across_sem,
    back_sem,
    short_sem,
    line_send,
    rs_recv,
    ag_recv,
    keep_sem,
    pair_sem,
    small_sem,
):
    place = Place()
    width = down.shape[1]
    groups = out.shape[0]
    half_rows = out.shape[2]
    last = line - 1
    side_rows = across_out.shape[1]
    shard_rows = (side_rows // line, short_out.shape[1])
    short_at = 2 * side_rows
    core = place.core
    away = 1 - core
    pair = place.other_core()
    opposite = place.across()
    neighbours = (place.along(1), place.along(-1))
    spots = (place.spot, last - place.spot)
    doubling = place.doubling()

    barrier = pltpu.get_barrier_semaphore()

    def greet(peer):
        pl.semaphore_signal(
            barrier, inc=1, device_id=peer, device_id_type=pl.DeviceIdType.MESH
        )

    for peer in doubling:
        greet(peer)
    for direction in range(2):
        pl.when(spots[direction] < last)(functools.partial(greet, neighbours[direction]))
    greeted = len(doubling) + jnp.where(spots[0] < last, 1, 0) + jnp.where(spots[1] < last, 1, 0)

    hidden = cand.shape[1]
    ff = up.shape[1]
    normed_two = operands.at[:, pl.ds(width + hidden, width)]
    normed = operands.at[:, pl.ds(0, width)]
    sources = [(feed, down), (up, normed_two), (gate, normed), (None, mix)]
    sum_at = [None, 0, ff, ff + 2 * hidden]

    def wide_copy(g, half, t):
        slot = g % 2
        to = wide.at[slot, t, half]
        if g < 3:
            cols = pl.ds(pl.multiple_of((half * 2 + t) * width, width), width)
            src = sources[g][0].at[:, cols]
        elif t == 0:
            cols = pl.ds(pl.multiple_of(half * width, width), width)
            src = cand.at[:, cols]
        else:
            cols = pl.ds(pl.multiple_of(width + half * width, width), width)
            src = operands.at[:, cols]
        return pltpu.make_async_copy(src, to, wide_sem.at[slot, t, half])

    def narrow_copy(g):
        return pltpu.make_async_copy(
            sources[g][1], narrow.at[g % 2], narrow_sem.at[g % 2]
        )

    def load(g):
        narrow_copy(g).start()
        for half in (away, core):
            for t in range(2):
                wide_copy(g, half, t).start()

    def side_at(side):
        return pl.ds(pl.multiple_of(side * side_rows, side_rows), side_rows)

    def shard_at(kind, shard):
        n = shard_rows[kind]
        start = place.side * side_rows if kind == 0 else short_at
        return pl.ds(pl.multiple_of(start + shard * n, 16), n)

    def core_copy(g, kind):
        rows = pl.ds(0, short_at) if kind == 0 else pl.ds(short_at, half_rows - short_at)
        return remote(
            leave.at[g, rows],
            core_in.at[g, rows],
            core_sem.at[0, g, kind],
            core_sem.at[1, g, kind],
            pair,
        )

    def rs_copy(g, kind, direction, source, s):
        rows = pl.ds(0, shard_rows[kind])
        return remote(
            partial.at[g, kind, direction, source, rows],
            partial.at[g, kind, direction, s, rows],
            line_send.at[g, kind, direction],
            rs_recv.at[g, kind, direction, s],
            neighbours[direction],
        )

    def ag_copy(g, kind, direction, shard, s):
        rows = shard_at(kind, shard)
        return remote(
            result.at[g, rows],
            result.at[g, rows],
            line_send.at[g, kind, direction],
            ag_recv.at[g, kind, direction, s],
            neighbours[direction],
        )

    def across_copy(g):
        return remote(
            across_out.at[g], across_in.at[g], across_sem.at[0, g], across_sem.at[1, g], opposite
        )

    def short_copy(g):
        return remote(
            short_out.at[g], short_in.at[g], short_sem.at[0, g], short_sem.at[1, g], opposite
        )

    def back_copy(g, rows):
        return remote(
            result.at[g, rows], result.at[g, rows], back_sem.at[0, g], back_sem.at[1, g], opposite
        )

    def keep_copy(g, rows):
        return pltpu.make_async_copy(result.at[g, rows], out.at[g, core, rows], keep_sem.at[g])

    def pair_copy(g, rows, to):
        return remote(
            result.at[g, rows], out.at[g, to, rows], pair_sem.at[0, g], pair_sem.at[1, g], pair
        )

    def hand_out(g, rows):
        keep_copy(g, rows).start()
        pair_copy(g, rows, core).start()

    def shard_of(direction, steps):
        return steps if direction == 0 else last - steps

    def rs_stage(g, kind, s):
        rows = pl.ds(0, shard_rows[kind])
        for direction in range(2):
            spot = spots[direction]
            mine = shard_at(kind, shard_of(direction, spot + last - s))

            def begin(direction=direction):
                first = shard_at(kind, shard_of(direction, last - s))
                partial[g, kind, direction, s, rows] = own[g, first].astype(BF16)
                rs_copy(g, kind, direction, s, s).start()

            def go_on(direction=direction, mine=mine):
                rs_copy(g, kind, direction, s - 1, s - 1).wait_recv()
                total = own[g, mine] + partial[g, kind, direction, s - 1, rows].astype(F32)
                partial[g, kind, direction, s - 1, rows] = total.astype(BF16)
                rs_copy(g, kind, direction, s - 1, s).start()

            pl.when(spot == 0)(begin)
            if s > 0:
                pl.when((spot > 0) & (spot <= s))(go_on)

    def combine(g, kind):
        rows = pl.ds(0, shard_rows[kind])
        mine = shard_at(kind, place.spot)
        for direction in range(2):

            def add(direction=direction):
                rs_copy(g, kind, direction, last - 1, last - 1).wait_recv()
                own[g, mine] += partial[g, kind, direction, last - 1, rows].astype(F32)

            pl.when(spots[direction] > 0)(add)

    def finished(g, kind, shard):
        rows = shard_at(kind, shard)
        hand_out(g, rows)
        if kind == 0:
            back_copy(g, rows).start()

    def ag_stage(g, kind, s):
        for direction in range(2):
            spot = spots[direction]
            shard = shard_of(direction, spot - s)

            def send(direction=direction, shard=shard):
                ag_copy(g, kind, direction, shard, s).start()

            def receive(direction=direction, shard=shard, send=send, spot=spot):
                ag_copy(g, kind, direction, shard, s - 1).wait_recv()
                if s < last:
                    pl.when(spot < last)(send)
                finished(g, kind, shard)

            if s == 0:
                pl.when(spot < last)(send)
            else:
                pl.when(spot >= s)(receive)
        if s == 0:
            finished(g, kind, place.spot)

    def across_first(g):
        core_copy(g, 0).wait_recv()
        theirs = side_at(1 - place.side)
        ours = side_at(place.side)
        across_out[g] = (own[g, theirs] + core_in[g, theirs].astype(F32)).astype(BF16)
        across_copy(g).start()
        own[g, ours] += core_in[g, ours].astype(F32)

    def across_done(g):
        across_copy(g).wait_recv()
        ours = side_at(place.side)
        own[g, ours] += across_in[g].astype(F32)
        rs_stage(g, 0, 0)

    def line_first(g):
        core_copy(g, 1).wait_recv()
        rows = pl.ds(short_at, half_rows - short_at)
        own[g, rows] += core_in[g, rows].astype(F32)
        rs_stage(g, 1, 0)

    def combine_across(g):
        combine(g, 0)
        mine = shard_at(0, place.spot)
        result[g, mine] = own[g, mine].astype(BF16)
        ag_stage(g, 0, 0)

    def combine_line(g):
        combine(g, 1)
        short_out[g] = own[g, shard_at(1, place.spot)].astype(BF16)
        short_copy(g).start()

    def short_done(g):
        short_copy(g).wait_recv()
        total = short_out[g].astype(F32) + short_in[g].astype(F32)
        result[g, shard_at(1, place.spot)] = total.astype(BF16)
        ag_stage(g, 1, 0)

    def back_done(g):
        rows = side_at(1 - place.side)
        back_copy(g, rows).wait_recv()
        hand_out(g, rows)

    chains = []
    for g in range(groups):
        middle_steps = [functools.partial(rs_stage, g, 0, s) for s in range(1, last)]
        later_steps = [functools.partial(ag_stage, g, 0, s) for s in range(1, line)]
        chains.append(
            [functools.partial(across_first, g), functools.partial(across_done, g)]
            + middle_steps
            + [functools.partial(combine_across, g)]
            + later_steps
            + [functools.partial(back_done, g)]
        )
        middle_steps = [functools.partial(rs_stage, g, 1, s) for s in range(1, last)]
        later_steps = [functools.partial(ag_stage, g, 1, s) for s in range(1, line)]
        chains.append(
            [functools.partial(line_first, g)]
            + middle_steps
            + [functools.partial(combine_line, g), functools.partial(short_done, g)]
            + later_steps
        )

    def advance(chain):
        if chain:
            chain.pop(0)()

    def small_copy(k):
        return remote(
            small_buf.at[0, k],
            small_buf.at[1, k],
            small_sem.at[0, k],
            small_sem.at[1, k],
            doubling[k],
        )

    def small_round(k):
        if k == 0:
            here = small.shape[1]
            small_buf[0, 0, 0:1, 0:here] = jnp.sum(small[...], axis=0, keepdims=True)
            small_buf[0, 0, 0:1, here:] = sums[0:1, :]
            small_copy(0).start()
            return
        small_copy(k - 1).wait()
        total = small_buf[0, k - 1] + small_buf[1, k - 1]
        if k < rounds:
            small_buf[0, k] = total
            small_copy(k).start()
        else:
            small_out[...] = total

    ones = turned.shape[1] - width
    for slot in range(2):
        turned[slot, width:] = jnp.ones((ones, turned.shape[2]), BF16)
    def tiles():
        load(0)
        for g in range(groups):
            if g + 1 < groups:
                load(g + 1)
            narrow_copy(g).wait()
            turned[g % 2, :width] = narrow[g % 2].T
            for half in (away, core):
                for t in range(2):
                    wide_copy(g, half, t).wait()
                    left = turned[(g if g < 3 or t == 1 else 2) % 2]
                    tile = dot(left, wide[g % 2, t, half])
                    if g in (1, 2) or (g == 3 and t == 0):
                        spot = half * width if g == 3 else (half * 2 + t) * width
                        spot = pl.multiple_of(sum_at[g] + spot, width)
                        sums[:, pl.ds(spot, width)] = tile[width : width + LANES]
                    tile = tile[:width]
                    if g == 0 or (g == 3 and t == 1):
                        tile = tile.T
                    rows = pl.ds(t * width, width)
                    if half is away:
                        leave[g, rows, :] = tile.astype(BF16)
                    else:
                        own[g, rows, :] = tile
                if half is away:
                    if g == 0:
                        pl.semaphore_wait(barrier, greeted)
                    for kind in range(2):
                        core_copy(g, kind).start()
                yield

    work = tiles()
    halves = 2 * groups
    small_at = 0
    for at, item in enumerate(sum_order(groups, [len(chain) for chain in chains])):
        if item < 0:
            next(work, None)
            halves -= 1
        else:
            advance(chains[item])
        if halves == 0 and at % 4 == 0 and small_at <= rounds:
            small_round(small_at)
            small_at += 1
    while small_at <= rounds:
        small_round(small_at)
        small_at += 1

    for g in range(groups):
        for kind in range(2):
            core_copy(g, kind).wait_send()
            for direction in range(2):

                def sent(kind=kind, direction=direction):
                    rows = side_at(0) if kind == 0 else pl.ds(short_at, half_rows - short_at)
                    remote(
                        result.at[g, rows],
                        result.at[g, rows],
                        line_send.at[g, kind, direction],
                        ag_recv.at[g, kind, direction, 0],
                        pair,
                    ).wait_send()

                pl.when(spots[direction] < last)(sent)
        across_copy(g).wait_send()
        short_copy(g).wait_send()
        back_copy(g, side_at(place.side)).wait_send()
        rows = pl.ds(0, half_rows)
        keep_copy(g, rows).wait()
        pair_copy(g, rows, away).wait_send()
        pair_copy(g, rows, away).wait_recv()


def unpack_kernel(
    perm_t,
    small_i,
    low_i,
    grad_i,
    down_i,
    up_i,
    gate_i,
    cand_i,
    out_i,
    block_out,
    grad_in,
    w_gate,
    w_cand,
    w_out,
    w_up,
    w_down,
    *vectors,
):
    at = 0
    for vector in vectors:
        n = vector.shape[1]
        vector[...] = small_i[:, at : at + n]
        at += n
    for source, target in (
        (down_i, w_down),
        (up_i, w_up),
        (gate_i, w_gate),
        (cand_i, w_cand),
        (out_i, w_out),
    ):
        target[0] = source[0].astype(F32)
    block_out[...] = dot(perm_t[...], low_i[0]).astype(BF16).reshape(block_out.shape)
    grad_in[...] = dot(perm_t[...], grad_i[0]).reshape(grad_in.shape)


def unpack(packed, small, low, grad, perm_t, rows, width, hidden, ff):
    packed = packed.reshape(4, ff, width)
    vectors = (width, width, width, width, ff, 2 * hidden, hidden)
    parts, chunk = low.shape[0], low.shape[1]
    chunks = parts // rows
    seq = chunks * chunk
    tall = ff // parts
    short = tall // 2
    spread = width // tall
    per_tile = width // short

    def column_block(t):
        return (0, t % spread, t // spread)

    return pl.pallas_call(
        unpack_kernel,
        grid=(parts,),
        out_shape=[
            jax.ShapeDtypeStruct((1, rows, seq, width), BF16),
            jax.ShapeDtypeStruct((1, rows, seq, width), F32),
            jax.ShapeDtypeStruct((1, width, 2 * hidden), F32),
            jax.ShapeDtypeStruct((1, width, hidden), F32),
            jax.ShapeDtypeStruct((1, hidden, width), F32),
            jax.ShapeDtypeStruct((1, width, ff), F32),
            jax.ShapeDtypeStruct((1, ff, width), F32),
        ]
        + [jax.ShapeDtypeStruct((1, n), F32) for n in vectors],
        in_specs=[
            whole(perm_t),
            whole(small),
            pl.BlockSpec((1, chunk, width), lambda t: (t, 0, 0)),
            pl.BlockSpec((1, chunk, width), lambda t: (t, 0, 0)),
            pl.BlockSpec((1, tall, width), lambda t: (0, t, 0)),
            pl.BlockSpec((1, tall, width), lambda t: (1, t, 0)),
            pl.BlockSpec((1, tall, width), lambda t: (2, t, 0)),
            pl.BlockSpec(
                (1, short, width),
                lambda t: (3, t // per_tile * 2 * per_tile + t % per_tile, 0),
            ),
            pl.BlockSpec(
                (1, short, width),
                lambda t: (3, t // per_tile * 2 * per_tile + per_tile + t % per_tile, 0),
            ),
        ],
        out_specs=[
            pl.BlockSpec((1, 1, chunk, width), lambda t: (0, t // chunks, t % chunks, 0)),
            pl.BlockSpec((1, 1, chunk, width), lambda t: (0, t // chunks, t % chunks, 0)),
            pl.BlockSpec((1, tall, width), column_block),
            pl.BlockSpec((1, short, width), lambda t: (0, t % per_tile, t // per_tile)),
            pl.BlockSpec((1, short, width), lambda t: (0, t, 0)),
            pl.BlockSpec((1, tall, width), column_block),
            pl.BlockSpec((1, tall, width), lambda t: (0, t, 0)),
        ]
        + [pl.BlockSpec((1, n), lambda t: (0, 0)) for n in vectors],
        compiler_params=pltpu.CompilerParams(vmem_limit_bytes=VMEM_LIMIT),
        name="unpack",
    )(perm_t, small, low, grad, packed, packed, packed, packed, packed)


def sum_gradients(operands, small, hidden, ff):
    place = Place()
    line = place.line
    rounds = len(place.doubling())
    operands = [a.reshape(-1, a.shape[-1]) for a in operands]
    tokens, width = operands[2].shape
    total = small.shape[1] + ff + 3 * hidden
    groups = 4
    half_rows = ff // 2
    side_rows = half_rows * 3 // 8
    shard = side_rows // line
    short = (half_rows - 2 * side_rows) // line
    anywhere = pl.BlockSpec(memory_space=pl.ANY)
    here = pl.BlockSpec(memory_space=pltpu.VMEM)
    packed, small_sum = pl.pallas_call(
        functools.partial(sum_kernel, line, rounds),
        out_shape=[
            jax.ShapeDtypeStruct((groups, 2, half_rows, width), BF16),
            jax.ShapeDtypeStruct((1, total), F32),
        ],
        in_specs=[anywhere] * 7 + [here],
        out_specs=[anywhere, here],
        scratch_shapes=[
            pltpu.VMEM((2, 2, 2, tokens, width), BF16),
            pltpu.VMEM((2, tokens, width), BF16),
            pltpu.VMEM((2, width + 2 * LANES, tokens), BF16),
            pltpu.VMEM((groups, half_rows, width), F32),
            pltpu.VMEM((groups, half_rows, width), BF16),
            pltpu.VMEM((groups, half_rows, width), BF16),
            pltpu.VMEM((groups, side_rows, width), BF16),
            pltpu.VMEM((groups, side_rows, width), BF16),
            pltpu.VMEM((groups, short, width), BF16),
            pltpu.VMEM((groups, short, width), BF16),
            pltpu.VMEM((groups, 2, 2, line - 1, max(shard, short), width), BF16),
            pltpu.VMEM((groups, half_rows, width), BF16),
            pltpu.VMEM((2, rounds, 1, total), F32),
            pltpu.VMEM((LANES, ff + 3 * hidden), F32),
            pltpu.SemaphoreType.DMA((2, 2, 2)),
            pltpu.SemaphoreType.DMA((2,)),
            pltpu.SemaphoreType.DMA((2, groups, 2)),
            pltpu.SemaphoreType.DMA((2, groups)),
            pltpu.SemaphoreType.DMA((2, groups)),
            pltpu.SemaphoreType.DMA((2, groups)),
            pltpu.SemaphoreType.DMA((groups, 2, 2)),
            pltpu.SemaphoreType.DMA((groups, 2, 2, line - 1)),
            pltpu.SemaphoreType.DMA((groups, 2, 2, line - 1)),
            pltpu.SemaphoreType.DMA((groups,)),
            pltpu.SemaphoreType.DMA((2, groups)),
            pltpu.SemaphoreType.DMA((2, rounds)),
        ],
        compiler_params=pltpu.CompilerParams(
            collective_id=2, has_side_effects=True, vmem_limit_bytes=VMEM_LIMIT
        ),
        name="sum_gradients",
    )(*operands, small)
    dp_size = lax.axis_size("dp")
    inner = 2 * line
    if dp_size > inner:
        members = [list(range(i, dp_size, inner)) for i in range(inner)]
        packed, small_sum = lax.psum((packed, small_sum), "dp", axis_index_groups=members)
    return packed, small_sum


def body(tokens, resets, cotangent, *stacked):
    rows, _, width = tokens.shape
    hidden = stacked[3].shape[2]
    ff = stacked[8].shape[2]
    low, grad_in, perm_t, (*operands, small) = local_grads(tokens, resets, cotangent, stacked)
    packed, small_sum = sum_gradients(operands, small, hidden, ff)
    block_out, grad_in, w_gate, w_cand, w_out, w_up, w_down, *vectors = unpack(
        packed, small_sum, low, grad_in, perm_t, rows, width, hidden, ff
    )
    g_one, b_out, g_two, b_down, b_up, b_gate, b_cand = vectors
    grads = (g_one, w_gate, b_gate, w_cand, b_cand, w_out, b_out, g_two, w_up, b_up, w_down, b_down)
    return (block_out, grad_in) + grads


def solution(mesh):
    vector = P("section", None)
    matrix = P("section", None, None)
    weight_specs = (
        vector,
        matrix,
        vector,
        matrix,
        vector,
        matrix,
        vector,
        vector,
        matrix,
        vector,
        matrix,
        vector,
    )
    tokens = P(("dp", "rep"), None, None)
    by_rows = P("section", ("dp", "rep"), None, None)
    return jax.shard_map(
        body,
        mesh=mesh,
        in_specs=(tokens, P(("dp", "rep"), None), tokens) + weight_specs,
        out_specs=(by_rows, by_rows) + weight_specs,
        check_vma=False,
    )
```

```python
import functools
import math

import jax
import jax.numpy as jnp
import numpy as np
from jax import lax
from jax.experimental import pallas as pl
from jax.experimental.pallas import tpu as pltpu
from jax.sharding import PartitionSpec as P

EPS = 1e-06
F32 = jnp.float32
BF16 = jnp.bfloat16
CHUNK = 256
LANES = 8
WIDTH = 256
GELU_A = math.sqrt(2.0 / math.pi)
GELU_B = 0.044715
LN4 = math.log(4.0)
EXP_TOP = 85.6
VMEM_LIMIT = 60 * 1024 * 1024
BLOCKS_VMEM = 63 * 1024 * 1024


def dot(a, b):
    return jnp.dot(a, b, preferred_element_type=F32)


def dot_nt(a, b):
    return lax.dot_general(a, b, (((1,), (1,)), ((), ())), preferred_element_type=F32)


def inv_scale(values):
    return lax.rsqrt(jnp.mean(values * values, axis=-1, keepdims=True) + EPS)


def partner_barrier_signal(partner):
    pl.semaphore_signal(
        pltpu.get_barrier_semaphore(),
        inc=1,
        device_id={"section": partner},
        device_id_type=pl.DeviceIdType.MESH,
    )


def interleave(*streams):
    live = list(streams)
    while live:
        for stream in list(live):
            if next(stream, live) is live:
                live.remove(stream)


def scan_segments(product, accum, carry, reverse):
    which = lax.broadcasted_iota(jnp.int32, product.shape, 0)
    span = 1
    while span < LANES:
        turn = LANES - span if reverse else span
        inside = which < LANES - span if reverse else which >= span
        accum = jnp.where(inside, product * pltpu.roll(accum, turn, 0) + accum, accum)
        product = jnp.where(inside, product * pltpu.roll(product, turn, 0), product)
        span *= 2
    reached = product * carry + accum
    edge = LANES - 1 if reverse else 0
    incoming = jnp.where(which == edge, carry, pltpu.roll(reached, LANES - 1 if reverse else 1, 0))
    end = 0 if reverse else LANES - 1
    return incoming, jnp.broadcast_to(reached[end : end + 1], reached.shape)


class Step:
    def __init__(self, step, rows, chunks):
        first = lax.axis_index("section") == 0
        apart = 2 * chunks
        joint = chunks + 1
        middle = step - apart
        final = middle >= (2 * rows - 2) * joint
        phase = jnp.where(step < apart, 0, jnp.where(final, 2 * rows - 1, 1 + middle // joint))
        alone = (step < apart) | final
        at = jnp.where(step < apart, step, middle - (2 * rows - 2) * joint)
        along = middle % joint
        self.early = jnp.where(alone, at // 2, jnp.minimum(along, chunks - 1))
        self.late = jnp.where(alone, at // 2, jnp.maximum(along - 1, 0))
        self.begins = jnp.where(alone, at % 2 == 0, along < chunks)
        self.ends = jnp.where(alone, at % 2 == 1, along > 0)
        self.forward = jnp.where(first, phase < rows, phase % 2 == 0)
        self.backward = jnp.logical_not(self.forward)
        self.row = jnp.where(first, phase % rows, phase // 2)
        base = self.row * chunks
        last = chunks - 1
        self.mixer = base + self.early
        self.feed = base + self.late
        self.back_feed = base + last - self.early
        self.back_mixer = base + last - self.late
        total = rows * chunks
        self.next_mixer = jnp.minimum(self.mixer + 1, total - 1)
        later = jnp.minimum(base + self.early + 1, total - 1)
        self.next_back = later // chunks * chunks + last - later % chunks


def blocks_kernel(
    rows,
    chunks,
    tok,
    cot,
    w_gate_all,
    w_cand_all,
    w_out_all,
    w_up_all,
    w_down_all,
    keep_rows,
    perm,
    g_one,
    b_gate,
    b_cand,
    b_out,
    g_two,
    b_up,
    b_down,
    operands_all,
    active_all,
    low_all,
    down_all,
    up_all,
    mix_all,
    gate_all,
    cand_all,
    grad_all,
    small_o,
    raw,
    keep,
    w_gate,
    w_cand,
    w_out,
    w_up,
    w_down,
    operands_o,
    active_o,
    low_o,
    down_o,
    up_o,
    mix_o,
    gate_o,
    cand_o,
    grad_o,
    ratio_s,
    slopes_s,
    middle_s,
    slope_up_s,
    inputs,
    send,
    received,
    coming,
    coming_back,
    carry,
    carry_back,
    normed_two_s,
    grad_middle_s,
    mix_s,
    load_sem,
    stage_sem,
    send_sem,
    input_sem,
    back_send_sem,
    received_sem,
):
    section = lax.axis_index("section")
    partner = 1 - section
    chunk, width = coming.shape
    hidden = w_cand.shape[1]
    ff = w_up.shape[1]
    span = chunk // LANES
    total = rows * chunks
    steps = 4 * chunks + (2 * rows - 2) * (chunks + 1)
    stages = (
        (operands_o, operands_all),
        (active_o, active_all),
        (low_o, low_all),
        (down_o, down_all),
        (up_o, up_all),
        (mix_o, mix_all),
        (gate_o, gate_all),
        (cand_o, cand_all),
        (grad_o, grad_all),
    )

    def stage_copy(which, at_chunk):
        source, target = stages[which]
        slot = at_chunk % 2
        return pltpu.make_async_copy(
            source.at[slot], target.at[at_chunk], stage_sem.at[which, slot]
        )

    def load_copy(which):
        pairs = (
            (w_gate_all, w_gate),
            (w_cand_all, w_cand),
            (w_out_all, w_out),
            (w_up_all, w_up),
            (w_down_all, w_down),
        )
        return pltpu.make_async_copy(*pairs[which], load_sem.at[which])

    def raw_copy(source):
        return pltpu.make_async_copy(source, raw, load_sem.at[5])

    def raw_chunk(at_chunk):
        start = pl.multiple_of(at_chunk % chunks * chunk, chunk)
        return raw[at_chunk // chunks, pl.ds(start, chunk)]

    def chunk_copy(slot):
        return remote(
            send.at[slot],
            inputs.at[slot],
            send_sem.at[slot],
            input_sem.at[slot],
            {"section": partner},
        )

    def back_copy(slot):
        return remote(
            send.at[slot],
            received.at[slot],
            back_send_sem.at[slot],
            received_sem.at[slot],
            {"section": partner},
        )

    def add_small(which, values):
        part = jnp.sum(values.reshape(-1, LANES, width), axis=0)
        small_o[:, which * width : (which + 1) * width] += part

    def blocks_step(c):
        step = Step(c, rows, chunks)

        @pl.when(c == 1)
        def _():
            load_copy(3).wait()
            load_copy(4).wait()

        starts = step.begins & (step.early == 0)

        @pl.when(step.forward & starts)
        def _():
            carry[...] = jnp.zeros_like(carry)

        @pl.when(step.backward & starts)
        def _():
            carry_back[...] = jnp.zeros_like(carry_back)

        @pl.when(step.forward & step.begins & (section == 0))
        def _():
            inputs[step.mixer] = coming[...]

        @pl.when(step.forward & step.begins & (section == 1))
        def _():
            chunk_copy(step.mixer).wait_recv()

        @pl.when(step.backward & step.begins & (section == 0))
        def _():
            back_copy(step.back_feed).wait_recv()
            coming_back[...] = received[step.back_feed]

        @pl.when(step.forward & step.begins & (step.mixer >= 2))
        def _():
            stage_copy(0, step.mixer).wait()

        @pl.when(step.forward & step.ends & (step.feed >= 2))
        def _():
            for which in (1, 2):
                stage_copy(which, step.feed).wait()

        @pl.when(step.backward & step.begins & (step.mixer >= 2))
        def _():
            for which in (3, 4, 5):
                stage_copy(which, step.back_feed).wait()

        @pl.when(step.backward & step.ends & (step.feed >= 2))
        def _():
            for which in (6, 7, 8):
                stage_copy(which, step.back_mixer).wait()

        def mixer():
            at_chunk = step.mixer
            slot = at_chunk % 2
            x = inputs[at_chunk].astype(F32)
            normed = (x * inv_scale(x) * g_one[...]).astype(BF16)
            operands_o[slot, :, :width] = normed
            yield
            for at in range(0, hidden, WIDTH):
                cols = slice(at, at + WIDTH)
                cols_in = slice(hidden + at, hidden + at + WIDTH)
                pre_f = dot(normed, w_gate[:, cols])
                pre_i = dot(normed, w_gate[:, cols_in])
                cand = dot(normed, w_cand[:, cols]) + b_cand[:, cols]
                u = jnp.exp(jnp.minimum((-LN4 - b_gate[:, cols]) - pre_f, EXP_TOP))
                v = jnp.exp(jnp.minimum((-LN4 - b_gate[:, cols_in]) - pre_i, EXP_TOP))
                d = 1.0 / (0.5 + u + v)
                ratio_f = (0.25 + v) * d
                ratio_i = (0.25 + u) * d
                ratio_s[at_chunk, :, cols] = ratio_f
                keep_w = jnp.concatenate([keep[at_chunk]] * (WIDTH // 128), axis=1)
                decay = ratio_f * keep_w
                drive = ratio_i * cand
                product = decay[0:LANES]
                accum = drive[0:LANES]
                for j in range(1, span):
                    r = slice(j * LANES, (j + 1) * LANES)
                    accum = decay[r] * accum + drive[r]
                    product = decay[r] * product
                state, carry[:, cols] = scan_segments(product, accum, carry[:, cols], False)
                before = []
                after = []
                for j in range(span):
                    r = slice(j * LANES, (j + 1) * LANES)
                    before.append(state)
                    state = decay[r] * state + drive[r]
                    after.append(state)
                operands_o[slot, :, width + at : width + at + WIDTH] = jnp.concatenate(
                    after, axis=0
                ).astype(BF16)
                lever = keep_w * jnp.concatenate(before, axis=0) - cand
                slopes_s[at_chunk, :, cols] = (lever * ((u * d) * ratio_f)).astype(BF16)
                slopes_s[at_chunk, :, cols_in] = (-lever * ((v * d) * ratio_i)).astype(BF16)
                yield
            mixed = dot(operands_o[slot, :, width : width + hidden], w_out[...])
            yield
            middle = x + (mixed + b_out[...])
            normed_two = (middle * inv_scale(middle) * g_two[...]).astype(BF16)
            operands_o[slot, :, width + hidden :] = normed_two
            yield
            middle_s[at_chunk] = middle
            normed_two_s[...] = normed_two

        def feed():
            at_chunk = step.feed
            slot = at_chunk % 2
            for at in range(0, ff, WIDTH):
                cols = slice(at, at + WIDTH)
                up = dot(normed_two_s[...], w_up[:, cols]) + b_up[:, cols]
                square = up * up
                half = 0.5 + 0.5 * jnp.tanh(up * (GELU_A + (GELU_A * GELU_B) * square))
                act = up * half
                active_o[slot, :, cols] = act.astype(BF16)
                slope = half + act * (1.0 - half) * (2 * GELU_A + (6 * GELU_A * GELU_B) * square)
                slope_up_s[at_chunk, :, cols] = slope.astype(BF16)
                if at % (2 * WIDTH):
                    yield
            down = dot(active_o[slot], w_down[...])
            yield
            low_o[slot] = (middle_s[at_chunk] + (down + b_down[...])).astype(BF16)

        def reorder():
            yield
            yield
            coming[...] = dot(perm[...], raw_chunk(step.next_mixer)).astype(BF16)

        def back_feed():
            at_chunk = step.back_feed
            slot = at_chunk % 2
            grad_down = coming_back[...]
            down_o[slot] = grad_down
            yield
            for at in range(0, ff, WIDTH):
                cols = slice(at, at + WIDTH)
                grad_active = dot_nt(grad_down, w_down[cols, :])
                slope = slope_up_s[at_chunk, :, cols].astype(F32)
                up_o[slot, :, cols] = (grad_active * slope).astype(BF16)
                if at % (2 * WIDTH):
                    yield
            q = dot_nt(up_o[slot], w_up[...])
            yield
            dy = grad_down.astype(F32)
            add_small(3, dy)
            middle = middle_s[at_chunk]
            r = inv_scale(middle)
            scaled = middle * r
            add_small(2, q * scaled)
            weighted = q * g_two[...]
            grad_middle = dy + r * (
                weighted - scaled * jnp.mean(weighted * scaled, axis=-1, keepdims=True)
            )
            add_small(1, grad_middle)
            grad_mix = grad_middle.astype(BF16)
            mix_o[slot] = grad_mix
            yield
            yield
            grad_middle_s[...] = grad_middle
            mix_s[...] = grad_mix

        def back_mixer():
            at_chunk = step.back_mixer
            slot = at_chunk % 2
            for at in range(0, hidden, WIDTH):
                cols = slice(at, at + WIDTH)
                cols_in = slice(hidden + at, hidden + at + WIDTH)
                grad_state = dot_nt(mix_s[...], w_out[cols, :])
                ratio_f = ratio_s[at_chunk, :, cols]
                decay = ratio_f * jnp.concatenate([keep[at_chunk]] * (WIDTH // 128), axis=1)
                last = slice((span - 1) * LANES, span * LANES)
                product = decay[last]
                accum = decay[last] * grad_state[last]
                for j in range(span - 2, -1, -1):
                    rj = slice(j * LANES, (j + 1) * LANES)
                    accum = decay[rj] * (grad_state[rj] + accum)
                    product = decay[rj] * product
                later, carry_back[:, cols] = scan_segments(product, accum, carry_back[:, cols], True)
                parts = [None] * span
                for j in range(span - 1, -1, -1):
                    rj = slice(j * LANES, (j + 1) * LANES)
                    carried = grad_state[rj] + later
                    parts[j] = carried
                    later = decay[rj] * carried
                carried = jnp.concatenate(parts, axis=0)
                gate_o[slot, :, cols] = (carried * slopes_s[at_chunk, :, cols].astype(F32)).astype(BF16)
                gate_o[slot, :, cols_in] = (
                    carried * slopes_s[at_chunk, :, cols_in].astype(F32)
                ).astype(BF16)
                cand_o[slot, :, cols] = (carried * (1.0 - ratio_f)).astype(BF16)
                yield
            p = dot_nt(gate_o[slot], w_gate[...]) + dot_nt(cand_o[slot], w_cand[...])
            yield
            x = inputs[at_chunk].astype(F32)
            r = inv_scale(x)
            scaled = x * r
            add_small(0, p * scaled)
            weighted = p * g_one[...]
            grad_input = grad_middle_s[...] + r * (
                weighted - scaled * jnp.mean(weighted * scaled, axis=-1, keepdims=True)
            )
            grad_o[slot] = grad_input.astype(BF16)

        def back_reorder():
            yield
            yield
            coming_back[...] = dot(perm[...], raw_chunk(step.next_back)).astype(BF16)

        both = step.begins & step.ends
        only_first = jnp.logical_not(step.ends)
        only_second = jnp.logical_not(step.begins)

        @pl.when(step.forward & only_first)
        def _():
            interleave(mixer(), reorder())

        @pl.when(step.forward & both)
        def _():
            interleave(mixer(), feed(), reorder())

        @pl.when(step.forward & only_second)
        def _():
            interleave(feed())

        @pl.when(step.backward & only_first)
        def _():
            interleave(back_feed(), back_reorder())

        @pl.when(step.backward & both)
        def _():
            interleave(back_feed(), back_mixer(), back_reorder())

        @pl.when(step.backward & only_second)
        def _():
            interleave(back_mixer())

        @pl.when(step.forward & step.ends & (section == 0))
        def _():
            send[step.feed] = low_o[step.feed % 2]
            chunk_copy(step.feed).start()

        @pl.when(step.backward & step.ends & (section == 1))
        def _():
            send[step.back_mixer] = grad_o[step.back_mixer % 2]
            back_copy(step.back_mixer).start()

        @pl.when(step.forward & step.begins)
        def _():
            stage_copy(0, step.mixer).start()

        @pl.when(step.forward & step.ends)
        def _():
            for which in (1, 2):
                stage_copy(which, step.feed).start()

        @pl.when(step.backward & step.begins)
        def _():
            for which in (3, 4, 5):
                stage_copy(which, step.back_feed).start()

        @pl.when(step.backward & step.ends)
        def _():
            for which in (6, 7, 8):
                stage_copy(which, step.back_mixer).start()

    partner_barrier_signal(partner)
    pl.when(section == 0)(lambda: raw_copy(tok).start())
    pl.when(section == 1)(lambda: raw_copy(cot).start())
    for which in range(5):
        load_copy(which).start()
    small_o[...] = jnp.zeros_like(small_o)
    raw_copy(tok).wait()
    coming[...] = dot(perm[...], raw_chunk(0)).astype(BF16)
    coming_back[...] = dot(perm[...], raw_chunk(chunks - 1)).astype(BF16)
    pl.semaphore_wait(pltpu.get_barrier_semaphore(), 1)
    for at_chunk in range(total):
        row = keep_rows[at_chunk : at_chunk + 1, :]
        keep[at_chunk] = jnp.broadcast_to(row, (128, chunk)).T
    for which in range(3):
        load_copy(which).wait()

    @pl.loop(0, steps)
    def _(c):
        blocks_step(c)

    @pl.when(section == 0)
    def _():
        for slot in range(total):
            chunk_copy(slot).wait_send()

    @pl.when(section == 1)
    def _():
        for slot in range(total):
            back_copy(slot).wait_send()

    for which in range(len(stages)):
        for slot in range(2):
            stage_copy(which, slot).wait()


def whole(array):
    zeros = (0,) * array.ndim
    return pl.BlockSpec(array.shape, lambda c: zeros, pipeline_mode=pl.Buffered(1))


def run_blocks(tokens, cotangent, keep, perm, weights, chunk):
    rows, seq, width = tokens.shape
    chunks = seq // chunk
    total = rows * chunks
    g_one, w_gate, b_gate, w_cand, b_cand, w_out, b_out, g_two, w_up, b_up, w_down, b_down = weights
    hidden = w_cand.shape[1]
    ff = w_up.shape[1]
    large = (w_gate, w_cand, w_out, w_up, w_down)
    little = (keep, perm, g_one, b_gate, b_cand, b_out, g_two, b_up, b_down)
    columns = (2 * width + hidden, ff, width, width, ff, width, 2 * hidden, hidden, width)
    anywhere = pl.BlockSpec(memory_space=pl.ANY)
    here = pl.BlockSpec(memory_space=pltpu.VMEM)
    return pl.pallas_call(
        functools.partial(blocks_kernel, rows, chunks),
        out_shape=[jax.ShapeDtypeStruct((total, chunk, n), BF16) for n in columns]
        + [jax.ShapeDtypeStruct((LANES, 4 * width), F32)],
        in_specs=[anywhere] * 7 + [here] * len(little),
        out_specs=[anywhere] * len(columns) + [here],
        scratch_shapes=[
            pltpu.VMEM(tokens.shape, BF16),
            pltpu.VMEM((total, chunk, 128), F32),
        ]
        + [pltpu.VMEM(w.shape, BF16) for w in large]
        + [pltpu.VMEM((2, chunk, n), BF16) for n in columns]
        + [
            pltpu.VMEM((total, chunk, hidden), F32),
            pltpu.VMEM((total, chunk, 2 * hidden), BF16),
            pltpu.VMEM((total, chunk, width), F32),
            pltpu.VMEM((total, chunk, ff), BF16),
            pltpu.VMEM((total, chunk, width), BF16),
            pltpu.VMEM((total, chunk, width), BF16),
            pltpu.VMEM((total, chunk, width), BF16),
            pltpu.VMEM((chunk, width), BF16),
            pltpu.VMEM((chunk, width), BF16),
            pltpu.VMEM((LANES, hidden), F32),
            pltpu.VMEM((LANES, hidden), F32),
            pltpu.VMEM((chunk, width), BF16),
            pltpu.VMEM((chunk, width), F32),
            pltpu.VMEM((chunk, width), BF16),
            pltpu.SemaphoreType.DMA((6,)),
            pltpu.SemaphoreType.DMA((len(columns), 2)),
            pltpu.SemaphoreType.DMA((total,)),
            pltpu.SemaphoreType.DMA((total,)),
            pltpu.SemaphoreType.DMA((total,)),
            pltpu.SemaphoreType.DMA((total,)),
        ],
        compiler_params=pltpu.CompilerParams(
            collective_id=0, has_side_effects=True, vmem_limit_bytes=BLOCKS_VMEM
        ),
        name="blocks",
    )(tokens, cotangent, *large, *little)


def local_grads(tokens, resets, cotangent, stacked):
    weights = tuple(w if w.ndim == 2 else w[0] for w in stacked)
    rows, seq, width = tokens.shape
    chunk = min(CHUNK, seq)
    total = rows * (seq // chunk)
    span = chunk // LANES
    keep = (1 - resets).astype(F32).reshape(total, LANES, span)
    keep = keep.transpose(0, 2, 1).reshape(total, chunk)
    at = np.arange(chunk)
    source = (at % LANES) * span + at // LANES
    perm_t = np.equal(at[:, None], source[None, :])
    perm = jnp.asarray(perm_t.T, BF16)
    perm_t = jnp.asarray(perm_t, BF16)
    operands, active, low, *grads, grad_in, small = run_blocks(
        tokens, cotangent, keep, perm, weights, chunk
    )
    return low, grad_in, perm_t, (operands, active, *grads, small)


class Place:
    def __init__(self):
        dp_size = lax.axis_size("dp")
        chips = dp_size // 2
        self.line = 4 if chips % 4 == 0 else chips
        dp = lax.axis_index("dp")
        self.side = lax.axis_index("rep")
        self.core = dp % 2
        self.base = (dp // 2) // self.line * self.line
        self.spot = (dp // 2) % self.line

    def along(self, step):
        return {"dp": (self.base + self.spot + step) * 2 + self.core}

    def across(self):
        return {"rep": 1 - self.side}

    def other_core(self):
        return {"dp": (self.base + self.spot) * 2 + 1 - self.core}

    def doubling(self):
        found = [self.other_core()]
        span = 1
        while span < self.line:
            found.append(self.along(span - 2 * span * ((self.spot // span) % 2)))
            span *= 2
        return found + [self.across()]


def remote(src, dst, send_sem, recv_sem, device):
    return pltpu.make_async_remote_copy(
        src_ref=src,
        dst_ref=dst,
        send_sem=send_sem,
        recv_sem=recv_sem,
        device_id=device,
        device_id_type=pl.DeviceIdType.MESH,
    )


SUM_ORDER = (
    -1, -1, 1, 0, -1, 1, -1, 3, 1, 2, 3, -1, 0, 3, 0, -1, 1, 5, 0, 3, 4, 2, 5, 1, 2, 0, -1, 3,
    2, 5, 0, 1, -1, 3, 7, 6, 4, 2, 5, 0, 4, 1, 7, 2, 4, 3, 6, 7, 2, 6, 4, 7, 6, 2, 3, 0, 4, 6,
    4, 1, 5, 6, 7, 6, 5, 2, 4, 7, 6, 4, 5, 7, 5, 0, 6, 7,
)


def sum_order(groups, lengths):
    if all(SUM_ORDER.count(c) == n for c, n in enumerate(lengths)):
        return SUM_ORDER
    order = []
    left = list(lengths)
    for g in range(groups):
        for _ in range(2):
            order.append(-1)
            for c in range(2 * g):
                if left[c]:
                    order.append(c)
                    left[c] -= 1
    while any(left):
        for c, n in enumerate(left):
            if n:
                order.append(c)
                left[c] -= 1
    return order


def sum_kernel(
    line,
    rounds,
    operands,
    feed,
    down,
    up,
    mix,
    gate,
    cand,
    small,
    out,
    small_out,
    wide,
    narrow,
    turned,
    own,
    leave,
    core_in,
    across_out,
    across_in,
    short_out,
    short_in,
    partial,
    result,
    small_buf,
    sums,
    wide_sem,
    narrow_sem,
    core_sem,
    across_sem,
    back_sem,
    short_sem,
    line_send,
    rs_recv,
    ag_recv,
    keep_sem,
    pair_sem,
    small_sem,
):
    place = Place()
    width = down.shape[1]
    groups = out.shape[0]
    half_rows = out.shape[2]
    last = line - 1
    side_rows = across_out.shape[1]
    shard_rows = (side_rows // line, short_out.shape[1])
    short_at = 2 * side_rows
    core = place.core
    away = 1 - core
    pair = place.other_core()
    opposite = place.across()
    neighbours = (place.along(1), place.along(-1))
    spots = (place.spot, last - place.spot)
    doubling = place.doubling()

    barrier = pltpu.get_barrier_semaphore()

    def greet(peer):
        pl.semaphore_signal(
            barrier, inc=1, device_id=peer, device_id_type=pl.DeviceIdType.MESH
        )

    for peer in doubling:
        greet(peer)
    for direction in range(2):
        pl.when(spots[direction] < last)(functools.partial(greet, neighbours[direction]))
    greeted = len(doubling) + jnp.where(spots[0] < last, 1, 0) + jnp.where(spots[1] < last, 1, 0)

    hidden = cand.shape[1]
    ff = up.shape[1]
    normed_two = operands.at[:, pl.ds(width + hidden, width)]
    normed = operands.at[:, pl.ds(0, width)]
    sources = [(feed, down), (up, normed_two), (gate, normed), (None, mix)]
    sum_at = [None, 0, ff, ff + 2 * hidden]

    def wide_copy(g, half, t):
        slot = g % 2
        to = wide.at[slot, t, half]
        if g < 3:
            cols = pl.ds(pl.multiple_of((half * 2 + t) * width, width), width)
            src = sources[g][0].at[:, cols]
        elif t == 0:
            cols = pl.ds(pl.multiple_of(half * width, width), width)
            src = cand.at[:, cols]
        else:
            cols = pl.ds(pl.multiple_of(width + half * width, width), width)
            src = operands.at[:, cols]
        return pltpu.make_async_copy(src, to, wide_sem.at[slot, t, half])

    def narrow_copy(g):
        return pltpu.make_async_copy(
            sources[g][1], narrow.at[g % 2], narrow_sem.at[g % 2]
        )

    def load(g, half):
        if half is away:
            narrow_copy(g).start()
        for t in range(2):
            wide_copy(g, half, t).start()

    def side_at(side):
        return pl.ds(pl.multiple_of(side * side_rows, side_rows), side_rows)

    def shard_at(kind, shard):
        n = shard_rows[kind]
        start = place.side * side_rows if kind == 0 else short_at
        return pl.ds(pl.multiple_of(start + shard * n, 16), n)

    def core_copy(g, kind):
        rows = pl.ds(0, short_at) if kind == 0 else pl.ds(short_at, half_rows - short_at)
        return remote(
            leave.at[g, rows],
            core_in.at[g, rows],
            core_sem.at[0, g, kind],
            core_sem.at[1, g, kind],
            pair,
        )

    def rs_copy(g, kind, direction, source, s):
        rows = pl.ds(0, shard_rows[kind])
        return remote(
            partial.at[g, kind, direction, source, rows],
            partial.at[g, kind, direction, s, rows],
            line_send.at[g, kind, direction],
            rs_recv.at[g, kind, direction, s],
            neighbours[direction],
        )

    def ag_copy(g, kind, direction, shard, s):
        rows = shard_at(kind, shard)
        return remote(
            result.at[g, rows],
            result.at[g, rows],
            line_send.at[g, kind, direction],
            ag_recv.at[g, kind, direction, s],
            neighbours[direction],
        )

    def across_copy(g):
        return remote(
            across_out.at[g], across_in.at[g], across_sem.at[0, g], across_sem.at[1, g], opposite
        )

    def short_copy(g):
        return remote(
            short_out.at[g], short_in.at[g], short_sem.at[0, g], short_sem.at[1, g], opposite
        )

    def back_copy(g, rows):
        return remote(
            result.at[g, rows], result.at[g, rows], back_sem.at[0, g], back_sem.at[1, g], opposite
        )

    def keep_copy(g, rows):
        return pltpu.make_async_copy(result.at[g, rows], out.at[g, core, rows], keep_sem.at[g])

    def pair_copy(g, rows, to):
        return remote(
            result.at[g, rows], out.at[g, to, rows], pair_sem.at[0, g], pair_sem.at[1, g], pair
        )

    def hand_out(g, rows):
        keep_copy(g, rows).start()
        pair_copy(g, rows, core).start()

    def shard_of(direction, steps):
        return steps if direction == 0 else last - steps

    def rs_stage(g, kind, s):
        rows = pl.ds(0, shard_rows[kind])
        for direction in range(2):
            spot = spots[direction]
            mine = shard_at(kind, shard_of(direction, spot + last - s))

            def begin(direction=direction):
                first = shard_at(kind, shard_of(direction, last - s))
                partial[g, kind, direction, s, rows] = own[g, first].astype(BF16)
                rs_copy(g, kind, direction, s, s).start()

            def go_on(direction=direction, mine=mine):
                rs_copy(g, kind, direction, s - 1, s - 1).wait_recv()
                total = own[g, mine] + partial[g, kind, direction, s - 1, rows].astype(F32)
                partial[g, kind, direction, s - 1, rows] = total.astype(BF16)
                rs_copy(g, kind, direction, s - 1, s).start()

            pl.when(spot == 0)(begin)
            if s > 0:
                pl.when((spot > 0) & (spot <= s))(go_on)

    def combine(g, kind):
        rows = pl.ds(0, shard_rows[kind])
        mine = shard_at(kind, place.spot)
        for direction in range(2):

            def add(direction=direction):
                rs_copy(g, kind, direction, last - 1, last - 1).wait_recv()
                own[g, mine] += partial[g, kind, direction, last - 1, rows].astype(F32)

            pl.when(spots[direction] > 0)(add)

    def finished(g, kind, shard):
        rows = shard_at(kind, shard)
        hand_out(g, rows)
        if kind == 0:
            back_copy(g, rows).start()

    def ag_stage(g, kind, s):
        for direction in range(2):
            spot = spots[direction]
            shard = shard_of(direction, spot - s)

            def send(direction=direction, shard=shard):
                ag_copy(g, kind, direction, shard, s).start()

            def receive(direction=direction, shard=shard, send=send, spot=spot):
                ag_copy(g, kind, direction, shard, s - 1).wait_recv()
                if s < last:
                    pl.when(spot < last)(send)
                finished(g, kind, shard)

            if s == 0:
                pl.when(spot < last)(send)
            else:
                pl.when(spot >= s)(receive)
        if s == 0:
            finished(g, kind, place.spot)

    def across_first(g):
        core_copy(g, 0).wait_recv()
        theirs = side_at(1 - place.side)
        ours = side_at(place.side)
        across_out[g] = (own[g, theirs] + core_in[g, theirs].astype(F32)).astype(BF16)
        across_copy(g).start()
        own[g, ours] += core_in[g, ours].astype(F32)

    def across_done(g):
        across_copy(g).wait_recv()
        ours = side_at(place.side)
        own[g, ours] += across_in[g].astype(F32)
        rs_stage(g, 0, 0)

    def line_first(g):
        core_copy(g, 1).wait_recv()
        rows = pl.ds(short_at, half_rows - short_at)
        own[g, rows] += core_in[g, rows].astype(F32)
        rs_stage(g, 1, 0)

    def combine_across(g):
        combine(g, 0)
        mine = shard_at(0, place.spot)
        result[g, mine] = own[g, mine].astype(BF16)
        ag_stage(g, 0, 0)

    def combine_line(g):
        combine(g, 1)
        short_out[g] = own[g, shard_at(1, place.spot)].astype(BF16)
        short_copy(g).start()

    def short_done(g):
        short_copy(g).wait_recv()
        total = short_out[g].astype(F32) + short_in[g].astype(F32)
        result[g, shard_at(1, place.spot)] = total.astype(BF16)
        ag_stage(g, 1, 0)

    def back_done(g):
        rows = side_at(1 - place.side)
        back_copy(g, rows).wait_recv()
        hand_out(g, rows)

    chains = []
    for g in range(groups):
        middle_steps = [functools.partial(rs_stage, g, 0, s) for s in range(1, last)]
        later_steps = [functools.partial(ag_stage, g, 0, s) for s in range(1, line)]
        chains.append(
            [functools.partial(across_first, g), functools.partial(across_done, g)]
            + middle_steps
            + [functools.partial(combine_across, g)]
            + later_steps
            + [functools.partial(back_done, g)]
        )
        middle_steps = [functools.partial(rs_stage, g, 1, s) for s in range(1, last)]
        later_steps = [functools.partial(ag_stage, g, 1, s) for s in range(1, line)]
        chains.append(
            [functools.partial(line_first, g)]
            + middle_steps
            + [functools.partial(combine_line, g), functools.partial(short_done, g)]
            + later_steps
        )

    def advance(chain):
        if chain:
            chain.pop(0)()

    def small_copy(k):
        return remote(
            small_buf.at[0, k],
            small_buf.at[1, k],
            small_sem.at[0, k],
            small_sem.at[1, k],
            doubling[k],
        )

    def small_round(k):
        if k == 0:
            here = small.shape[1]
            small_buf[0, 0, 0:1, 0:here] = jnp.sum(small[...], axis=0, keepdims=True)
            small_buf[0, 0, 0:1, here:] = sums[0:1, :]
            small_copy(0).start()
            return
        small_copy(k - 1).wait()
        total = small_buf[0, k - 1] + small_buf[1, k - 1]
        if k < rounds:
            small_buf[0, k] = total
            small_copy(k).start()
        else:
            small_out[...] = total

    load(0, away)
    ones = turned.shape[1] - width
    for slot in range(2):
        turned[slot, width:] = jnp.ones((ones, turned.shape[2]), BF16)
    def tiles():
        for g in range(groups):
            for half in (away, core):
                if half is away:
                    load(g, core)
                    narrow_copy(g).wait()
                    turned[g % 2, :width] = narrow[g % 2].T
                elif g + 1 < groups:
                    load(g + 1, away)
                for t in range(2):
                    wide_copy(g, half, t).wait()
                    left = turned[(g if g < 3 or t == 1 else 2) % 2]
                    tile = dot(left, wide[g % 2, t, half])
                    if g in (1, 2) or (g == 3 and t == 0):
                        spot = half * width if g == 3 else (half * 2 + t) * width
                        spot = pl.multiple_of(sum_at[g] + spot, width)
                        sums[:, pl.ds(spot, width)] = tile[width : width + LANES]
                    tile = tile[:width]
                    if g == 0 or (g == 3 and t == 1):
                        tile = tile.T
                    rows = pl.ds(t * width, width)
                    if half is away:
                        leave[g, rows, :] = tile.astype(BF16)
                    else:
                        own[g, rows, :] = tile
                if half is away:
                    if g == 0:
                        pl.semaphore_wait(barrier, greeted)
                    for kind in range(2):
                        core_copy(g, kind).start()
                yield

    work = tiles()
    halves = 2 * groups
    small_at = 0
    for at, item in enumerate(sum_order(groups, [len(chain) for chain in chains])):
        if item < 0:
            next(work, None)
            halves -= 1
        else:
            advance(chains[item])
        if halves == 0 and at % 8 == 0 and small_at <= rounds:
            small_round(small_at)
            small_at += 1
    while small_at <= rounds:
        small_round(small_at)
        small_at += 1

    for g in range(groups):
        for kind in range(2):
            core_copy(g, kind).wait_send()
            for direction in range(2):

                def sent(kind=kind, direction=direction):
                    rows = side_at(0) if kind == 0 else pl.ds(short_at, half_rows - short_at)
                    remote(
                        result.at[g, rows],
                        result.at[g, rows],
                        line_send.at[g, kind, direction],
                        ag_recv.at[g, kind, direction, 0],
                        pair,
                    ).wait_send()

                pl.when(spots[direction] < last)(sent)
        across_copy(g).wait_send()
        short_copy(g).wait_send()
        back_copy(g, side_at(place.side)).wait_send()
        rows = pl.ds(0, half_rows)
        keep_copy(g, rows).wait()
        pair_copy(g, rows, away).wait_send()
        pair_copy(g, rows, away).wait_recv()


def unpack_kernel(
    perm_t,
    small_i,
    low_i,
    grad_i,
    down_i,
    up_i,
    gate_i,
    cand_i,
    out_i,
    block_out,
    grad_in,
    w_gate,
    w_cand,
    w_out,
    w_up,
    w_down,
    *vectors,
):
    at = 0
    for vector in vectors:
        n = vector.shape[1]
        vector[...] = small_i[:, at : at + n]
        at += n
    for source, target in (
        (down_i, w_down),
        (up_i, w_up),
        (gate_i, w_gate),
        (cand_i, w_cand),
        (out_i, w_out),
    ):
        target[0] = source[0].astype(F32)
    block_out[...] = dot(perm_t[...], low_i[0]).astype(BF16).reshape(block_out.shape)
    grad_in[...] = dot(perm_t[...], grad_i[0]).reshape(grad_in.shape)


def unpack(packed, small, low, grad, perm_t, rows, width, hidden, ff):
    packed = packed.reshape(4, ff, width)
    vectors = (width, width, width, width, ff, 2 * hidden, hidden)
    parts, chunk = low.shape[0], low.shape[1]
    chunks = parts // rows
    seq = chunks * chunk
    tall = ff // parts
    short = tall // 2
    spread = width // tall
    per_tile = width // short

    def column_block(t):
        return (0, t % spread, t // spread)

    return pl.pallas_call(
        unpack_kernel,
        grid=(parts,),
        out_shape=[
            jax.ShapeDtypeStruct((1, rows, seq, width), BF16),
            jax.ShapeDtypeStruct((1, rows, seq, width), F32),
            jax.ShapeDtypeStruct((1, width, 2 * hidden), F32),
            jax.ShapeDtypeStruct((1, width, hidden), F32),
            jax.ShapeDtypeStruct((1, hidden, width), F32),
            jax.ShapeDtypeStruct((1, width, ff), F32),
            jax.ShapeDtypeStruct((1, ff, width), F32),
        ]
        + [jax.ShapeDtypeStruct((1, n), F32) for n in vectors],
        in_specs=[
            whole(perm_t),
            whole(small),
            pl.BlockSpec((1, chunk, width), lambda t: (t, 0, 0)),
            pl.BlockSpec((1, chunk, width), lambda t: (t, 0, 0)),
            pl.BlockSpec((1, tall, width), lambda t: (0, t, 0)),
            pl.BlockSpec((1, tall, width), lambda t: (1, t, 0)),
            pl.BlockSpec((1, tall, width), lambda t: (2, t, 0)),
            pl.BlockSpec(
                (1, short, width),
                lambda t: (3, t // per_tile * 2 * per_tile + t % per_tile, 0),
            ),
            pl.BlockSpec(
                (1, short, width),
                lambda t: (3, t // per_tile * 2 * per_tile + per_tile + t % per_tile, 0),
            ),
        ],
        out_specs=[
            pl.BlockSpec((1, 1, chunk, width), lambda t: (0, t // chunks, t % chunks, 0)),
            pl.BlockSpec((1, 1, chunk, width), lambda t: (0, t // chunks, t % chunks, 0)),
            pl.BlockSpec((1, tall, width), column_block),
            pl.BlockSpec((1, short, width), lambda t: (0, t % per_tile, t // per_tile)),
            pl.BlockSpec((1, short, width), lambda t: (0, t, 0)),
            pl.BlockSpec((1, tall, width), column_block),
            pl.BlockSpec((1, tall, width), lambda t: (0, t, 0)),
        ]
        + [pl.BlockSpec((1, n), lambda t: (0, 0)) for n in vectors],
        compiler_params=pltpu.CompilerParams(vmem_limit_bytes=VMEM_LIMIT),
        name="unpack",
    )(perm_t, small, low, grad, packed, packed, packed, packed, packed)


def sum_gradients(operands, small, hidden, ff):
    place = Place()
    line = place.line
    rounds = len(place.doubling())
    operands = [a.reshape(-1, a.shape[-1]) for a in operands]
    tokens, width = operands[2].shape
    total = small.shape[1] + ff + 3 * hidden
    groups = 4
    half_rows = ff // 2
    side_rows = half_rows * 3 // 8
    shard = side_rows // line
    short = (half_rows - 2 * side_rows) // line
    anywhere = pl.BlockSpec(memory_space=pl.ANY)
    here = pl.BlockSpec(memory_space=pltpu.VMEM)
    packed, small_sum = pl.pallas_call(
        functools.partial(sum_kernel, line, rounds),
        out_shape=[
            jax.ShapeDtypeStruct((groups, 2, half_rows, width), BF16),
            jax.ShapeDtypeStruct((1, total), F32),
        ],
        in_specs=[anywhere] * 7 + [here],
        out_specs=[anywhere, here],
        scratch_shapes=[
            pltpu.VMEM((2, 2, 2, tokens, width), BF16),
            pltpu.VMEM((2, tokens, width), BF16),
            pltpu.VMEM((2, width + 2 * LANES, tokens), BF16),
            pltpu.VMEM((groups, half_rows, width), F32),
            pltpu.VMEM((groups, half_rows, width), BF16),
            pltpu.VMEM((groups, half_rows, width), BF16),
            pltpu.VMEM((groups, side_rows, width), BF16),
            pltpu.VMEM((groups, side_rows, width), BF16),
            pltpu.VMEM((groups, short, width), BF16),
            pltpu.VMEM((groups, short, width), BF16),
            pltpu.VMEM((groups, 2, 2, line - 1, max(shard, short), width), BF16),
            pltpu.VMEM((groups, half_rows, width), BF16),
            pltpu.VMEM((2, rounds, 1, total), F32),
            pltpu.VMEM((LANES, ff + 3 * hidden), F32),
            pltpu.SemaphoreType.DMA((2, 2, 2)),
            pltpu.SemaphoreType.DMA((2,)),
            pltpu.SemaphoreType.DMA((2, groups, 2)),
            pltpu.SemaphoreType.DMA((2, groups)),
            pltpu.SemaphoreType.DMA((2, groups)),
            pltpu.SemaphoreType.DMA((2, groups)),
            pltpu.SemaphoreType.DMA((groups, 2, 2)),
            pltpu.SemaphoreType.DMA((groups, 2, 2, line - 1)),
            pltpu.SemaphoreType.DMA((groups, 2, 2, line - 1)),
            pltpu.SemaphoreType.DMA((groups,)),
            pltpu.SemaphoreType.DMA((2, groups)),
            pltpu.SemaphoreType.DMA((2, rounds)),
        ],
        compiler_params=pltpu.CompilerParams(
            collective_id=2, has_side_effects=True, vmem_limit_bytes=VMEM_LIMIT
        ),
        name="sum_gradients",
    )(*operands, small)
    dp_size = lax.axis_size("dp")
    inner = 2 * line
    if dp_size > inner:
        members = [list(range(i, dp_size, inner)) for i in range(inner)]
        packed, small_sum = lax.psum((packed, small_sum), "dp", axis_index_groups=members)
    return packed, small_sum


def body(tokens, resets, cotangent, *stacked):
    rows, _, width = tokens.shape
    hidden = stacked[3].shape[2]
    ff = stacked[8].shape[2]
    low, grad_in, perm_t, (*operands, small) = local_grads(tokens, resets, cotangent, stacked)
    packed, small_sum = sum_gradients(operands, small, hidden, ff)
    block_out, grad_in, w_gate, w_cand, w_out, w_up, w_down, *vectors = unpack(
        packed, small_sum, low, grad_in, perm_t, rows, width, hidden, ff
    )
    g_one, b_out, g_two, b_down, b_up, b_gate, b_cand = vectors
    grads = (g_one, w_gate, b_gate, w_cand, b_cand, w_out, b_out, g_two, w_up, b_up, w_down, b_down)
    return (block_out, grad_in) + grads


def solution(mesh):
    vector = P("section", None)
    matrix = P("section", None, None)
    weight_specs = (
        vector,
        matrix,
        vector,
        matrix,
        vector,
        matrix,
        vector,
        vector,
        matrix,
        vector,
        matrix,
        vector,
    )
    tokens = P(("dp", "rep"), None, None)
    by_rows = P("section", ("dp", "rep"), None, None)
    return jax.shard_map(
        body,
        mesh=mesh,
        in_specs=(tokens, P(("dp", "rep"), None), tokens) + weight_specs,
        out_specs=(by_rows, by_rows) + weight_specs,
        check_vma=False,
    )
```

```python
import functools
import math

import jax
import jax.numpy as jnp
import numpy as np
from jax import lax
from jax.experimental import pallas as pl
from jax.experimental.pallas import tpu as pltpu
from jax.sharding import PartitionSpec as P

EPS = 1e-06
F32 = jnp.float32
BF16 = jnp.bfloat16
CHUNK = 256
LANES = 8
WIDTH = 256
GELU_A = math.sqrt(2.0 / math.pi)
GELU_B = 0.044715
LN4 = math.log(4.0)
EXP_TOP = 85.6
VMEM_LIMIT = 60 * 1024 * 1024
BLOCKS_VMEM = 63 * 1024 * 1024
UNPACK_VMEM = 40 * 1024 * 1024
SUM_VMEM = 53 * 1024 * 1024


def dot(a, b):
    return jnp.dot(a, b, preferred_element_type=F32)


def dot_nt(a, b):
    return lax.dot_general(a, b, (((1,), (1,)), ((), ())), preferred_element_type=F32)


def inv_scale(values):
    return lax.rsqrt(jnp.mean(values * values, axis=-1, keepdims=True) + EPS)


def partner_barrier_signal(partner):
    pl.semaphore_signal(
        pltpu.get_barrier_semaphore(),
        inc=1,
        device_id={"section": partner},
        device_id_type=pl.DeviceIdType.MESH,
    )


def interleave(*streams):
    live = list(streams)
    while live:
        for stream in list(live):
            if next(stream, live) is live:
                live.remove(stream)


def scan_segments(product, accum, carry, reverse):
    which = lax.broadcasted_iota(jnp.int32, product.shape, 0)
    span = 1
    while span < LANES:
        turn = LANES - span if reverse else span
        inside = which < LANES - span if reverse else which >= span
        accum = jnp.where(inside, product * pltpu.roll(accum, turn, 0) + accum, accum)
        product = jnp.where(inside, product * pltpu.roll(product, turn, 0), product)
        span *= 2
    reached = product * carry + accum
    edge = LANES - 1 if reverse else 0
    incoming = jnp.where(which == edge, carry, pltpu.roll(reached, LANES - 1 if reverse else 1, 0))
    end = 0 if reverse else LANES - 1
    return incoming, jnp.broadcast_to(reached[end : end + 1], reached.shape)


class Step:
    @staticmethod
    def count(rows, chunks):
        return 4 * chunks + (2 * rows - 2) * (chunks + 1)

    def __init__(self, step, rows, chunks):
        first = lax.axis_index("section") == 0
        apart = 2 * chunks
        joint = chunks + 1
        opening = step < apart
        middle = step - apart
        length = jnp.where(first, (2 * rows - 2) * joint, (rows - 1) * (apart + 1))
        closing = middle >= length
        at = jnp.where(opening, step, middle - length)
        alone = opening | closing
        begins, ends = at % 2 == 0, at % 2 == 1
        phase, along = 1 + middle // joint, middle % joint
        pair, within = middle // (apart + 1), middle % (apart + 1)
        moving = jnp.logical_not(alone)
        ahead = moving & first & (phase < rows)
        back = moving & first & (phase >= rows)
        turn = moving & jnp.logical_not(first)
        last_steps = closing & (at < apart)
        self.f_begins = (opening & begins) | (ahead & (along < chunks)) | (
            turn & (within >= chunks) & (within < apart)
        )
        self.f_ends = (opening & ends) | (ahead & (along > 0)) | (turn & (within > chunks))
        self.b_begins = (last_steps & begins) | (back & (along < chunks)) | (turn & (within < chunks))
        self.b_ends = (last_steps & ends) | (back & (along > 0)) | (
            turn & (within > 0) & (within <= chunks)
        )
        f_row = jnp.where(opening, 0, jnp.where(first, phase, pair + 1))
        b_row = jnp.where(closing, rows - 1, jnp.where(first, phase - rows, pair))
        f_along = jnp.where(first, along, within - chunks)
        b_along = jnp.where(first, along, within)
        last = chunks - 1
        total = rows * chunks

        def chunk(row, k):
            return jnp.clip(row * chunks + k, 0, total - 1)

        half = at // 2
        self.mixer = chunk(f_row, jnp.where(alone, half, f_along))
        self.feed = chunk(f_row, jnp.where(alone, half, f_along - 1))
        b_early = jnp.where(alone, half, b_along)
        self.back_feed = chunk(b_row, last - b_early)
        self.back_mixer = chunk(b_row, last - jnp.where(alone, half, b_along - 1))
        self.f_starts = self.f_begins & (self.mixer % chunks == 0)
        self.b_starts = self.b_begins & (self.back_feed % chunks == last)
        self.next_mixer = jnp.minimum(self.mixer + 1, total - 1)
        later = chunk(b_row, b_early + 1)
        self.next_back = later // chunks * chunks + last - later % chunks
        self.b_early = b_row * chunks + b_early
        self.b_late = b_row * chunks + jnp.where(alone, half, b_along - 1)


def blocks_kernel(
    rows,
    chunks,
    tok,
    cot,
    w_gate_all,
    w_cand_all,
    w_out_all,
    w_up_all,
    w_down_all,
    keep_rows,
    perm,
    g_one,
    b_gate,
    b_cand,
    b_out,
    g_two,
    b_up,
    b_down,
    operands_all,
    active_all,
    low_all,
    down_all,
    up_all,
    mix_all,
    gate_all,
    cand_all,
    grad_all,
    small_o,
    raw,
    keep,
    w_gate,
    w_cand,
    w_out,
    w_up,
    w_down,
    operands_o,
    active_o,
    low_o,
    down_o,
    up_o,
    mix_o,
    gate_o,
    cand_o,
    grad_o,
    ratio_s,
    slopes_s,
    middle_s,
    slope_up_s,
    inputs,
    send,
    received,
    coming,
    coming_back,
    carry,
    carry_back,
    normed_two_s,
    grad_middle_s,
    mix_s,
    load_sem,
    stage_sem,
    send_sem,
    input_sem,
    back_send_sem,
    received_sem,
):
    section = lax.axis_index("section")
    partner = 1 - section
    chunk, width = coming.shape
    hidden = w_cand.shape[1]
    ff = w_up.shape[1]
    span = chunk // LANES
    total = rows * chunks
    steps = Step.count(rows, chunks)
    stages = (
        (operands_o, operands_all),
        (active_o, active_all),
        (low_o, low_all),
        (down_o, down_all),
        (up_o, up_all),
        (mix_o, mix_all),
        (gate_o, gate_all),
        (cand_o, cand_all),
        (grad_o, grad_all),
    )

    def stage_copy(which, at_chunk):
        source, target = stages[which]
        slot = at_chunk % 2
        return pltpu.make_async_copy(
            source.at[slot], target.at[at_chunk], stage_sem.at[which, slot]
        )

    def load_copy(which):
        pairs = (
            (w_gate_all, w_gate),
            (w_cand_all, w_cand),
            (w_out_all, w_out),
            (w_up_all, w_up),
            (w_down_all, w_down),
        )
        return pltpu.make_async_copy(*pairs[which], load_sem.at[which])

    def raw_copy(source, row):
        return pltpu.make_async_copy(source.at[row], raw.at[row], load_sem.at[5 + row])

    def raw_chunk(at_chunk):
        start = pl.multiple_of(at_chunk % chunks * chunk, chunk)
        return raw[at_chunk // chunks, pl.ds(start, chunk)]

    def chunk_copy(slot):
        return remote(
            send.at[slot],
            inputs.at[slot],
            send_sem.at[slot],
            input_sem.at[slot],
            {"section": partner},
        )

    def back_copy(slot):
        return remote(
            send.at[slot],
            received.at[slot],
            back_send_sem.at[slot],
            received_sem.at[slot],
            {"section": partner},
        )

    def add_small(which, values):
        part = jnp.sum(values.reshape(-1, LANES, width), axis=0)
        small_o[:, which * width : (which + 1) * width] += part

    def blocks_step(c):
        step = Step(c, rows, chunks)

        @pl.when(c == 1)
        def _():
            load_copy(3).wait()
            load_copy(4).wait()
            for row in range(1, rows):
                raw_copy(tok, row).wait()

        has_f = step.f_begins | step.f_ends
        has_b = step.b_begins | step.b_ends

        @pl.when(has_f)
        def _():
            @pl.when(step.f_begins)
            def _():
                @pl.when(step.f_starts)
                def _():
                    carry[...] = jnp.zeros_like(carry)

                @pl.when(section == 0)
                def _():
                    inputs[step.mixer] = coming[...]

                @pl.when(section == 1)
                def _():
                    chunk_copy(step.mixer).wait_recv()

                @pl.when(step.mixer >= 2)
                def _():
                    stage_copy(0, step.mixer).wait()

            @pl.when(step.f_ends & (step.feed >= 2))
            def _():
                for which in (1, 2):
                    stage_copy(which, step.feed).wait()

        @pl.when(has_b)
        def _():
            @pl.when(step.b_begins)
            def _():
                @pl.when(step.b_starts)
                def _():
                    carry_back[...] = jnp.zeros_like(carry_back)

                @pl.when(section == 0)
                def _():
                    back_copy(step.back_feed).wait_recv()
                    coming_back[...] = received[step.back_feed]

                @pl.when(step.b_early >= 2)
                def _():
                    for which in (3, 4, 5):
                        stage_copy(which, step.back_feed).wait()

            @pl.when(step.b_ends & (step.b_late >= 2))
            def _():
                for which in (6, 7, 8):
                    stage_copy(which, step.back_mixer).wait()

        def mixer():
            at_chunk = step.mixer
            slot = at_chunk % 2
            x = inputs[at_chunk].astype(F32)
            normed = (x * inv_scale(x) * g_one[...]).astype(BF16)
            operands_o[slot, :, :width] = normed
            yield
            for at in range(0, hidden, WIDTH):
                cols = slice(at, at + WIDTH)
                cols_in = slice(hidden + at, hidden + at + WIDTH)
                pre_f = dot(normed, w_gate[:, cols])
                pre_i = dot(normed, w_gate[:, cols_in])
                cand = dot(normed, w_cand[:, cols]) + b_cand[:, cols]
                u = jnp.exp(jnp.minimum((-LN4 - b_gate[:, cols]) - pre_f, EXP_TOP))
                v = jnp.exp(jnp.minimum((-LN4 - b_gate[:, cols_in]) - pre_i, EXP_TOP))
                d = 1.0 / (0.5 + u + v)
                ratio_f = (0.25 + v) * d
                ratio_i = (0.25 + u) * d
                ratio_s[at_chunk, :, cols] = ratio_f
                keep_w = jnp.concatenate([keep[at_chunk]] * (WIDTH // 128), axis=1)
                decay = ratio_f * keep_w
                drive = ratio_i * cand
                product = decay[0:LANES]
                accum = drive[0:LANES]
                for j in range(1, span):
                    r = slice(j * LANES, (j + 1) * LANES)
                    accum = decay[r] * accum + drive[r]
                    product = decay[r] * product
                state, carry[:, cols] = scan_segments(product, accum, carry[:, cols], False)
                before = []
                after = []
                for j in range(span):
                    r = slice(j * LANES, (j + 1) * LANES)
                    before.append(state)
                    state = decay[r] * state + drive[r]
                    after.append(state)
                operands_o[slot, :, width + at : width + at + WIDTH] = jnp.concatenate(
                    after, axis=0
                ).astype(BF16)
                lever = keep_w * jnp.concatenate(before, axis=0) - cand
                slopes_s[at_chunk, :, cols] = (lever * ((u * d) * ratio_f)).astype(BF16)
                slopes_s[at_chunk, :, cols_in] = (-lever * ((v * d) * ratio_i)).astype(BF16)
                yield
            mixed = dot(operands_o[slot, :, width : width + hidden], w_out[...])
            yield
            middle = x + (mixed + b_out[...])
            normed_two = (middle * inv_scale(middle) * g_two[...]).astype(BF16)
            operands_o[slot, :, width + hidden :] = normed_two
            yield
            middle_s[at_chunk] = middle
            normed_two_s[...] = normed_two

        def feed():
            at_chunk = step.feed
            slot = at_chunk % 2
            for at in range(0, ff, WIDTH):
                cols = slice(at, at + WIDTH)
                up = dot(normed_two_s[...], w_up[:, cols]) + b_up[:, cols]
                square = up * up
                half = 0.5 + 0.5 * jnp.tanh(up * (GELU_A + (GELU_A * GELU_B) * square))
                act = up * half
                active_o[slot, :, cols] = act.astype(BF16)
                slope = half + act * (1.0 - half) * (2 * GELU_A + (6 * GELU_A * GELU_B) * square)
                slope_up_s[at_chunk, :, cols] = slope.astype(BF16)
                if at % (2 * WIDTH):
                    yield
            down = dot(active_o[slot], w_down[...])
            yield
            low_o[slot] = (middle_s[at_chunk] + (down + b_down[...])).astype(BF16)

        def reorder():
            yield
            yield
            coming[...] = dot(perm[...], raw_chunk(step.next_mixer)).astype(BF16)

        def back_feed():
            at_chunk = step.back_feed
            slot = at_chunk % 2
            grad_down = coming_back[...]
            down_o[slot] = grad_down
            yield
            for at in range(0, ff, WIDTH):
                cols = slice(at, at + WIDTH)
                grad_active = dot_nt(grad_down, w_down[cols, :])
                slope = slope_up_s[at_chunk, :, cols].astype(F32)
                up_o[slot, :, cols] = (grad_active * slope).astype(BF16)
                if at % (2 * WIDTH):
                    yield
            q = dot_nt(up_o[slot], w_up[...])
            yield
            dy = grad_down.astype(F32)
            add_small(3, dy)
            middle = middle_s[at_chunk]
            r = inv_scale(middle)
            scaled = middle * r
            add_small(2, q * scaled)
            weighted = q * g_two[...]
            grad_middle = dy + r * (
                weighted - scaled * jnp.mean(weighted * scaled, axis=-1, keepdims=True)
            )
            add_small(1, grad_middle)
            grad_mix = grad_middle.astype(BF16)
            mix_o[slot] = grad_mix
            yield
            yield
            grad_middle_s[...] = grad_middle
            mix_s[...] = grad_mix

        def back_mixer():
            at_chunk = step.back_mixer
            slot = at_chunk % 2
            for at in range(0, hidden, WIDTH):
                cols = slice(at, at + WIDTH)
                cols_in = slice(hidden + at, hidden + at + WIDTH)
                grad_state = dot_nt(mix_s[...], w_out[cols, :])
                ratio_f = ratio_s[at_chunk, :, cols]
                decay = ratio_f * jnp.concatenate([keep[at_chunk]] * (WIDTH // 128), axis=1)
                last = slice((span - 1) * LANES, span * LANES)
                product = decay[last]
                accum = decay[last] * grad_state[last]
                for j in range(span - 2, -1, -1):
                    rj = slice(j * LANES, (j + 1) * LANES)
                    accum = decay[rj] * (grad_state[rj] + accum)
                    product = decay[rj] * product
                later, carry_back[:, cols] = scan_segments(product, accum, carry_back[:, cols], True)
                parts = [None] * span
                for j in range(span - 1, -1, -1):
                    rj = slice(j * LANES, (j + 1) * LANES)
                    carried = grad_state[rj] + later
                    parts[j] = carried
                    later = decay[rj] * carried
                carried = jnp.concatenate(parts, axis=0)
                gate_o[slot, :, cols] = (carried * slopes_s[at_chunk, :, cols].astype(F32)).astype(BF16)
                gate_o[slot, :, cols_in] = (
                    carried * slopes_s[at_chunk, :, cols_in].astype(F32)
                ).astype(BF16)
                cand_o[slot, :, cols] = (carried * (1.0 - ratio_f)).astype(BF16)
                yield
            p = dot_nt(gate_o[slot], w_gate[...]) + dot_nt(cand_o[slot], w_cand[...])
            yield
            x = inputs[at_chunk].astype(F32)
            r = inv_scale(x)
            scaled = x * r
            add_small(0, p * scaled)
            weighted = p * g_one[...]
            grad_input = grad_middle_s[...] + r * (
                weighted - scaled * jnp.mean(weighted * scaled, axis=-1, keepdims=True)
            )
            grad_o[slot] = grad_input.astype(BF16)

        def back_reorder():
            yield
            yield
            coming_back[...] = dot(perm[...], raw_chunk(step.next_back)).astype(BF16)

        no_f_begins = jnp.logical_not(step.f_begins)
        no_f_ends = jnp.logical_not(step.f_ends)
        no_b_begins = jnp.logical_not(step.b_begins)
        no_b_ends = jnp.logical_not(step.b_ends)

        @pl.when(has_f)
        def _():
            @pl.when(step.f_begins & no_f_ends & no_b_ends)
            def _():
                interleave(mixer(), reorder())

            @pl.when(step.f_begins & step.f_ends)
            def _():
                interleave(mixer(), feed(), reorder())

            @pl.when(no_f_begins)
            def _():
                interleave(feed())

            @pl.when(step.f_begins & step.b_ends)
            def _():
                interleave(back_mixer(), mixer())

        @pl.when(has_b & jnp.logical_not(has_f))
        def _():
            @pl.when(no_b_ends)
            def _():
                interleave(back_feed(), back_reorder())

            @pl.when(step.b_begins & step.b_ends)
            def _():
                interleave(back_feed(), back_mixer(), back_reorder())

            @pl.when(no_b_begins)
            def _():
                interleave(back_mixer())

        @pl.when(has_f)
        def _():
            @pl.when(step.f_ends & (section == 0))
            def _():
                send[step.feed] = low_o[step.feed % 2]
                chunk_copy(step.feed).start()

            @pl.when(step.f_begins)
            def _():
                stage_copy(0, step.mixer).start()

            @pl.when(step.f_ends)
            def _():
                for which in (1, 2):
                    stage_copy(which, step.feed).start()

        @pl.when(has_b)
        def _():
            @pl.when(step.b_ends & (section == 1))
            def _():
                send[step.back_mixer] = grad_o[step.back_mixer % 2]
                back_copy(step.back_mixer).start()

            @pl.when(step.b_begins)
            def _():
                for which in (3, 4, 5):
                    stage_copy(which, step.back_feed).start()

            @pl.when(step.b_ends)
            def _():
                for which in (6, 7, 8):
                    stage_copy(which, step.back_mixer).start()

    partner_barrier_signal(partner)
    pl.when(section == 0)(lambda: raw_copy(tok, 0).start())
    pl.when(section == 1)(lambda: raw_copy(cot, 0).start())
    for which in range(3):
        load_copy(which).start()
    small_o[...] = jnp.zeros_like(small_o)
    for at_chunk in range(total):
        row = keep_rows[at_chunk : at_chunk + 1, :]
        keep[at_chunk] = jnp.broadcast_to(row, (128, chunk)).T
    raw_copy(tok, 0).wait()
    coming[...] = dot(perm[...], raw_chunk(0)).astype(BF16)
    coming_back[...] = dot(perm[...], raw_chunk(chunks - 1)).astype(BF16)
    for which in range(3):
        load_copy(which).wait()
    for which in range(3, 5):
        load_copy(which).start()
    for row in range(1, rows):
        pl.when(section == 0)(functools.partial(lambda row: raw_copy(tok, row).start(), row))
        pl.when(section == 1)(functools.partial(lambda row: raw_copy(cot, row).start(), row))
    pl.semaphore_wait(pltpu.get_barrier_semaphore(), 1)

    @pl.loop(0, steps)
    def _(c):
        blocks_step(c)

    @pl.when(section == 0)
    def _():
        for slot in range(total):
            chunk_copy(slot).wait_send()

    @pl.when(section == 1)
    def _():
        for slot in range(total):
            back_copy(slot).wait_send()

    for which in range(len(stages)):
        for slot in range(2):
            stage_copy(which, slot).wait()


def run_blocks(tokens, cotangent, keep, perm, weights, chunk):
    rows, seq, width = tokens.shape
    chunks = seq // chunk
    total = rows * chunks
    g_one, w_gate, b_gate, w_cand, b_cand, w_out, b_out, g_two, w_up, b_up, w_down, b_down = weights
    hidden = w_cand.shape[1]
    ff = w_up.shape[1]
    large = (w_gate, w_cand, w_out, w_up, w_down)
    little = (keep, perm, g_one, b_gate, b_cand, b_out, g_two, b_up, b_down)
    columns = (2 * width + hidden, ff, width, width, ff, width, 2 * hidden, hidden, width)
    anywhere = pl.BlockSpec(memory_space=pl.ANY)
    here = pl.BlockSpec(memory_space=pltpu.VMEM)
    return pl.pallas_call(
        functools.partial(blocks_kernel, rows, chunks),
        out_shape=[jax.ShapeDtypeStruct((total, chunk, n), BF16) for n in columns]
        + [jax.ShapeDtypeStruct((LANES, 4 * width), F32)],
        in_specs=[anywhere] * 7 + [here] * len(little),
        out_specs=[anywhere] * len(columns) + [here],
        scratch_shapes=[
            pltpu.VMEM(tokens.shape, BF16),
            pltpu.VMEM((total, chunk, 128), F32),
        ]
        + [pltpu.VMEM(w.shape, BF16) for w in large]
        + [pltpu.VMEM((2, chunk, n), BF16) for n in columns]
        + [
            pltpu.VMEM((total, chunk, hidden), F32),
            pltpu.VMEM((total, chunk, 2 * hidden), BF16),
            pltpu.VMEM((total, chunk, width), F32),
            pltpu.VMEM((total, chunk, ff), BF16),
            pltpu.VMEM((total, chunk, width), BF16),
            pltpu.VMEM((total, chunk, width), BF16),
            pltpu.VMEM((total, chunk, width), BF16),
            pltpu.VMEM((chunk, width), BF16),
            pltpu.VMEM((chunk, width), BF16),
            pltpu.VMEM((LANES, hidden), F32),
            pltpu.VMEM((LANES, hidden), F32),
            pltpu.VMEM((chunk, width), BF16),
            pltpu.VMEM((chunk, width), F32),
            pltpu.VMEM((chunk, width), BF16),
            pltpu.SemaphoreType.DMA((5 + rows,)),
            pltpu.SemaphoreType.DMA((len(columns), 2)),
            pltpu.SemaphoreType.DMA((total,)),
            pltpu.SemaphoreType.DMA((total,)),
            pltpu.SemaphoreType.DMA((total,)),
            pltpu.SemaphoreType.DMA((total,)),
        ],
        compiler_params=pltpu.CompilerParams(
            collective_id=0, has_side_effects=True, vmem_limit_bytes=BLOCKS_VMEM
        ),
        name="blocks",
    )(tokens, cotangent, *large, *little)


def local_grads(tokens, resets, cotangent, stacked):
    weights = tuple(w if w.ndim == 2 else w[0] for w in stacked)
    rows, seq, width = tokens.shape
    chunk = min(CHUNK, seq)
    total = rows * (seq // chunk)
    span = chunk // LANES
    keep = (1 - resets).astype(F32).reshape(total, LANES, span)
    keep = keep.transpose(0, 2, 1).reshape(total, chunk)
    at = np.arange(chunk)
    source = (at % LANES) * span + at // LANES
    perm_t = np.equal(at[:, None], source[None, :])
    perm = jnp.asarray(perm_t.T, BF16)
    perm_t = jnp.asarray(perm_t, BF16)
    operands, active, low, *grads, grad_in, small = run_blocks(
        tokens, cotangent, keep, perm, weights, chunk
    )
    return low, grad_in, perm_t, (operands, active, *grads, small)


class Place:
    def __init__(self):
        dp_size = lax.axis_size("dp")
        chips = dp_size // 2
        self.line = 4 if chips % 4 == 0 else chips
        dp = lax.axis_index("dp")
        self.side = lax.axis_index("rep")
        self.core = dp % 2
        self.base = (dp // 2) // self.line * self.line
        self.spot = (dp // 2) % self.line

    def along(self, step):
        return {"dp": (self.base + self.spot + step) * 2 + self.core}

    def across(self):
        return {"rep": 1 - self.side}

    def other_core(self):
        return {"dp": (self.base + self.spot) * 2 + 1 - self.core}

    def doubling(self):
        found = [self.other_core()]
        span = 1
        while span < self.line:
            found.append(self.along(span - 2 * span * ((self.spot // span) % 2)))
            span *= 2
        return found + [self.across()]


def remote(src, dst, send_sem, recv_sem, device):
    return pltpu.make_async_remote_copy(
        src_ref=src,
        dst_ref=dst,
        send_sem=send_sem,
        recv_sem=recv_sem,
        device_id=device,
        device_id_type=pl.DeviceIdType.MESH,
    )


SUM_ORDER = (
    -1, -1, 0, 1, -1, 1, -1, 1, 2, 3, -1, 3, 0, -1, 5, 3, 1, 0, -1, 5, 3, 2, 4, 1, 0, -1, 2,
    5, 7, 1, 6, 0, 2, 1, 3, 0, 2, 3, 4, 0, 7, 6, 2, 3, 4, 6, 2, 7, 4, 5, 3, 0, 6, 4, 6, 5, 7,
    0, 2, 4, 6, 7, 4, 6, 4, 5, 1, 7, 6, 5, 7, 4, 2, 5, 6, 7,
)


def sum_order(groups, lengths):
    if all(SUM_ORDER.count(c) == n for c, n in enumerate(lengths)):
        return SUM_ORDER
    order = []
    left = list(lengths)
    for g in range(groups):
        for _ in range(2):
            order.append(-1)
            for c in range(2 * g):
                if left[c]:
                    order.append(c)
                    left[c] -= 1
    while any(left):
        for c, n in enumerate(left):
            if n:
                order.append(c)
                left[c] -= 1
    return order


def sum_kernel(
    line,
    rounds,
    operands,
    feed,
    down,
    up,
    mix,
    gate,
    cand,
    small,
    out,
    small_out,
    wide,
    narrow,
    turned,
    own,
    leave,
    core_in,
    across_out,
    across_in,
    short_out,
    short_in,
    partial,
    small_buf,
    sums,
    wide_sem,
    narrow_sem,
    core_sem,
    across_sem,
    back_sem,
    short_sem,
    line_send,
    rs_recv,
    ag_recv,
    pair_sem,
    small_sem,
):
    place = Place()
    width = down.shape[1]
    groups = out.shape[0]
    half_rows = out.shape[2]
    last = line - 1
    side_rows = across_out.shape[1]
    shard_rows = (side_rows // line, short_out.shape[1])
    short_at = 2 * side_rows
    core = place.core
    away = 1 - core
    pair = place.other_core()
    opposite = place.across()
    neighbours = (place.along(1), place.along(-1))
    spots = (place.spot, last - place.spot)
    doubling = place.doubling()

    barrier = pltpu.get_barrier_semaphore()

    def greet(peer):
        pl.semaphore_signal(
            barrier, inc=1, device_id=peer, device_id_type=pl.DeviceIdType.MESH
        )

    for peer in doubling:
        greet(peer)
    for direction in range(2):
        pl.when(spots[direction] < last)(functools.partial(greet, neighbours[direction]))
    greeted = len(doubling) + jnp.where(spots[0] < last, 1, 0) + jnp.where(spots[1] < last, 1, 0)

    hidden = cand.shape[1]
    ff = up.shape[1]
    normed_two = operands.at[:, pl.ds(width + hidden, width)]
    normed = operands.at[:, pl.ds(0, width)]
    sources = [(feed, down), (up, normed_two), (gate, normed), (None, mix)]
    sum_at = [None, 0, ff, ff + 2 * hidden]

    def wide_copy(g, half, t):
        slot = g % 2
        to = wide.at[slot, t, half]
        if g < 3:
            cols = pl.ds(pl.multiple_of((half * 2 + t) * width, width), width)
            src = sources[g][0].at[:, cols]
        elif t == 0:
            cols = pl.ds(pl.multiple_of(half * width, width), width)
            src = cand.at[:, cols]
        else:
            cols = pl.ds(pl.multiple_of(width + half * width, width), width)
            src = operands.at[:, cols]
        return pltpu.make_async_copy(src, to, wide_sem.at[slot, t, half])

    def narrow_copy(g):
        return pltpu.make_async_copy(
            sources[g][1], narrow.at[g % 2], narrow_sem.at[g % 2]
        )

    def load(g, half):
        if half is away:
            narrow_copy(g).start()
        for t in range(2):
            wide_copy(g, half, t).start()

    def side_at(side):
        return pl.ds(pl.multiple_of(side * side_rows, side_rows), side_rows)

    def shard_at(kind, shard):
        n = shard_rows[kind]
        start = place.side * side_rows if kind == 0 else short_at
        return pl.ds(pl.multiple_of(start + shard * n, 16), n)

    def core_copy(g, kind):
        rows = pl.ds(0, short_at) if kind == 0 else pl.ds(short_at, half_rows - short_at)
        return remote(
            leave.at[g, rows],
            core_in.at[g, rows],
            core_sem.at[0, g, kind],
            core_sem.at[1, g, kind],
            pair,
        )

    def rs_copy(g, kind, direction, source, s):
        rows = pl.ds(0, shard_rows[kind])
        return remote(
            partial.at[g, kind, direction, source, rows],
            partial.at[g, kind, direction, s, rows],
            line_send.at[g, kind, direction],
            rs_recv.at[g, kind, direction, s],
            neighbours[direction],
        )

    def ag_copy(g, kind, direction, shard, s):
        rows = shard_at(kind, shard)
        return remote(
            out.at[g, core, rows],
            out.at[g, core, rows],
            line_send.at[g, kind, direction],
            ag_recv.at[g, kind, direction, s],
            neighbours[direction],
        )

    def across_copy(g):
        return remote(
            across_out.at[g], across_in.at[g], across_sem.at[0, g], across_sem.at[1, g], opposite
        )

    def short_copy(g):
        return remote(
            short_out.at[g], short_in.at[g], short_sem.at[0, g], short_sem.at[1, g], opposite
        )

    def back_copy(g, rows):
        return remote(
            out.at[g, core, rows], out.at[g, core, rows], back_sem.at[0, g], back_sem.at[1, g], opposite
        )

    def pair_copy(g, rows, to):
        return remote(
            out.at[g, core, rows], out.at[g, to, rows], pair_sem.at[0, g], pair_sem.at[1, g], pair
        )

    def hand_out(g, rows):
        pair_copy(g, rows, core).start()

    def shard_of(direction, steps):
        return steps if direction == 0 else last - steps

    def rs_stage(g, kind, s):
        rows = pl.ds(0, shard_rows[kind])
        for direction in range(2):
            spot = spots[direction]
            mine = shard_at(kind, shard_of(direction, spot + last - s))

            def begin(direction=direction):
                first = shard_at(kind, shard_of(direction, last - s))
                partial[g, kind, direction, s, rows] = own[g, first].astype(BF16)
                rs_copy(g, kind, direction, s, s).start()

            def go_on(direction=direction, mine=mine):
                rs_copy(g, kind, direction, s - 1, s - 1).wait_recv()
                total = own[g, mine] + partial[g, kind, direction, s - 1, rows].astype(F32)
                partial[g, kind, direction, s - 1, rows] = total.astype(BF16)
                rs_copy(g, kind, direction, s - 1, s).start()

            pl.when(spot == 0)(begin)
            if s > 0:
                pl.when((spot > 0) & (spot <= s))(go_on)

    def combine(g, kind):
        rows = pl.ds(0, shard_rows[kind])
        mine = shard_at(kind, place.spot)
        for direction in range(2):

            def add(direction=direction):
                rs_copy(g, kind, direction, last - 1, last - 1).wait_recv()
                own[g, mine] += partial[g, kind, direction, last - 1, rows].astype(F32)

            pl.when(spots[direction] > 0)(add)

    def finished(g, kind, shard):
        rows = shard_at(kind, shard)
        hand_out(g, rows)
        if kind == 0:
            back_copy(g, rows).start()

    def ag_stage(g, kind, s):
        for direction in range(2):
            spot = spots[direction]
            shard = shard_of(direction, spot - s)

            def send(direction=direction, shard=shard):
                ag_copy(g, kind, direction, shard, s).start()

            def receive(direction=direction, shard=shard, send=send, spot=spot):
                ag_copy(g, kind, direction, shard, s - 1).wait_recv()
                if s < last:
                    pl.when(spot < last)(send)
                finished(g, kind, shard)

            if s == 0:
                pl.when(spot < last)(send)
            else:
                pl.when(spot >= s)(receive)
        if s == 0:
            finished(g, kind, place.spot)

    def across_first(g):
        core_copy(g, 0).wait_recv()
        theirs = side_at(1 - place.side)
        ours = side_at(place.side)
        across_out[g] = (own[g, theirs] + core_in[g, theirs].astype(F32)).astype(BF16)
        across_copy(g).start()
        own[g, ours] += core_in[g, ours].astype(F32)

    def across_done(g):
        across_copy(g).wait_recv()
        ours = side_at(place.side)
        own[g, ours] += across_in[g].astype(F32)
        rs_stage(g, 0, 0)

    def line_first(g):
        core_copy(g, 1).wait_recv()
        rows = pl.ds(short_at, half_rows - short_at)
        own[g, rows] += core_in[g, rows].astype(F32)
        rs_stage(g, 1, 0)

    def combine_across(g):
        combine(g, 0)
        mine = shard_at(0, place.spot)
        out[g, core, mine] = own[g, mine].astype(BF16)
        ag_stage(g, 0, 0)

    def combine_line(g):
        combine(g, 1)
        short_out[g] = own[g, shard_at(1, place.spot)].astype(BF16)
        short_copy(g).start()

    def short_done(g):
        short_copy(g).wait_recv()
        total = short_out[g].astype(F32) + short_in[g].astype(F32)
        out[g, core, shard_at(1, place.spot)] = total.astype(BF16)
        ag_stage(g, 1, 0)

    def back_done(g):
        rows = side_at(1 - place.side)
        back_copy(g, rows).wait_recv()
        hand_out(g, rows)

    chains = []
    for g in range(groups):
        middle_steps = [functools.partial(rs_stage, g, 0, s) for s in range(1, last)]
        later_steps = [functools.partial(ag_stage, g, 0, s) for s in range(1, line)]
        chains.append(
            [functools.partial(across_first, g), functools.partial(across_done, g)]
            + middle_steps
            + [functools.partial(combine_across, g)]
            + later_steps
            + [functools.partial(back_done, g)]
        )
        middle_steps = [functools.partial(rs_stage, g, 1, s) for s in range(1, last)]
        later_steps = [functools.partial(ag_stage, g, 1, s) for s in range(1, line)]
        chains.append(
            [functools.partial(line_first, g)]
            + middle_steps
            + [functools.partial(combine_line, g), functools.partial(short_done, g)]
            + later_steps
        )

    def advance(chain):
        if chain:
            chain.pop(0)()

    def small_copy(k):
        return remote(
            small_buf.at[0, k],
            small_buf.at[1, k],
            small_sem.at[0, k],
            small_sem.at[1, k],
            doubling[k],
        )

    def small_round(k):
        if k == 0:
            here = small.shape[1]
            small_buf[0, 0, 0:1, 0:here] = jnp.sum(small[...], axis=0, keepdims=True)
            small_buf[0, 0, 0:1, here:] = sums[0:1, :]
            small_copy(0).start()
            return
        small_copy(k - 1).wait()
        total = small_buf[0, k - 1] + small_buf[1, k - 1]
        if k < rounds:
            small_buf[0, k] = total
            small_copy(k).start()
        else:
            small_out[...] = total

    load(0, away)
    ones = turned.shape[1] - width
    for slot in range(2):
        turned[slot, width:] = jnp.ones((ones, turned.shape[2]), BF16)
    def tiles():
        for g in range(groups):
            for half in (away, core):
                if half is away:
                    load(g, core)
                    narrow_copy(g).wait()
                    turned[g % 2, :width] = narrow[g % 2].T
                elif g + 1 < groups:
                    load(g + 1, away)
                for t in range(2):
                    wide_copy(g, half, t).wait()
                    left = turned[(g if g < 3 or t == 1 else 2) % 2]
                    tile = dot(left, wide[g % 2, t, half])
                    if g in (1, 2) or (g == 3 and t == 0):
                        spot = half * width if g == 3 else (half * 2 + t) * width
                        spot = pl.multiple_of(sum_at[g] + spot, width)
                        sums[:, pl.ds(spot, width)] = tile[width : width + LANES]
                    tile = tile[:width]
                    if g == 0 or (g == 3 and t == 1):
                        tile = tile.T
                    rows = pl.ds(t * width, width)
                    if half is away:
                        leave[g, rows, :] = tile.astype(BF16)
                    else:
                        own[g, rows, :] = tile
                if half is away:
                    if g == 0:
                        pl.semaphore_wait(barrier, greeted)
                    for kind in range(2):
                        core_copy(g, kind).start()
                yield

    work = tiles()
    halves = 2 * groups
    small_at = 0
    for at, item in enumerate(sum_order(groups, [len(chain) for chain in chains])):
        if item < 0:
            next(work, None)
            halves -= 1
        else:
            advance(chains[item])
        if halves == 0 and at % 8 == 0 and small_at <= rounds:
            small_round(small_at)
            small_at += 1
    while small_at <= rounds:
        small_round(small_at)
        small_at += 1

    for g in range(groups):
        for kind in range(2):
            core_copy(g, kind).wait_send()
            for direction in range(2):

                def sent(kind=kind, direction=direction):
                    rows = side_at(0) if kind == 0 else pl.ds(short_at, half_rows - short_at)
                    remote(
                        out.at[g, core, rows],
                        out.at[g, core, rows],
                        line_send.at[g, kind, direction],
                        ag_recv.at[g, kind, direction, 0],
                        pair,
                    ).wait_send()

                pl.when(spots[direction] < last)(sent)
        across_copy(g).wait_send()
        short_copy(g).wait_send()
        back_copy(g, side_at(place.side)).wait_send()
        rows = pl.ds(0, half_rows)
        pair_copy(g, rows, away).wait_send()
        pair_copy(g, rows, away).wait_recv()


def unpack_kernel(
    rows,
    low,
    grad,
    packed,
    small,
    perm_t,
    block_out,
    grad_in,
    w_gate,
    w_cand,
    w_out,
    w_up,
    w_down,
    *rest,
):
    *vectors, low_s, grad_s, block_s, grad_f, wide_s, load_sem, store_sem = rest
    groups, parts, piece, width = wide_s.shape
    total, chunk, _ = low_s.shape
    chunks = total // rows
    split = width // piece

    def load(which, t):
        if which < groups:
            return None
        source, target = ((low, low_s), (grad, grad_s))[which - groups]
        return pltpu.make_async_copy(source.at[t], target.at[t], load_sem.at[which - groups, t])

    def store(which, t):
        tile, sub = t // split, t % split * piece
        if which == 0:
            to = w_down.at[0, pl.ds(t * piece, piece)]
        elif which < 3:
            to = (w_up, w_gate)[which - 1].at[0, pl.ds(sub, piece), pl.ds(tile * width, width)]
        elif which == 3 and tile % 2 == 0:
            to = w_cand.at[0, pl.ds(sub, piece), pl.ds(tile // 2 * width, width)]
        elif which == 3:
            to = w_out.at[0, pl.ds(tile // 2 * width + sub, piece)]
        else:
            to = (block_out, grad_in)[which - groups]
            to = to.at[0, t // chunks, pl.ds(t % chunks * chunk, chunk)]
        source = wide_s.at[which, t] if which < groups else (block_s, grad_f)[which - groups].at[t]
        return pltpu.make_async_copy(source, to, store_sem.at[which])

    order = [(which, t) for t in range(parts) for which in range(groups + 2) if which < groups or t < total]
    for which, t in order:
        if which >= groups:
            load(which, t).start()
    at = 0
    for vector in vectors:
        n = vector.shape[1]
        vector[...] = small[:, at : at + n]
        at += n
    for which, t in order:
        if which >= groups:
            load(which, t).wait()
        if which < groups:
            wide_s[which, t] = packed[which, pl.ds(t * piece, piece)].astype(F32)
        elif which == groups:
            block_s[t] = dot(perm_t[...], low_s[t]).astype(BF16)
        else:
            grad_f[t] = dot(perm_t[...], grad_s[t])
        store(which, t).start()
    for which in range(groups):
        everything = wide_s.at[which]
        pltpu.make_async_copy(everything, everything, store_sem.at[which]).wait()
    pltpu.make_async_copy(block_s, block_s, store_sem.at[groups]).wait()
    pltpu.make_async_copy(grad_f, grad_f, store_sem.at[groups + 1]).wait()


def unpack(packed, small, low, grad, perm_t, rows, width, hidden, ff):
    packed = packed.reshape(4, ff, width)
    vectors = (width, width, width, width, ff, 2 * hidden, hidden)
    total, chunk, _ = low.shape
    seq = total // rows * chunk
    piece = width // 2
    parts = ff // piece
    anywhere = pl.BlockSpec(memory_space=pl.ANY)
    here = pl.BlockSpec(memory_space=pltpu.VMEM)
    return pl.pallas_call(
        functools.partial(unpack_kernel, rows),
        out_shape=[
            jax.ShapeDtypeStruct((1, rows, seq, width), BF16),
            jax.ShapeDtypeStruct((1, rows, seq, width), F32),
            jax.ShapeDtypeStruct((1, width, 2 * hidden), F32),
            jax.ShapeDtypeStruct((1, width, hidden), F32),
            jax.ShapeDtypeStruct((1, hidden, width), F32),
            jax.ShapeDtypeStruct((1, width, ff), F32),
            jax.ShapeDtypeStruct((1, ff, width), F32),
        ]
        + [jax.ShapeDtypeStruct((1, n), F32) for n in vectors],
        in_specs=[anywhere] * 2 + [here] * 3,
        out_specs=[anywhere] * 7 + [here] * len(vectors),
        scratch_shapes=[
            pltpu.VMEM(low.shape, BF16),
            pltpu.VMEM(grad.shape, BF16),
            pltpu.VMEM(low.shape, BF16),
            pltpu.VMEM(grad.shape, F32),
            pltpu.VMEM((4, parts, piece, width), F32),
            pltpu.SemaphoreType.DMA((2, total)),
            pltpu.SemaphoreType.DMA((6,)),
        ],
        compiler_params=pltpu.CompilerParams(vmem_limit_bytes=UNPACK_VMEM),
        name="unpack",
    )(low, grad, packed, small, perm_t)


def sum_gradients(operands, small, hidden, ff):
    place = Place()
    line = place.line
    rounds = len(place.doubling())
    operands = [a.reshape(-1, a.shape[-1]) for a in operands]
    tokens, width = operands[2].shape
    total = small.shape[1] + ff + 3 * hidden
    groups = 4
    half_rows = ff // 2
    side_rows = half_rows * 3 // 8
    shard = side_rows // line
    short = (half_rows - 2 * side_rows) // line
    packed_shape = (groups, 2, half_rows, width)
    dp_size = lax.axis_size("dp")
    inner = 2 * line
    outer = dp_size > inner
    anywhere = pl.BlockSpec(memory_space=pl.ANY)
    here = pl.BlockSpec(memory_space=pltpu.VMEM)
    packed, small_sum = pl.pallas_call(
        functools.partial(sum_kernel, line, rounds),
        out_shape=[
            jax.ShapeDtypeStruct(packed_shape, BF16) if outer else pltpu.VMEM(packed_shape, BF16),
            jax.ShapeDtypeStruct((1, total), F32),
        ],
        in_specs=[anywhere] * 7 + [here],
        out_specs=[here, here],
        scratch_shapes=[
            pltpu.VMEM((2, 2, 2, tokens, width), BF16),
            pltpu.VMEM((2, tokens, width), BF16),
            pltpu.VMEM((2, width + 2 * LANES, tokens), BF16),
            pltpu.VMEM((groups, half_rows, width), F32),
            pltpu.VMEM((groups, half_rows, width), BF16),
            pltpu.VMEM((groups, half_rows, width), BF16),
            pltpu.VMEM((groups, side_rows, width), BF16),
            pltpu.VMEM((groups, side_rows, width), BF16),
            pltpu.VMEM((groups, short, width), BF16),
            pltpu.VMEM((groups, short, width), BF16),
            pltpu.VMEM((groups, 2, 2, line - 1, max(shard, short), width), BF16),
            pltpu.VMEM((2, rounds, 1, total), F32),
            pltpu.VMEM((LANES, ff + 3 * hidden), F32),
            pltpu.SemaphoreType.DMA((2, 2, 2)),
            pltpu.SemaphoreType.DMA((2,)),
            pltpu.SemaphoreType.DMA((2, groups, 2)),
            pltpu.SemaphoreType.DMA((2, groups)),
            pltpu.SemaphoreType.DMA((2, groups)),
            pltpu.SemaphoreType.DMA((2, groups)),
            pltpu.SemaphoreType.DMA((groups, 2, 2)),
            pltpu.SemaphoreType.DMA((groups, 2, 2, line - 1)),
            pltpu.SemaphoreType.DMA((groups, 2, 2, line - 1)),
            pltpu.SemaphoreType.DMA((2, groups)),
            pltpu.SemaphoreType.DMA((2, rounds)),
        ],
        compiler_params=pltpu.CompilerParams(
            collective_id=2,
            has_side_effects=True,
            vmem_limit_bytes=VMEM_LIMIT if outer else SUM_VMEM,
        ),
        name="sum_gradients",
    )(*operands, small)
    if outer:
        members = [list(range(i, dp_size, inner)) for i in range(inner)]
        packed, small_sum = lax.psum((packed, small_sum), "dp", axis_index_groups=members)
    return packed, small_sum


def body(tokens, resets, cotangent, *stacked):
    rows, _, width = tokens.shape
    hidden = stacked[3].shape[2]
    ff = stacked[8].shape[2]
    low, grad_in, perm_t, (*operands, small) = local_grads(tokens, resets, cotangent, stacked)
    packed, small_sum = sum_gradients(operands, small, hidden, ff)
    block_out, grad_in, w_gate, w_cand, w_out, w_up, w_down, *vectors = unpack(
        packed, small_sum, low, grad_in, perm_t, rows, width, hidden, ff
    )
    g_one, b_out, g_two, b_down, b_up, b_gate, b_cand = vectors
    grads = (g_one, w_gate, b_gate, w_cand, b_cand, w_out, b_out, g_two, w_up, b_up, w_down, b_down)
    return (block_out, grad_in) + grads


def solution(mesh):
    vector = P("section", None)
    matrix = P("section", None, None)
    weight_specs = (
        vector,
        matrix,
        vector,
        matrix,
        vector,
        matrix,
        vector,
        vector,
        matrix,
        vector,
        matrix,
        vector,
    )
    tokens = P(("dp", "rep"), None, None)
    by_rows = P("section", ("dp", "rep"), None, None)
    return jax.shard_map(
        body,
        mesh=mesh,
        in_specs=(tokens, P(("dp", "rep"), None), tokens) + weight_specs,
        out_specs=(by_rows, by_rows) + weight_specs,
        check_vma=False,
    )
```
